32 devices in a mesh: rep: 2 (over y), row: 16 (over z, x, core).
Axes of the slice: x: 2, y: 2, z: 4, core: 2. Of those that a mesh axis runs over, the one named last changes fastest.
Arguments:
- states: float32 [2, 128, 16384], P('rep', None, 'row'), parts along dimension 0, may hold values from -6 to 6
- weights: bfloat16 [32768, 16384], P(('rep', 'row')), parts along dimension 0, may hold values from -0.0625 to 0.0625
- pert_table: float32 [32, 16384], P('rep', 'row'), parts along dimension 0, may hold values from -6 to 6
- eps_gain: float32 [32768], P(('rep', 'row')), parts along dimension 0, may hold values from 0.5 to 2
- decay: float32 [32768], P(('rep', 'row')), parts along dimension 0, may hold values from 0.1 to 1
- perts: int32 [2], P('rep'), parts along dimension 0, may hold values from 0 to 15
Outputs:
- grad_w: bfloat16 [32768, 16384], P(('rep', 'row')), parts along dimension 0
- grad_x: float32 [2, 128, 16384], P('rep', None, 'row'), parts along dimension 0
- grad_table: float32 [32, 16384], P('rep', 'row'), parts along dimension 0
- grad_eps: float32 [32768], P(('rep', 'row')), parts along dimension 0
- grad_decay: float32 [32768], P(('rep', 'row')), parts along dimension 0
The draws below stay inside these ranges and needn't reach their ends.
There are 2 independent parts, one for each index of `rep`. The reference program is written for one: setup_inputs(seed, part) draws one part's arguments, and reference() takes and returns one part's arrays. A program takes and returns all parts, laid end to end along the dimension named above; each array names one. Nothing has to cross between parts.
All inputs are finite; a program needn't handle non-finite values.
Results may differ from the reference program's by a relative error of at most 0.0074.
Values may be sent and summed in bfloat16 or wider, within the bound.
No kernel may reach another device: no remote copies, remote signals or barrier semaphores. Data moves between devices by JAX's collectives and lax.ppermute only.
A program may use at most 320 MiB of HBM per device.

```python
import math
import jax
import jax.numpy as jnp
from jax import lax

G = 16384
K = 128
TRAJ = 1
PERTS = 16


def with_spikes(array, own_key, source, target, blocks, factor):
    def block_of(axis_at):
        return (jnp.arange(array.shape[axis_at]) // (array.shape[axis_at] // blocks)).reshape((-1,) + (1,) * (array.ndim - 1 - axis_at))

    near = jax.random.permutation(own_key, blocks)[block_of(target)]
    far = (block_of(target) + blocks // 2) % blocks
    return jnp.where((block_of(source) == near) | (block_of(source) == far), factor * array, array)


def block_scale(key, shape, shards, least, top_value):
    level, own = 1.0, jax.random.fold_in(key, 6)
    for axis_at, shards_of in shards:
        draws = jnp.exp(jax.random.uniform(jax.random.fold_in(own, axis_at), (shards_of,), jnp.float32, least / len(shards), top_value / len(shards)))
        level = level * jnp.repeat(draws, shape[axis_at] // shards_of).reshape([-1 if axis == axis_at else 1 for axis in range(len(shape))])
    return level


def noise(key, shape, width, reach, pieces=(), kind=jnp.bfloat16):
    gain = block_scale(key, shape, pieces, -0.22, 0.18) if pieces else 1.0
    array = jax.random.normal(key, shape, jnp.float32) * width * gain
    return jnp.minimum(jnp.maximum(array, -reach), reach).astype(kind)


def gaussian_with(own_key, dims, scale, bound, split, heavy, kind=jnp.bfloat16):
    entries = scale * jax.random.normal(own_key, dims, jnp.float32)
    if split:
        entries = entries * block_scale(own_key, dims, split, -0.22, 0.18)
    return jnp.clip(with_spikes(entries, jax.random.fold_in(own_key, 3), *heavy), -bound, bound).astype(kind)


def setup_inputs(seed: int = 0, part: int = 0) -> dict:
    key_of = jax.random.split(jax.random.key(seed), 7)
    part_splits = jax.random.split(jax.random.fold_in(key_of[6], part), 7)
    states = noise(part_splits[0], (TRAJ, K, G), 1.0, 6.0, ((2, 16),), jnp.float32)
    weights = gaussian_with(part_splits[1], (G, G), G ** -0.5, 0.0625, ((0, 16),), (1, 0, 16, 2.0))
    pert_table = noise(part_splits[2], (PERTS, G), 1.0, 6.0, ((1, 16),), jnp.float32)
    eps_gain = jnp.clip(jnp.exp(math.log(2.0) - 1.3862944 * jax.random.uniform(part_splits[3], (G,), jnp.float32) ** block_scale(part_splits[3], (G,), ((0, 16),), -0.2, 0.2)), 0.5, 2.0)
    decay = jnp.clip(jnp.exp(math.log(1.0) - 2.3025851 * jax.random.uniform(part_splits[4], (G,), jnp.float32) ** block_scale(part_splits[4], (G,), ((0, 16),), -0.2, 0.2)), 0.1, 1.0)
    perts = jax.random.randint(part_splits[5], (TRAJ,), 0, PERTS).astype(jnp.int32)
    return {"states": states, "weights": weights, "pert_table": pert_table, "eps_gain": eps_gain, "decay": decay, "perts": perts}


def cheb_matrix(count):
    index = jnp.arange(count)
    points = jnp.cos(jnp.pi * index.astype(jnp.float32) / (count - 1))
    signs = jnp.where(index % 2 == 0, 1.0, -1.0).astype(jnp.float32)
    ends = jnp.where((index == 0) | (index == count - 1), 2.0, 1.0).astype(jnp.float32)
    weight_c = signs * ends
    same = index[:, None] == index[None, :]
    spread = points[:, None] - points[None, :]
    spread = jnp.where(same, 1.0, spread)
    off = jnp.where(same, 0.0, (weight_c[:, None] / weight_c[None, :]) / spread)
    return off - jnp.diag(jnp.sum(off, axis=1))


def reference(states, weights, pert_table, eps_gain, decay, perts):
    scale = 2.0 / 1024.0
    cheb = cheb_matrix(K)
    total_rows = TRAJ * K
    xb = states.astype(jnp.bfloat16)
    flat = xb.reshape(total_rows, G)
    onehot = (perts[:, None] == jnp.arange(PERTS, dtype=jnp.int32)[None, :]).astype(jnp.float32)
    drive = jnp.dot(onehot, pert_table, precision=lax.Precision.HIGHEST)
    pre = jnp.dot(flat, weights.T, preferred_element_type=jnp.float32).reshape(TRAJ, K, G)
    pre = pre + drive[:, None, :]
    act = jnp.tanh(pre)
    deriv = scale * jnp.einsum("kl,clg->ckg", cheb, states, precision=lax.Precision.HIGHEST)
    resid = deriv - (eps_gain * act - decay * states)
    delta = (-eps_gain * (1.0 - act * act) * resid).astype(jnp.bfloat16)
    dflat = delta.reshape(total_rows, G)
    grad_w = jnp.dot(dflat.T, flat, preferred_element_type=jnp.float32).astype(jnp.bfloat16)
    back = jnp.dot(dflat, weights, preferred_element_type=jnp.float32).reshape(TRAJ, K, G)
    grad_x = scale * jnp.einsum("lk,clg->ckg", cheb, resid, precision=lax.Precision.HIGHEST) + decay * resid + back
    node_sums = jnp.sum(delta.astype(jnp.float32), axis=1)
    grad_table = jnp.dot(onehot.T, node_sums, precision=lax.Precision.HIGHEST)
    grad_eps = -jnp.sum(act * resid, axis=(0, 1))
    grad_decay = jnp.sum(states * resid, axis=(0, 1))
    return (grad_w, grad_x, grad_table, grad_eps, grad_decay)
```

```python
import jax
import jax.numpy as jnp
import numpy as np
from jax import lax
from jax.experimental import pallas as pl
from jax.experimental.pallas import tpu as pltpu
from jax.sharding import PartitionSpec as P


def cheb_matrix(count):
    index = jnp.arange(count)
    points = jnp.cos(jnp.pi * index.astype(jnp.float32) / (count - 1))
    signs = jnp.where(index % 2 == 0, 1.0, -1.0).astype(jnp.float32)
    ends = jnp.where((index == 0) | (index == count - 1), 2.0, 1.0).astype(jnp.float32)
    weight_c = signs * ends
    same = index[:, None] == index[None, :]
    spread = points[:, None] - points[None, :]
    spread = jnp.where(same, 1.0, spread)
    off = jnp.where(same, 0.0, weight_c[:, None] / weight_c[None, :] / spread)
    return off - jnp.diag(jnp.sum(off, axis=1))


def chip_ring(chips):
    rows = 4
    cols = chips // rows
    cells = [(0, col) for col in range(cols)]
    for row in range(1, rows):
        span = range(1, cols)
        cells += [(row, col) for col in (reversed(span) if row % 2 else span)]
    cells += [(row, 0) for row in range(rows - 1, 0, -1)]
    return [row * cols + col for row, col in cells]


def grad_w_kernel(offs_ref, delta_ref, own_ref, other_ref, *refs):
    out_ref = refs[-1]
    block = pl.program_id(0)

    @pl.when(block == 0)
    def _():
        out_ref[...] = jnp.dot(
            delta_ref[...], own_ref[...], preferred_element_type=jnp.float32
        ).astype(out_ref.dtype)

    @pl.when(block == 1)
    def _():
        out_ref[...] = jnp.dot(
            delta_ref[...], other_ref[...], preferred_element_type=jnp.float32
        ).astype(out_ref.dtype)


def grad_w_piece(offsets, delta_t, own, other, so_far, shape):
    rows, nodes = delta_t.shape
    slab = own.shape[1]
    tile = rows // 2
    whole = lambda height, width: pl.BlockSpec((height, width), lambda b, t, offs: (0, 0))
    in_specs = [
        pl.BlockSpec((tile, nodes), lambda b, t, offs: (t, 0)),
        whole(nodes, slab),
        whole(nodes, slab),
    ]
    operands = [offsets, delta_t, own, other]
    aliases = {}
    if so_far is not None:
        in_specs.append(pl.BlockSpec(memory_space=pl.ANY))
        operands.append(so_far)
        aliases = {4: 0}
    return pl.pallas_call(
        grad_w_kernel,
        out_shape=jax.ShapeDtypeStruct(shape, jnp.bfloat16),
        grid_spec=pltpu.PrefetchScalarGridSpec(
            num_scalar_prefetch=1,
            grid=(2, rows // tile),
            in_specs=in_specs,
            out_specs=pl.BlockSpec((tile, slab), lambda b, t, offs: (t, offs[b])),
        ),
        input_output_aliases=aliases,
        compiler_params=pltpu.CompilerParams(vmem_limit_bytes=24 * 2**20),
        cost_estimate=pl.CostEstimate(
            flops=2 * 2 * rows * nodes * slab,
            bytes_accessed=2 * 2 * rows * slab,
            transcendentals=0,
        ),
    )(*operands)


def body(chips, states, weights, pert_table, eps_gain, decay, perts):
    scale = 2.0 / 1024.0
    traj, nodes, slab = states.shape
    total = traj * nodes
    order = chip_ring(chips)
    place = np.argsort(order)
    me = lax.axis_index("row")
    core = me % 2
    order_of = jnp.asarray(np.array(order, dtype=np.int32))
    mine = jnp.asarray(place.astype(np.int32))[me // 2]

    def device_at(step, same_core):
        chip = order_of[(mine + step) % chips]
        return 2 * chip + (core if same_core else 1 - core)

    def ring(array, way):
        pairs = []
        for at, chip in enumerate(order):
            to = order[(at + way) % chips]
            pairs += [(2 * chip, 2 * to), (2 * chip + 1, 2 * to + 1)]
        return lax.ppermute(array, "row", pairs)

    def swap(array):
        return lax.ppermute(array, "row", [(i, i ^ 1) for i in range(2 * chips)])

    def columns(step, same_core):
        return lax.dynamic_slice_in_dim(
            weights, device_at(step, same_core) * slab, slab, axis=1
        )

    cheb = cheb_matrix(nodes)
    xb = states.astype(jnp.bfloat16).reshape(total, slab)

    half = chips // 2
    cut = total // 2
    blocks = {0: xb}
    back_flow, ahead_flow = xb, xb
    for step in range(1, half):
        back_flow = ring(back_flow, 1)
        ahead_flow = ring(ahead_flow, -1)
        blocks[-step] = back_flow
        blocks[step] = ahead_flow
    blocks[half] = jnp.concatenate(
        [ring(back_flow[:cut], 1), ring(ahead_flow[cut:], -1)], axis=0
    )
    near = [0]
    for step in range(1, half):
        near += [-step, step]
    near.append(half)
    pairs = {step: (blocks[step], swap(blocks[step])) for step in near}

    onehot = (perts[:, None] == jnp.arange(pert_table.shape[0], dtype=jnp.int32)[None, :]).astype(
        jnp.float32
    )
    drive = jnp.dot(onehot, pert_table, precision=lax.Precision.HIGHEST)
    deriv = scale * jnp.einsum("kl,clg->ckg", cheb, states, precision=lax.Precision.HIGHEST)
    pre = jnp.zeros((total, slab), jnp.float32)
    for step in near:
        for same_core, block in zip((True, False), pairs[step]):
            pre = pre + lax.dot_general(
                block,
                columns(step, same_core),
                (((1,), (1,)), ((), ())),
                preferred_element_type=jnp.float32,
            )
    pre = pre.reshape(traj, nodes, slab) + drive[:, None, :]
    act = jnp.tanh(pre)
    resid = deriv - (eps_gain * act - decay * states)
    delta = (-eps_gain * (1.0 - act * act) * resid).astype(jnp.bfloat16)
    dflat = delta.reshape(total, slab)
    delta_t = dflat.T

    def share(step):
        def part(same_core):
            return jnp.dot(
                dflat, columns(step, same_core), preferred_element_type=jnp.float32
            )

        other = swap(part(False).astype(jnp.bfloat16))
        return part(True) + other.astype(jnp.float32)

    far = share(half)
    ahead_sum = ring(far[:cut].astype(jnp.bfloat16), 1).astype(jnp.float32)
    back_sum = ring(far[cut:].astype(jnp.bfloat16), -1).astype(jnp.float32)
    for step in range(half - 1, 0, -1):
        ahead, back = share(step), share(-step)
        if step == half - 1:
            ahead = jnp.concatenate([ahead[:cut] + ahead_sum, ahead[cut:]], axis=0)
            back = jnp.concatenate([back[:cut], back[cut:] + back_sum], axis=0)
        else:
            ahead, back = ahead + ahead_sum, back + back_sum
        ahead_sum = ring(ahead.astype(jnp.bfloat16), 1).astype(jnp.float32)
        back_sum = ring(back.astype(jnp.bfloat16), -1).astype(jnp.float32)
    back = share(0) + ahead_sum + back_sum

    grad_w = None
    for step in near:
        offsets = jnp.stack([device_at(step, True), device_at(step, False)])
        grad_w = grad_w_piece(offsets, delta_t, *pairs[step], grad_w, weights.shape)

    back = back.reshape(traj, nodes, slab)
    grad_x = (
        scale * jnp.einsum("lk,clg->ckg", cheb, resid, precision=lax.Precision.HIGHEST)
        + decay * resid
        + back
    )
    node_sums = jnp.sum(delta.astype(jnp.float32), axis=1)
    grad_table = jnp.dot(onehot.T, node_sums, precision=lax.Precision.HIGHEST)
    grad_eps = -jnp.sum(act * resid, axis=(0, 1))
    grad_decay = jnp.sum(states * resid, axis=(0, 1))
    return (grad_w, grad_x, grad_table, grad_eps, grad_decay)


def solution(mesh):
    chips = mesh.shape["row"] // 2
    in_specs = (
        P("rep", None, "row"),
        P(("rep", "row"), None),
        P("rep", "row"),
        P(("rep", "row")),
        P(("rep", "row")),
        P("rep"),
    )
    out_specs = (
        P(("rep", "row"), None),
        P("rep", None, "row"),
        P("rep", "row"),
        P(("rep", "row")),
        P(("rep", "row")),
    )

    def run(*args):
        return body(chips, *args)

    return jax.shard_map(run, mesh=mesh, in_specs=in_specs, out_specs=out_specs, check_vma=False)
```

```python
import functools

import jax
import jax.numpy as jnp
import numpy as np
from jax import lax
from jax.experimental import pallas as pl
from jax.experimental.pallas import tpu as pltpu
from jax.sharding import PartitionSpec as P

SCALE = 2.0 / 1024.0
VMEM_LIMIT = 24 * 2**20
LONGEST_RING = 16


def cheb_matrix(count):
    index = np.arange(count)
    points = np.cos(np.pi * index / (count - 1))
    signs = np.where(index % 2 == 0, 1.0, -1.0)
    weight_c = signs * np.where((index == 0) | (index == count - 1), 2.0, 1.0)
    same = index[:, None] == index[None, :]
    spread = np.where(same, 1.0, points[:, None] - points[None, :])
    off = np.where(same, 0.0, weight_c[:, None] / weight_c[None, :] / spread)
    return jnp.asarray((off - np.diag(np.sum(off, axis=1))).astype(np.float32))


def chip_ring(chips):
    rows = 4
    cols = chips // rows
    cells = [(0, col) for col in range(cols)]
    for row in range(1, rows):
        span = range(1, cols)
        cells += [(row, col) for col in (reversed(span) if row % 2 else span)]
    cells += [(row, 0) for row in range(rows - 1, 0, -1)]
    return [row * cols + col for row, col in cells]


def whole(shape):
    return pl.BlockSpec(shape, lambda *_: (0,) * len(shape))


def cost(products, nodes, slab, rows):
    return pl.CostEstimate(
        flops=2 * products * nodes * slab * rows // 16,
        bytes_accessed=2 * products * slab * rows // 16,
        transcendentals=0,
    )


def pre_kernel(count, first, *refs):
    xs, (w_ref, *acc_ref), out_ref = refs[1 : 1 + count], refs[1 + count : -1], refs[-1]
    block, tile = pl.program_id(0), w_ref.shape[0]
    here = pl.ds(pl.multiple_of(pl.program_id(1) * tile, tile), tile)
    for at in range(count):

        @pl.when(block == at)
        def _():
            part = lax.dot_general(
                w_ref[...], xs[at][...], (((1,), (1,)), ((), ())),
                preferred_element_type=jnp.float32,
            )
            if at > 0:
                part += out_ref[here, :]
            elif not first:
                part += acc_ref[0][here, :]
            out_ref[here, :] = part


def add_products(offs, base, xs, weights, acc):
    nodes, slab = xs[0].shape
    rows, count = weights.shape[0], len(xs)
    tile = rows // 2
    first = acc is None
    return pl.pallas_call(
        functools.partial(pre_kernel, count, first),
        out_shape=jax.ShapeDtypeStruct((rows, nodes), jnp.float32),
        grid_spec=pltpu.PrefetchScalarGridSpec(
            num_scalar_prefetch=1,
            grid=(count, rows // tile),
            in_specs=[whole((nodes, slab))] * count
            + [pl.BlockSpec((tile, slab), lambda b, t, offs: (t, offs[base + b]))]
            + ([] if first else [whole((rows, nodes))]),
            out_specs=whole((rows, nodes)),
        ),
        compiler_params=pltpu.CompilerParams(vmem_limit_bytes=VMEM_LIMIT),
        cost_estimate=cost(count, nodes, slab, rows),
    )(offs, *xs, weights, *([] if first else [acc]))


def middle_kernel(
    offs, x_ref, w_ref, acc_ref, deriv_ref, states_ref, drive_ref, eps_ref, decay_ref,
    resid_ref, delta_ref, delta_t_ref, sums_ref,
):
    part = acc_ref[...] + lax.dot_general(
        w_ref[...], x_ref[...], (((1,), (1,)), ((), ())),
        preferred_element_type=jnp.float32,
    )
    states = states_ref[...]
    act = jnp.tanh(part.T + drive_ref[...])
    eps = eps_ref[...]
    resid = deriv_ref[...] - (eps * act - decay_ref[...] * states)
    delta = (-eps * (1.0 - act * act) * resid).astype(jnp.bfloat16)
    wide = delta.astype(jnp.float32)
    resid_ref[...] = resid
    delta_ref[...] = delta
    delta_t_ref[...] = wide.T.astype(jnp.bfloat16)
    sums_ref[0:1, :] = jnp.sum(wide, axis=0, keepdims=True)
    sums_ref[1:2, :] = -jnp.sum(act * resid, axis=0, keepdims=True)
    sums_ref[2:3, :] = jnp.sum(states * resid, axis=0, keepdims=True)


def middle(offs, base, x, weights, acc, deriv, states, drive, eps, decay):
    nodes, slab = x.shape
    rows = weights.shape[0]
    tile = max(rows // 4, 128)
    by_gene = pl.BlockSpec((nodes, tile), lambda t, offs: (0, t))
    row = pl.BlockSpec((1, tile), lambda t, offs: (0, t))
    turned = pl.BlockSpec((tile, nodes), lambda t, offs: (t, 0))
    return pl.pallas_call(
        middle_kernel,
        out_shape=(
            jax.ShapeDtypeStruct((nodes, rows), jnp.float32),
            jax.ShapeDtypeStruct((nodes, rows), jnp.bfloat16),
            jax.ShapeDtypeStruct((rows, nodes), jnp.bfloat16),
            jax.ShapeDtypeStruct((8, rows), jnp.float32),
        ),
        grid_spec=pltpu.PrefetchScalarGridSpec(
            num_scalar_prefetch=1,
            grid=(rows // tile,),
            in_specs=[
                whole((nodes, slab)),
                pl.BlockSpec((tile, slab), lambda t, offs: (t, offs[base])),
                turned, by_gene, by_gene, row, row, row,
            ],
            out_specs=(by_gene, by_gene, turned, pl.BlockSpec((8, tile), lambda t, offs: (0, t))),
        ),
        compiler_params=pltpu.CompilerParams(vmem_limit_bytes=VMEM_LIMIT),
        cost_estimate=cost(2, nodes, slab, rows),
    )(offs, x, weights, acc, deriv, states, drive, eps, decay)


def share_kernel(cuts, offs, delta_ref, w_ref, *outs):
    block, tile = pl.program_id(0), w_ref.shape[1]
    nodes = delta_ref.shape[0]
    here = pl.ds(pl.multiple_of(pl.program_id(1) * tile, tile), tile)
    part = jnp.dot(delta_ref[...], w_ref[...], preferred_element_type=jnp.float32)
    for at in range(cuts[-1] // nodes):

        @pl.when(block == at)
        def _():
            for start, end, out_ref in zip(cuts[:-1], cuts[1:], outs):
                low, high = max(start, at * nodes), min(end, (at + 1) * nodes)
                if low < high:
                    rows = part[low - at * nodes : high - at * nodes]
                    out_ref[low - start : high - start, here] = rows.astype(out_ref.dtype)


def shares(offs, at, delta, weights, slab, dtype, cuts):
    nodes, rows = delta.shape
    count = len(at)
    tile = max(slab // 2, 128)
    heights = [end - start for start, end in zip(cuts[:-1], cuts[1:])]

    def place(b, j, offs):
        block = offs[at[-1]]
        for index in range(count - 2, -1, -1):
            block = jnp.where(b == index, offs[at[index]], block)
        return (0, block * (slab // tile) + j)

    return pl.pallas_call(
        functools.partial(share_kernel, cuts),
        out_shape=[jax.ShapeDtypeStruct((height, slab), dtype) for height in heights],
        grid_spec=pltpu.PrefetchScalarGridSpec(
            num_scalar_prefetch=1,
            grid=(count, slab // tile),
            in_specs=[whole((nodes, rows)), pl.BlockSpec((rows, tile), place)],
            out_specs=[whole((height, slab)) for height in heights],
        ),
        compiler_params=pltpu.CompilerParams(vmem_limit_bytes=VMEM_LIMIT),
        cost_estimate=cost(count, nodes, slab, rows),
    )(offs, delta, weights)


def grad_w_kernel(count, *refs):
    delta_ref, xs, (out_ref, mark_ref) = refs[1], refs[2 : 2 + count], refs[-2:]
    block = pl.program_id(0)
    slab = out_ref.shape[1]

    @pl.when(block == 0)
    def _():
        mark_ref[...] = jnp.zeros_like(mark_ref)

    width = min(256, slab)
    for at in range(count):

        @pl.when(block == at)
        def _():
            for col in range(0, slab, width):
                out_ref[:, col : col + width] = jnp.dot(
                    delta_ref[...], xs[at][:, col : col + width],
                    preferred_element_type=jnp.float32,
                ).astype(out_ref.dtype)


def grad_w_piece(offs, base, delta_t, xs, so_far, mark, shape):
    rows, nodes = delta_t.shape
    slab, count = xs[0].shape[1], len(xs)
    first = so_far is None
    return pl.pallas_call(
        functools.partial(grad_w_kernel, count),
        out_shape=(
            jax.ShapeDtypeStruct(shape, jnp.bfloat16),
            jax.ShapeDtypeStruct((8, 128), jnp.float32),
        ),
        grid_spec=pltpu.PrefetchScalarGridSpec(
            num_scalar_prefetch=1,
            grid=(count,),
            in_specs=[whole((rows, nodes))] + [whole((nodes, slab))] * count
            + ([] if first else [pl.BlockSpec(memory_space=pl.ANY)] * 2),
            out_specs=(
                pl.BlockSpec((rows, slab), lambda b, offs: (0, offs[base + b])),
                whole((8, 128)),
            ),
        ),
        input_output_aliases={} if first else {2 + count: 0},
        compiler_params=pltpu.CompilerParams(vmem_limit_bytes=VMEM_LIMIT),
        cost_estimate=cost(count, nodes, slab, rows),
    )(offs, delta_t, *xs, *([] if first else [so_far, mark]))


def ring_body(chips, states, weights, pert_table, eps_gain, decay, perts):
    _, nodes, slab = states.shape
    rows = weights.shape[0]
    order = chip_ring(chips)
    place = np.argsort(order)
    half, cut = chips // 2, nodes // 2

    near = [0]
    for step in range(1, half):
        near += [-step, step]
    near.append(half)
    sides = {}
    listing = [(0, 0)]
    for step in range(half):
        now = [0] if step == 0 else [-step, step]
        then = [half] if step == half - 1 else [-step - 1, step + 1]
        listing += [(at, 1) for at in now] + [(at, 0) for at in then]
    listing.append((half, 1))
    sides = {key: at for at, key in enumerate(listing)}
    table = np.array(
        [
            [
                2 * order[(place[device // 2] + step) % chips] + (device % 2 ^ side)
                for step, side in listing
            ]
            for device in range(2 * chips)
        ],
        dtype=np.int32,
    )
    me = lax.axis_index("row")
    offs = lax.dynamic_slice(jnp.asarray(table), (me, 0), (1, 2 * chips)).reshape(-1)

    def ring(array, way):
        pairs = []
        for at, chip in enumerate(order):
            to = order[(at + way) % chips]
            pairs += [(2 * chip, 2 * to), (2 * chip + 1, 2 * to + 1)]
        return lax.ppermute(array, "row", pairs)

    def swap(array):
        return lax.ppermute(array, "row", [(i, i ^ 1) for i in range(2 * chips)])

    cheb = cheb_matrix(nodes)
    flat = states.reshape(nodes, slab)
    xb = flat.astype(jnp.bfloat16)

    x = {(0, 0): xb}
    acc, base = None, 0
    behind, ahead = xb, xb
    for step in range(1, half + 1):
        if step < half:
            behind, ahead = ring(behind, 1), ring(ahead, -1)
        else:
            behind, ahead = ring(behind[:cut], 1), ring(ahead[cut:], -1)
        for now in [0] if step == 1 else [1 - step, step - 1]:
            x[now, 1] = swap(x[now, 0])
        count = {1: 1, 2: 3}.get(step, 4)
        acc = add_products(
            offs, base, [x[key] for key in listing[base : base + count]], weights, acc
        )
        base += count
        behind, ahead, acc = lax.optimization_barrier((behind, ahead, acc))
        if step < half:
            x[-step, 0], x[step, 0] = behind, ahead
        else:
            x[half, 0] = jnp.concatenate([behind, ahead], axis=0)
    x[half, 1] = swap(x[half, 0])
    count = 3
    acc = add_products(
        offs, base, [x[key] for key in listing[base : base + count]], weights, acc
    )
    base += count

    onehot = (perts[:, None] == jnp.arange(pert_table.shape[0], dtype=jnp.int32)[None, :]).astype(
        jnp.float32
    )
    drive = jnp.dot(onehot, pert_table, precision=lax.Precision.HIGHEST)
    deriv = SCALE * jnp.dot(cheb, flat, precision=lax.Precision.HIGHEST)

    resid, delta, delta_t, sums = middle(
        offs, base, x[half, 1], weights, acc, deriv, flat, drive,
        eps_gain.reshape(1, rows), decay.reshape(1, rows),
    )

    def share(offs, steps):
        count = len(steps)
        pieces = 2 if count == 1 else 3
        cuts = [0] + [count * nodes * at // pieces // 16 * 16 for at in range(1, pieces)]
        cuts.append(count * nodes)
        others = shares(
            offs, [sides[step, 1] for step in steps], delta, weights, slab, jnp.bfloat16, cuts
        )
        offs, *others = lax.optimization_barrier((offs, *others))
        swapped = jnp.concatenate([swap(other) for other in others], axis=0)
        owns = shares(
            offs, [sides[step, 0] for step in steps], delta, weights, slab, jnp.float32,
            [at * nodes for at in range(count + 1)],
        )
        return [
            own + swapped[at * nodes : (at + 1) * nodes].astype(jnp.float32)
            for at, own in enumerate(owns)
        ]

    gate = lax.optimization_barrier
    pieces, cuts = [], [0, 5, 10, len(listing)]
    for base, end in zip(cuts[:-1], cuts[1:]):
        pieces.append((base, listing[base:end]))
    grad_w, mark = None, None

    (far,) = share(offs, [half])
    far = far.astype(jnp.bfloat16)
    far, offs = gate((far, offs))
    ahead, behind = ring(far[:cut], 1), ring(far[cut:], -1)
    for step in range(half - 1, -1, -1):
        if step > 0:
            own_ahead, own_behind = share(offs, [step, -step])
        else:
            (near_share,) = share(offs, [0])
        if step < half - 1:
            base, keys = pieces.pop(0)
            grad_w, mark = grad_w_piece(
                offs, base, delta_t, [x[key] for key in keys], grad_w, mark, weights.shape
            )
            ahead, behind, mark = gate((ahead, behind, mark))
        if step == 0:
            break
        ahead, behind = ahead.astype(jnp.float32), behind.astype(jnp.float32)
        if step == half - 1:
            ahead = jnp.concatenate([own_ahead[:cut] + ahead, own_ahead[cut:]], axis=0)
            behind = jnp.concatenate([own_behind[:cut], own_behind[cut:] + behind], axis=0)
        else:
            ahead, behind = own_ahead + ahead, own_behind + behind
        ahead, behind = ahead.astype(jnp.bfloat16), behind.astype(jnp.bfloat16)
        ahead, behind, offs = gate((ahead, behind, offs))
        ahead, behind = ring(ahead, 1), ring(behind, -1)

    local = (
        SCALE
        * lax.dot_general(
            cheb, resid, (((0,), (0,)), ((), ())), precision=lax.Precision.HIGHEST
        )
        + decay * resid
    )
    local = lax.optimization_barrier(local + near_share)
    grad_x = local + ahead.astype(jnp.float32) + behind.astype(jnp.float32)
    grad_x = grad_x.reshape(states.shape)
    grad_table = onehot.T * sums[0:1]
    return (grad_w, grad_x, grad_table, sums[1], sums[2])


def plain_body(states, weights, pert_table, eps_gain, decay, perts):
    traj, nodes, slab = states.shape
    total = traj * nodes
    cheb = cheb_matrix(nodes)
    xb = states.astype(jnp.bfloat16).reshape(total, slab)
    full = lax.all_gather(xb, "row", axis=1, tiled=True)
    pre = lax.dot_general(
        full, weights, (((1,), (1,)), ((), ())), preferred_element_type=jnp.float32
    )
    onehot = (perts[:, None] == jnp.arange(pert_table.shape[0], dtype=jnp.int32)[None, :]).astype(
        jnp.float32
    )
    drive = jnp.dot(onehot, pert_table, precision=lax.Precision.HIGHEST)
    act = jnp.tanh(pre.reshape(traj, nodes, slab) + drive[:, None, :])
    deriv = SCALE * jnp.einsum("kl,clg->ckg", cheb, states, precision=lax.Precision.HIGHEST)
    resid = deriv - (eps_gain * act - decay * states)
    delta = (-eps_gain * (1.0 - act * act) * resid).astype(jnp.bfloat16)
    dflat = delta.reshape(total, slab)
    grad_w = lax.dot_general(
        dflat, full, (((0,), (0,)), ((), ())), preferred_element_type=jnp.float32
    ).astype(jnp.bfloat16)
    back = jnp.dot(dflat, weights, preferred_element_type=jnp.float32)
    back = lax.psum_scatter(back, "row", scatter_dimension=1, tiled=True)
    grad_x = (
        SCALE * jnp.einsum("lk,clg->ckg", cheb, resid, precision=lax.Precision.HIGHEST)
        + decay * resid
        + back.reshape(traj, nodes, slab)
    )
    node_sums = jnp.sum(delta.astype(jnp.float32), axis=1)
    grad_table = jnp.dot(onehot.T, node_sums, precision=lax.Precision.HIGHEST)
    grad_eps = -jnp.sum(act * resid, axis=(0, 1))
    grad_decay = jnp.sum(states * resid, axis=(0, 1))
    return (grad_w, grad_x, grad_table, grad_eps, grad_decay)


def solution(mesh):
    chips = mesh.shape["row"] // 2
    in_specs = (
        P("rep", None, "row"),
        P(("rep", "row"), None),
        P("rep", "row"),
        P(("rep", "row")),
        P(("rep", "row")),
        P("rep"),
    )
    out_specs = (
        P(("rep", "row"), None),
        P("rep", None, "row"),
        P("rep", "row"),
        P(("rep", "row")),
        P(("rep", "row")),
    )

    def run(states, *others):
        if states.shape[0] == 1 and chips <= LONGEST_RING:
            return ring_body(chips, states, *others)
        return plain_body(states, *others)

    return jax.shard_map(run, mesh=mesh, in_specs=in_specs, out_specs=out_specs, check_vma=False)
```

```python
import functools

import jax
import jax.numpy as jnp
import numpy as np
from jax import lax
from jax.experimental import pallas as pl
from jax.experimental.pallas import tpu as pltpu
from jax.sharding import PartitionSpec as P

SCALE = 2.0 / 1024.0
VMEM_LIMIT = 16 * 2**20
PARTS = 2
LONGEST_RING = 16


def cheb_matrix(count):
    index = np.arange(count)
    points = np.cos(np.pi * index / (count - 1))
    signs = np.where(index % 2 == 0, 1.0, -1.0)
    weight_c = signs * np.where((index == 0) | (index == count - 1), 2.0, 1.0)
    same = index[:, None] == index[None, :]
    spread = np.where(same, 1.0, points[:, None] - points[None, :])
    off = np.where(same, 0.0, weight_c[:, None] / weight_c[None, :] / spread)
    return jnp.asarray((off - np.diag(np.sum(off, axis=1))).astype(np.float32))


def chip_ring(chips):
    rows = 4
    cols = chips // rows
    cells = [(0, col) for col in range(cols)]
    for row in range(1, rows):
        span = range(1, cols)
        cells += [(row, col) for col in (reversed(span) if row % 2 else span)]
    cells += [(row, 0) for row in range(rows - 1, 0, -1)]
    return [row * cols + col for row, col in cells]


VMEM_REF = pl.BlockSpec(memory_space=pltpu.VMEM)
SMEM_REF = pl.BlockSpec(memory_space=pltpu.SMEM)
ANY_REF = pl.BlockSpec(memory_space=pl.ANY)
HBM_REF = pl.BlockSpec(memory_space=pltpu.HBM)


def cost(products, nodes, slab, rows):
    return pl.CostEstimate(
        flops=2 * products * nodes * slab * rows // 16,
        bytes_accessed=2 * products * slab * rows // 16,
        transcendentals=0,
    )


def call(kernel, out_shape, out_specs, scratch, costs, aliases=None):
    def run(operands, in_specs):
        return pl.pallas_call(
            kernel,
            out_shape=out_shape,
            in_specs=in_specs,
            out_specs=out_specs,
            scratch_shapes=scratch,
            input_output_aliases=aliases or {},
            compiler_params=pltpu.CompilerParams(vmem_limit_bytes=VMEM_LIMIT),
            cost_estimate=costs,
        )(*operands)

    return run


def columns_of(offs_ref, at, slab):
    return pl.ds(pl.multiple_of(offs_ref[at] * slab, slab), slab)


def pre_kernel(base, count, loads, first, *refs):
    offs_ref, w_ref = refs[:2]
    xs = refs[2 : 2 + count]
    rest = refs[2 + count :]
    acc_ref, rest = (None, rest) if first else (rest[0], rest[1:])
    out_ref, blocks, sems = rest[0], rest[1 : 1 + loads], rest[-1]
    rows, slab = blocks[0].shape
    tile = rows // PARTS
    copies = []
    for at in range(loads):
        here = columns_of(offs_ref, base + at, slab)
        for part in range(PARTS):
            band = pl.ds(part * tile, tile)
            copy = pltpu.make_async_copy(
                w_ref.at[band, here], blocks[at].at[band, :], sems.at[at, part]
            )
            copy.start()
            copies.append(copy)
    for at in range(count):
        for part in range(PARTS):
            copies[at * PARTS + part].wait()
            band = pl.ds(part * tile, tile)
            total = lax.dot_general(
                blocks[at][band, :], xs[at][...], (((1,), (1,)), ((), ())),
                preferred_element_type=jnp.float32,
            )
            if at > 0:
                total += out_ref[band, :]
            elif not first:
                total += acc_ref[band, :]
            out_ref[band, :] = total
    for copy in copies[count * PARTS :]:
        copy.wait()


def add_products(offs, base, xs, weights, acc, slab, loads):
    nodes, rows, count = xs[0].shape[0], weights.shape[0], len(xs)
    first = acc is None
    out = call(
        functools.partial(pre_kernel, base, count, loads, first),
        [jax.ShapeDtypeStruct((rows, nodes), jnp.float32)]
        + [pltpu.VMEM((rows, slab), jnp.bfloat16)] * loads,
        [VMEM_REF] * (1 + loads),
        [pltpu.SemaphoreType.DMA((loads, PARTS))],
        cost(count, nodes, slab, rows),
    )(
        [offs, weights, *xs] + ([] if first else [acc]),
        [SMEM_REF, HBM_REF] + [VMEM_REF] * (count + (0 if first else 1)),
    )
    return out[0], out[1:]


def middle_kernel(
    x_ref, w_ref, acc_ref, deriv_ref, states_ref, drive_ref, eps_ref, decay_ref,
    resid_ref, delta_ref, delta_t_ref, sums_ref,
):
    rows = w_ref.shape[0]
    tile = max(rows // 4, 128)
    for start in range(0, rows, tile):
        band = pl.ds(start, tile)
        part = acc_ref[band, :] + lax.dot_general(
            w_ref[band, :], x_ref[...], (((1,), (1,)), ((), ())),
            preferred_element_type=jnp.float32,
        )
        states = states_ref[:, band]
        act = jnp.tanh(part.T + drive_ref[:, band])
        eps = eps_ref[:, band]
        resid = deriv_ref[:, band] - (eps * act - decay_ref[:, band] * states)
        delta = (-eps * (1.0 - act * act) * resid).astype(jnp.bfloat16)
        wide = delta.astype(jnp.float32)
        resid_ref[:, band] = resid
        delta_ref[:, band] = delta
        delta_t_ref[band, :] = wide.T.astype(jnp.bfloat16)
        sums_ref[0:1, band] = jnp.sum(wide, axis=0, keepdims=True)
        sums_ref[1:2, band] = -jnp.sum(act * resid, axis=0, keepdims=True)
        sums_ref[2:3, band] = jnp.sum(states * resid, axis=0, keepdims=True)


def middle(x, block, acc, deriv, states, drive, eps, decay):
    nodes, slab = x.shape
    rows = block.shape[0]
    return call(
        middle_kernel,
        [
            jax.ShapeDtypeStruct((nodes, rows), jnp.float32),
            jax.ShapeDtypeStruct((nodes, rows), jnp.bfloat16),
            jax.ShapeDtypeStruct((rows, nodes), jnp.bfloat16),
            jax.ShapeDtypeStruct((8, rows), jnp.float32),
        ],
        [VMEM_REF] * 4,
        [],
        cost(2, nodes, slab, rows),
    )([x, block, acc, deriv, states, drive, eps, decay], [VMEM_REF] * 8)


def share_kernel(cuts, offs_ref, delta_ref, *refs):
    nodes = delta_ref.shape[0]
    count = cuts[-1] // nodes
    blocks, outs = refs[: 2 * count], refs[2 * count :]
    slab = blocks[0].shape[1]
    tile = max(slab // 2, 128)
    for at, block_ref in enumerate(blocks):
        for col in range(0, slab, tile):
            here = pl.ds(col, tile)
            part = jnp.dot(
                delta_ref[...], block_ref[:, here], preferred_element_type=jnp.float32
            )
            if at >= count:
                outs[len(cuts) - 1 + at - count][:, here] = part
                continue
            for start, end, out_ref in zip(cuts[:-1], cuts[1:], outs):
                low, high = max(start, at * nodes), min(end, (at + 1) * nodes)
                if low < high:
                    rows = part[low - at * nodes : high - at * nodes]
                    out_ref[low - start : high - start, here] = rows.astype(out_ref.dtype)


def shares(offs, delta, blocks, cuts):
    nodes, rows = delta.shape
    slab = blocks[0].shape[1]
    own = len(blocks) // 2
    heights = [end - start for start, end in zip(cuts[:-1], cuts[1:])]
    outs = call(
        functools.partial(share_kernel, cuts),
        [jax.ShapeDtypeStruct((height, slab), jnp.bfloat16) for height in heights]
        + [jax.ShapeDtypeStruct((nodes, slab), jnp.float32)] * own,
        [VMEM_REF] * (len(heights) + own),
        [],
        cost(len(blocks), nodes, slab, rows),
    )([offs, delta, *blocks], [SMEM_REF] + [VMEM_REF] * (1 + len(blocks)))
    return outs[: len(heights)], outs[len(heights) :]


def grad_w_kernel(base, count, *refs):
    offs_ref, delta_ref, xs = refs[0], refs[1], refs[2 : 2 + count]
    out_ref, mark_ref, held, sems = refs[-4:]
    rows, slab = delta_ref.shape[0], xs[0].shape[1]
    slots, tile = held.shape[:2]
    mark_ref[...] = jnp.zeros_like(mark_ref)
    copies = []
    for at in range(count):
        here = columns_of(offs_ref, base + at, slab)
        for start in range(0, rows, tile):
            band = pl.ds(start, tile)
            slot = len(copies) % slots
            if len(copies) >= slots:
                copies[-slots].wait()
            held[slot] = jnp.dot(
                delta_ref[band, :], xs[at][...], preferred_element_type=jnp.float32
            ).astype(held.dtype)
            copy = pltpu.make_async_copy(held.at[slot], out_ref.at[band, here], sems.at[slot])
            copy.start()
            copies.append(copy)
    for copy in copies[-slots:]:
        copy.wait()


def grad_w_piece(offs, base, delta_t, xs, so_far, mark, shape):
    rows, nodes = delta_t.shape
    slab, count = xs[0].shape[1], len(xs)
    tile = max(rows // 4, 128)
    first = so_far is None
    return call(
        functools.partial(grad_w_kernel, base, count),
        [jax.ShapeDtypeStruct(shape, jnp.bfloat16), jax.ShapeDtypeStruct((8, 128), jnp.float32)],
        [ANY_REF, VMEM_REF],
        [pltpu.VMEM((6, tile, slab), jnp.bfloat16), pltpu.SemaphoreType.DMA((6,))],
        cost(count, nodes, slab, rows),
        {} if first else {2 + count: 0},
    )(
        [offs, delta_t, *xs] + ([] if first else [so_far, mark]),
        [SMEM_REF] + [VMEM_REF] * (1 + count) + ([] if first else [ANY_REF] * 2),
    )


def ring_body(chips, states, weights, pert_table, eps_gain, decay, perts):
    _, nodes, slab = states.shape
    rows = weights.shape[0]
    order = chip_ring(chips)
    place = np.argsort(order)
    half, cut = chips // 2, nodes // 2

    near = [0]
    for step in range(1, half):
        near += [-step, step]
    near.append(half)
    listing = [(0, 0)]
    for step in range(half):
        now = [0] if step == 0 else [-step, step]
        then = [half] if step == half - 1 else [-step - 1, step + 1]
        listing += [(at, 1) for at in now] + [(at, 0) for at in then]
    listing.append((half, 1))
    table = np.array(
        [
            [
                2 * order[(place[device // 2] + step) % chips] + (device % 2 ^ side)
                for step, side in listing
            ]
            for device in range(2 * chips)
        ],
        dtype=np.int32,
    )
    me = lax.axis_index("row")
    offs = lax.dynamic_slice(jnp.asarray(table), (me, 0), (1, 2 * chips)).reshape(-1)

    def ring(array, way):
        pairs = []
        for at, chip in enumerate(order):
            to = order[(at + way) % chips]
            pairs += [(2 * chip, 2 * to), (2 * chip + 1, 2 * to + 1)]
        return lax.ppermute(array, "row", pairs)

    def swap(array):
        return lax.ppermute(array, "row", [(i, i ^ 1) for i in range(2 * chips)])

    weights = pltpu.with_memory_space_constraint(weights, pltpu.HBM)
    cheb = cheb_matrix(nodes)
    flat = states.reshape(nodes, slab)
    xb = flat.astype(jnp.bfloat16)

    x = {(0, 0): xb}
    acc, base, block = None, 0, {}

    def next_products(acc, base, count, loads):
        keys = listing[base : base + loads]
        acc, loaded = add_products(
            offs, base, [x[key] for key in keys[:count]], weights, acc, slab, loads
        )
        block.update(zip(keys, loaded))
        return acc, base + count

    behind, ahead = xb, xb
    for step in range(1, half + 1):
        if step < half:
            behind, ahead = ring(behind, 1), ring(ahead, -1)
        else:
            behind, ahead = ring(behind[:cut], 1), ring(ahead[cut:], -1)
        for now in [0] if step == 1 else [1 - step, step - 1]:
            x[now, 1] = swap(x[now, 0])
        count = {1: 1, 2: 3}.get(step, 4)
        acc, base = next_products(acc, base, count, count)
        behind, ahead, acc = lax.optimization_barrier((behind, ahead, acc))
        if step < half:
            x[-step, 0], x[step, 0] = behind, ahead
        else:
            x[half, 0] = jnp.concatenate([behind, ahead], axis=0)
    x[half, 1] = swap(x[half, 0])
    acc, base = next_products(acc, base, 3, 4)

    onehot = (perts[:, None] == jnp.arange(pert_table.shape[0], dtype=jnp.int32)[None, :]).astype(
        jnp.float32
    )
    drive = jnp.dot(onehot, pert_table, precision=lax.Precision.HIGHEST)
    deriv = SCALE * jnp.dot(cheb, flat, precision=lax.Precision.HIGHEST)

    resid, delta, delta_t, sums = middle(
        x[half, 1], block[half, 1], acc, deriv, flat, drive,
        eps_gain.reshape(1, rows), decay.reshape(1, rows),
    )

    def share(steps):
        count = len(steps)
        parts = 2 if count == 1 else 3
        cuts = [0] + [count * nodes * at // parts // 16 * 16 for at in range(1, parts)]
        cuts.append(count * nodes)
        blocks = [block[step, side] for side in (1, 0) for step in steps]
        others, owns = shares(offs, delta, blocks, cuts)
        swapped = jnp.concatenate([swap(other) for other in others], axis=0)
        return [
            own + swapped[at * nodes : (at + 1) * nodes].astype(jnp.float32)
            for at, own in enumerate(owns)
        ]

    gate = lax.optimization_barrier
    first = len(listing) // 8
    each = (len(listing) - first) // (half - 1)
    cuts = [0] + [first + each * at for at in range(half - 1)] + [len(listing)]
    pieces = [(base, listing[base:end]) for base, end in zip(cuts[:-1], cuts[1:])]
    grad_w, mark = None, None

    def next_piece(grad_w, mark):
        base, keys = pieces.pop(0)
        return grad_w_piece(
            offs, base, delta_t, [x[key] for key in keys], grad_w, mark, weights.shape
        )

    (far,) = share([half])
    far = far.astype(jnp.bfloat16)
    grad_w, mark = next_piece(grad_w, mark)
    far, offs, mark = gate((far, offs, mark))
    ahead, behind = ring(far[:cut], 1), ring(far[cut:], -1)
    for step in range(half - 1, -1, -1):
        if step > 0:
            own_ahead, own_behind = share([step, -step])
        else:
            (near_share,) = share([0])
        if step < half - 1:
            grad_w, mark = next_piece(grad_w, mark)
            ahead, behind, mark = gate((ahead, behind, mark))
        if step == 0:
            break
        ahead, behind = ahead.astype(jnp.float32), behind.astype(jnp.float32)
        if step == half - 1:
            ahead = jnp.concatenate([own_ahead[:cut] + ahead, own_ahead[cut:]], axis=0)
            behind = jnp.concatenate([own_behind[:cut], own_behind[cut:] + behind], axis=0)
        else:
            ahead, behind = own_ahead + ahead, own_behind + behind
        ahead, behind = ahead.astype(jnp.bfloat16), behind.astype(jnp.bfloat16)
        ahead, behind, offs = gate((ahead, behind, offs))
        ahead, behind = ring(ahead, 1), ring(behind, -1)

    local = (
        SCALE
        * lax.dot_general(
            cheb, resid, (((0,), (0,)), ((), ())), precision=lax.Precision.HIGHEST
        )
        + decay * resid
    )
    local = gate(local)
    grad_x = local + near_share + ahead.astype(jnp.float32) + behind.astype(jnp.float32)
    grad_x = grad_x.reshape(states.shape)
    grad_table = onehot.T * sums[0:1]
    return (grad_w, grad_x, grad_table, sums[1], sums[2])


def plain_body(states, weights, pert_table, eps_gain, decay, perts):
    traj, nodes, slab = states.shape
    total = traj * nodes
    cheb = cheb_matrix(nodes)
    xb = states.astype(jnp.bfloat16).reshape(total, slab)
    full = lax.all_gather(xb, "row", axis=1, tiled=True)
    pre = lax.dot_general(
        full, weights, (((1,), (1,)), ((), ())), preferred_element_type=jnp.float32
    )
    onehot = (perts[:, None] == jnp.arange(pert_table.shape[0], dtype=jnp.int32)[None, :]).astype(
        jnp.float32
    )
    drive = jnp.dot(onehot, pert_table, precision=lax.Precision.HIGHEST)
    act = jnp.tanh(pre.reshape(traj, nodes, slab) + drive[:, None, :])
    deriv = SCALE * jnp.einsum("kl,clg->ckg", cheb, states, precision=lax.Precision.HIGHEST)
    resid = deriv - (eps_gain * act - decay * states)
    delta = (-eps_gain * (1.0 - act * act) * resid).astype(jnp.bfloat16)
    dflat = delta.reshape(total, slab)
    grad_w = lax.dot_general(
        dflat, full, (((0,), (0,)), ((), ())), preferred_element_type=jnp.float32
    ).astype(jnp.bfloat16)
    back = jnp.dot(dflat, weights, preferred_element_type=jnp.float32)
    back = lax.psum_scatter(back, "row", scatter_dimension=1, tiled=True)
    grad_x = (
        SCALE * jnp.einsum("lk,clg->ckg", cheb, resid, precision=lax.Precision.HIGHEST)
        + decay * resid
        + back.reshape(traj, nodes, slab)
    )
    node_sums = jnp.sum(delta.astype(jnp.float32), axis=1)
    grad_table = jnp.dot(onehot.T, node_sums, precision=lax.Precision.HIGHEST)
    grad_eps = -jnp.sum(act * resid, axis=(0, 1))
    grad_decay = jnp.sum(states * resid, axis=(0, 1))
    return (grad_w, grad_x, grad_table, grad_eps, grad_decay)


def solution(mesh):
    chips = mesh.shape["row"] // 2
    in_specs = (
        P("rep", None, "row"),
        P(("rep", "row"), None),
        P("rep", "row"),
        P(("rep", "row")),
        P(("rep", "row")),
        P("rep"),
    )
    out_specs = (
        P(("rep", "row"), None),
        P("rep", None, "row"),
        P("rep", "row"),
        P(("rep", "row")),
        P(("rep", "row")),
    )

    def run(states, *others):
        if states.shape[0] == 1 and chips <= LONGEST_RING:
            return ring_body(chips, states, *others)
        return plain_body(states, *others)

    return jax.shard_map(run, mesh=mesh, in_specs=in_specs, out_specs=out_specs, check_vma=False)
```

```python
import functools

import jax
import jax.numpy as jnp
import numpy as np
from jax import lax
from jax.experimental import pallas as pl
from jax.experimental.pallas import tpu as pltpu
from jax.sharding import PartitionSpec as P

SCALE = 2.0 / 1024.0
VMEM_LIMIT = 4 * 2**20
BANDS = 8
LONGEST_RING = 16


def cheb_matrix(count):
    index = np.arange(count)
    points = np.cos(np.pi * index / (count - 1))
    signs = np.where(index % 2 == 0, 1.0, -1.0)
    weight_c = signs * np.where((index == 0) | (index == count - 1), 2.0, 1.0)
    same = index[:, None] == index[None, :]
    spread = np.where(same, 1.0, points[:, None] - points[None, :])
    off = np.where(same, 0.0, weight_c[:, None] / weight_c[None, :] / spread)
    return jnp.asarray((off - np.diag(np.sum(off, axis=1))).astype(np.float32))


def chip_ring(chips):
    rows = 4
    cols = chips // rows
    cells = [(0, col) for col in range(cols)]
    for row in range(1, rows):
        span = range(1, cols)
        cells += [(row, col) for col in (reversed(span) if row % 2 else span)]
    cells += [(row, 0) for row in range(rows - 1, 0, -1)]
    return [row * cols + col for row, col in cells]


VMEM_REF = pl.BlockSpec(memory_space=pltpu.VMEM)
SMEM_REF = pl.BlockSpec(memory_space=pltpu.SMEM)
ANY_REF = pl.BlockSpec(memory_space=pl.ANY)
HBM_REF = pl.BlockSpec(memory_space=pltpu.HBM)


def cost(products, nodes, slab, rows):
    return pl.CostEstimate(
        flops=2 * products * nodes * slab * rows // 16,
        bytes_accessed=2 * products * slab * rows // 16,
        transcendentals=0,
    )


def call(kernel, out_shape, out_specs, scratch, costs, aliases=None, more=0):
    def run(operands, in_specs):
        return pl.pallas_call(
            kernel,
            out_shape=out_shape,
            in_specs=in_specs,
            out_specs=out_specs,
            scratch_shapes=scratch,
            input_output_aliases=aliases or {},
            compiler_params=pltpu.CompilerParams(vmem_limit_bytes=VMEM_LIMIT + more),
            cost_estimate=costs,
        )(*operands)

    return run


def columns_of(offs_ref, at, slab):
    return pl.ds(pl.multiple_of(offs_ref[at] * slab, slab), slab)


def load_rows(w_ref, held_ref, sems, start):
    tile = held_ref.shape[0] // sems.shape[0]
    copies = []
    for at in range(sems.shape[0]):
        band = pl.ds(at * tile, tile)
        copy = pltpu.make_async_copy(
            w_ref.at[pl.ds(start + at * tile, tile), :], held_ref.at[band, :], sems.at[at]
        )
        copy.start()
        copies.append(copy)
    return copies


def product(held_ref, band, here, x_ref):
    return lax.dot_general(
        held_ref[band, here], x_ref[...], (((1,), (1,)), ((), ())),
        preferred_element_type=jnp.float32,
    )


def first_kernel(base, offs_ref, w_ref, x_ref, out_ref, head_ref, sems):
    slab = x_ref.shape[1]
    tile = head_ref.shape[0] // sems.shape[0]
    here = columns_of(offs_ref, base, slab)
    for at, copy in enumerate(load_rows(w_ref, head_ref, sems, 0)):
        copy.wait()
        band = pl.ds(at * tile, tile)
        out_ref[band, :] = product(head_ref, band, here, x_ref)


def second_kernel(base, count, *refs):
    offs_ref, w_ref, acc_ref, head_ref = refs[:4]
    xs, (out_ref, rest_ref, sems) = refs[4 : 4 + count], refs[4 + count :]
    slab = xs[0].shape[1]
    start = head_ref.shape[0]
    copies = load_rows(w_ref, rest_ref, sems, start)
    tile = rest_ref.shape[0]
    for low in range(0, start, tile):
        band = pl.ds(low, tile)
        total = acc_ref[band, :]
        for at in range(1, count):
            total += product(head_ref, band, columns_of(offs_ref, base + at, slab), xs[at])
        out_ref[band, :] = total
    for copy in copies:
        copy.wait()
    total = None
    for at in range(count):
        part = product(rest_ref, slice(None), columns_of(offs_ref, base + at, slab), xs[at])
        total = part if total is None else total + part
    out_ref[pl.ds(start, tile), :] = total


def pre_kernel(base, count, offs_ref, acc_ref, head_ref, rest_ref, *refs):
    xs, out_ref = refs[:count], refs[count]
    slab = xs[0].shape[1]
    tile = rest_ref.shape[0]
    rows = out_ref.shape[0]
    for low in range(0, rows, tile):
        held_ref, start = (head_ref, low) if low < rows - tile else (rest_ref, 0)
        total = acc_ref[pl.ds(low, tile), :]
        for at in range(count):
            here = columns_of(offs_ref, base + at, slab)
            total += product(held_ref, pl.ds(start, tile), here, xs[at])
        out_ref[pl.ds(low, tile), :] = total


def first_products(offs, base, x, weights):
    (nodes, slab), (rows, genes) = x.shape, weights.shape
    head = rows * 3 // 4
    return call(
        functools.partial(first_kernel, base),
        [
            jax.ShapeDtypeStruct((rows, nodes), jnp.float32),
            pltpu.VMEM((head, genes), jnp.bfloat16),
        ],
        [VMEM_REF] * 2,
        [pltpu.SemaphoreType.DMA((6,))],
        cost(1, nodes, slab, rows),
    )([offs, weights, x], [SMEM_REF, HBM_REF, VMEM_REF])


def second_products(offs, base, xs, weights, acc, head):
    (nodes, slab), (rows, genes) = xs[0].shape, weights.shape
    count = len(xs)
    return call(
        functools.partial(second_kernel, base, count),
        [
            jax.ShapeDtypeStruct((rows, nodes), jnp.float32),
            pltpu.VMEM((rows - head.shape[0], genes), jnp.bfloat16),
        ],
        [VMEM_REF] * 2,
        [pltpu.SemaphoreType.DMA((2,))],
        cost(count, nodes, slab, rows),
    )([offs, weights, acc, head, *xs], [SMEM_REF, HBM_REF] + [VMEM_REF] * (2 + count))


def add_products(offs, base, xs, acc, head, rest):
    nodes, slab = xs[0].shape
    rows, count = acc.shape[0], len(xs)
    return call(
        functools.partial(pre_kernel, base, count),
        jax.ShapeDtypeStruct((rows, nodes), jnp.float32),
        VMEM_REF,
        [],
        cost(count, nodes, slab, rows),
    )([offs, acc, head, rest, *xs], [SMEM_REF] + [VMEM_REF] * (3 + count))


def middle_kernel(
    base, offs_ref, x_ref, head_ref, rest_ref, acc_ref, deriv_ref, states_ref, drive_ref,
    eps_ref, decay_ref, resid_ref, delta_ref, delta_t_ref, sums_ref,
):
    rows, tile = acc_ref.shape[0], rest_ref.shape[0]
    here = columns_of(offs_ref, base, x_ref.shape[1])
    for start in range(0, rows, tile):
        held_ref, low = (head_ref, start) if start < rows - tile else (rest_ref, 0)
        band = pl.ds(start, tile)
        part = acc_ref[band, :] + product(held_ref, pl.ds(low, tile), here, x_ref)
        states = states_ref[:, band]
        act = jnp.tanh(part.T + drive_ref[:, band])
        eps = eps_ref[:, band]
        resid = deriv_ref[:, band] - (eps * act - decay_ref[:, band] * states)
        delta = (-eps * (1.0 - act * act) * resid).astype(jnp.bfloat16)
        wide = delta.astype(jnp.float32)
        resid_ref[:, band] = resid
        delta_ref[:, band] = delta
        delta_t_ref[band, :] = wide.T.astype(jnp.bfloat16)
        sums_ref[0:1, band] = jnp.sum(wide, axis=0, keepdims=True)
        sums_ref[1:2, band] = -jnp.sum(act * resid, axis=0, keepdims=True)
        sums_ref[2:3, band] = jnp.sum(states * resid, axis=0, keepdims=True)


def middle(offs, base, x, head, rest, acc, deriv, states, drive, eps, decay):
    nodes, slab = x.shape
    rows = acc.shape[0]
    return call(
        functools.partial(middle_kernel, base),
        [
            jax.ShapeDtypeStruct((nodes, rows), jnp.float32),
            jax.ShapeDtypeStruct((nodes, rows), jnp.bfloat16),
            jax.ShapeDtypeStruct((rows, nodes), jnp.bfloat16),
            jax.ShapeDtypeStruct((8, rows), jnp.float32),
        ],
        [VMEM_REF] * 4,
        [],
        cost(2, nodes, slab, rows),
    )(
        [offs, x, head, rest, acc, deriv, states, drive, eps, decay],
        [SMEM_REF] + [VMEM_REF] * 9,
    )


def share_kernel(at_places, cuts, offs_ref, delta_ref, head_ref, rest_ref, *outs):
    nodes = delta_ref.shape[0]
    count = cuts[-1] // nodes
    slab = outs[0].shape[1]
    split = head_ref.shape[0]
    tile = max(slab // 2, 128)
    for at, place in enumerate(at_places):
        for col in range(0, slab, tile):
            here = pl.ds(col, tile)
            there = pl.ds(pl.multiple_of(offs_ref[place] * slab + col, tile), tile)
            part = jnp.dot(
                delta_ref[:, :split], head_ref[:, there], preferred_element_type=jnp.float32
            ) + jnp.dot(
                delta_ref[:, split:], rest_ref[:, there], preferred_element_type=jnp.float32
            )
            if at >= count:
                outs[len(cuts) - 1 + at - count][:, here] = part
                continue
            for start, end, out_ref in zip(cuts[:-1], cuts[1:], outs):
                low, high = max(start, at * nodes), min(end, (at + 1) * nodes)
                if low < high:
                    rows = part[low - at * nodes : high - at * nodes]
                    out_ref[low - start : high - start, here] = rows.astype(out_ref.dtype)


def shares(offs, at_places, delta, head, rest, slab, cuts):
    nodes, rows = delta.shape
    own = len(at_places) // 2
    heights = [end - start for start, end in zip(cuts[:-1], cuts[1:])]
    outs = call(
        functools.partial(share_kernel, at_places, cuts),
        [jax.ShapeDtypeStruct((height, slab), jnp.bfloat16) for height in heights]
        + [jax.ShapeDtypeStruct((nodes, slab), jnp.float32)] * own,
        [VMEM_REF] * (len(heights) + own),
        [],
        cost(len(at_places), nodes, slab, rows),
    )([offs, delta, head, rest], [SMEM_REF] + [VMEM_REF] * 3)
    return outs[: len(heights)], outs[len(heights) :]


def grad_w_kernel(first, last, count, *refs):
    offs_ref, delta_ref, xs = refs[0], refs[1], refs[2 : 2 + count]
    out_ref, mark_ref, held, sems = refs[-4:]
    slab = xs[0].shape[1]
    slots, tile = held.shape[:2]
    mark_ref[...] = jnp.zeros_like(mark_ref)
    copies = []
    for row in range(first, last):
        band = pl.ds(row * tile, tile)
        slot = len(copies) % slots
        if len(copies) >= slots:
            copies[-slots].wait()
        for at in range(count):
            held[slot, :, columns_of(offs_ref, at, slab)] = jnp.dot(
                delta_ref[band, :], xs[at][...], preferred_element_type=jnp.float32
            ).astype(held.dtype)
        copy = pltpu.make_async_copy(held.at[slot], out_ref.at[band, :], sems.at[slot])
        copy.start()
        copies.append(copy)
    for copy in copies[-slots:]:
        copy.wait()


def grad_w_piece(offs, first, last, bands, delta_t, xs, so_far, mark, shape):
    rows, nodes = delta_t.shape
    slab, count = xs[0].shape[1], len(xs)
    start = so_far is None
    return call(
        functools.partial(grad_w_kernel, first, last, count),
        [jax.ShapeDtypeStruct(shape, jnp.bfloat16), jax.ShapeDtypeStruct((8, 128), jnp.float32)],
        [ANY_REF, VMEM_REF],
        [pltpu.VMEM((2, rows // bands, shape[1]), jnp.bfloat16), pltpu.SemaphoreType.DMA((2,))],
        cost((last - first) * count // bands, nodes, slab, rows),
        {} if start else {2 + count: 0},
        2 * 2 * (rows // bands) * shape[1],
    )(
        [offs, delta_t, *xs] + ([] if start else [so_far, mark]),
        [SMEM_REF] + [VMEM_REF] * (1 + count) + ([] if start else [ANY_REF] * 2),
    )


def ring_body(chips, states, weights, pert_table, eps_gain, decay, perts):
    _, nodes, slab = states.shape
    rows = weights.shape[0]
    order = chip_ring(chips)
    place = np.argsort(order)
    half, cut = chips // 2, nodes // 2

    near = [0]
    for step in range(1, half):
        near += [-step, step]
    near.append(half)
    listing = [(0, 0)]
    for step in range(half):
        now = [0] if step == 0 else [-step, step]
        then = [half] if step == half - 1 else [-step - 1, step + 1]
        listing += [(at, 1) for at in now] + [(at, 0) for at in then]
    listing.append((half, 1))
    sides = {key: at for at, key in enumerate(listing)}
    table = np.array(
        [
            [
                2 * order[(place[device // 2] + step) % chips] + (device % 2 ^ side)
                for step, side in listing
            ]
            for device in range(2 * chips)
        ],
        dtype=np.int32,
    )
    me = lax.axis_index("row")
    offs = lax.dynamic_slice(jnp.asarray(table), (me, 0), (1, 2 * chips)).reshape(-1)

    def ring(array, way):
        pairs = []
        for at, chip in enumerate(order):
            to = order[(at + way) % chips]
            pairs += [(2 * chip, 2 * to), (2 * chip + 1, 2 * to + 1)]
        return lax.ppermute(array, "row", pairs)

    def swap(array):
        return lax.ppermute(array, "row", [(i, i ^ 1) for i in range(2 * chips)])

    weights = pltpu.with_memory_space_constraint(weights, pltpu.HBM)
    cheb = cheb_matrix(nodes)
    flat = states.reshape(nodes, slab)
    xb = flat.astype(jnp.bfloat16)

    x = {(0, 0): xb}
    behind, ahead, base = xb, xb, 0
    for step in range(1, half + 1):
        if step < half:
            behind, ahead = ring(behind, 1), ring(ahead, -1)
        else:
            behind, ahead = ring(behind[:cut], 1), ring(ahead[cut:], -1)
        for now in [0] if step == 1 else [1 - step, step - 1]:
            x[now, 1] = swap(x[now, 0])
        count = {1: 1, 2: 3}.get(step, 4)
        xs = [x[key] for key in listing[base : base + count]]
        if step == 1:
            acc, head = first_products(offs, 0, xs[0], weights)
        elif step == 2:
            acc, rest = second_products(offs, 0, [x[0, 0], *xs], weights, acc, head)
        else:
            acc = add_products(offs, base, xs, acc, head, rest)
        base += count
        behind, ahead, acc = lax.optimization_barrier((behind, ahead, acc))
        if step < half:
            x[-step, 0], x[step, 0] = behind, ahead
        else:
            x[half, 0] = jnp.concatenate([behind, ahead], axis=0)
    x[half, 1] = swap(x[half, 0])
    xs = [x[key] for key in listing[base : base + 3]]
    acc = add_products(offs, base, xs, acc, head, rest)
    base += 3

    onehot = (perts[:, None] == jnp.arange(pert_table.shape[0], dtype=jnp.int32)[None, :]).astype(
        jnp.float32
    )
    drive = jnp.dot(onehot, pert_table, precision=lax.Precision.HIGHEST)
    deriv = SCALE * jnp.dot(cheb, flat, precision=lax.Precision.HIGHEST)

    resid, delta, delta_t, sums = middle(
        offs, base, x[half, 1], head, rest, acc, deriv, flat, drive,
        eps_gain.reshape(1, rows), decay.reshape(1, rows),
    )

    def share(steps):
        count = len(steps)
        parts = 2 if count == 1 else 3
        cuts = [0] + [count * nodes * at // parts // 16 * 16 for at in range(1, parts)]
        cuts.append(count * nodes)
        places = [sides[step, side] for side in (1, 0) for step in steps]
        others, owns = shares(offs, places, delta, head, rest, slab, cuts)
        swapped = jnp.concatenate([swap(other) for other in others], axis=0)
        return [
            own + swapped[at * nodes : (at + 1) * nodes].astype(jnp.float32)
            for at, own in enumerate(owns)
        ]

    gate = lax.optimization_barrier
    cuts = [0, 1] + [1 + (BANDS - 1) * at // (half - 1) for at in range(1, half)]
    pieces = list(zip(cuts[:-1], cuts[1:]))
    grad_w, mark = None, None

    def next_piece(grad_w, mark):
        first, last = pieces.pop(0)
        return grad_w_piece(
            offs, first, last, BANDS, delta_t, [x[key] for key in listing], grad_w, mark,
            weights.shape,
        )

    (far,) = share([half])
    far = far.astype(jnp.bfloat16)
    grad_w, mark = next_piece(grad_w, mark)
    far, offs, mark = gate((far, offs, mark))
    ahead, behind = ring(far[:cut], 1), ring(far[cut:], -1)
    for step in range(half - 1, -1, -1):
        if step > 0:
            own_ahead, own_behind = share([step, -step])
        else:
            (near_share,) = share([0])
        if step < half - 1:
            grad_w, mark = next_piece(grad_w, mark)
            ahead, behind, mark = gate((ahead, behind, mark))
        if step == 0:
            break
        ahead, behind = ahead.astype(jnp.float32), behind.astype(jnp.float32)
        if step == half - 1:
            ahead = jnp.concatenate([own_ahead[:cut] + ahead, own_ahead[cut:]], axis=0)
            behind = jnp.concatenate([own_behind[:cut], own_behind[cut:] + behind], axis=0)
        else:
            ahead, behind = own_ahead + ahead, own_behind + behind
        ahead, behind = ahead.astype(jnp.bfloat16), behind.astype(jnp.bfloat16)
        ahead, behind, offs = gate((ahead, behind, offs))
        ahead, behind = ring(ahead, 1), ring(behind, -1)

    local = (
        SCALE
        * lax.dot_general(
            cheb, resid, (((0,), (0,)), ((), ())), precision=lax.Precision.HIGHEST
        )
        + decay * resid
    )
    local = gate(local)
    grad_x = local + near_share + ahead.astype(jnp.float32) + behind.astype(jnp.float32)
    grad_x = grad_x.reshape(states.shape)
    grad_table = onehot.T * sums[0:1]
    return (grad_w, grad_x, grad_table, sums[1], sums[2])


def plain_body(states, weights, pert_table, eps_gain, decay, perts):
    traj, nodes, slab = states.shape
    total = traj * nodes
    cheb = cheb_matrix(nodes)
    xb = states.astype(jnp.bfloat16).reshape(total, slab)
    full = lax.all_gather(xb, "row", axis=1, tiled=True)
    pre = lax.dot_general(
        full, weights, (((1,), (1,)), ((), ())), preferred_element_type=jnp.float32
    )
    onehot = (perts[:, None] == jnp.arange(pert_table.shape[0], dtype=jnp.int32)[None, :]).astype(
        jnp.float32
    )
    drive = jnp.dot(onehot, pert_table, precision=lax.Precision.HIGHEST)
    act = jnp.tanh(pre.reshape(traj, nodes, slab) + drive[:, None, :])
    deriv = SCALE * jnp.einsum("kl,clg->ckg", cheb, states, precision=lax.Precision.HIGHEST)
    resid = deriv - (eps_gain * act - decay * states)
    delta = (-eps_gain * (1.0 - act * act) * resid).astype(jnp.bfloat16)
    dflat = delta.reshape(total, slab)
    grad_w = lax.dot_general(
        dflat, full, (((0,), (0,)), ((), ())), preferred_element_type=jnp.float32
    ).astype(jnp.bfloat16)
    back = jnp.dot(dflat, weights, preferred_element_type=jnp.float32)
    back = lax.psum_scatter(back, "row", scatter_dimension=1, tiled=True)
    grad_x = (
        SCALE * jnp.einsum("lk,clg->ckg", cheb, resid, precision=lax.Precision.HIGHEST)
        + decay * resid
        + back.reshape(traj, nodes, slab)
    )
    node_sums = jnp.sum(delta.astype(jnp.float32), axis=1)
    grad_table = jnp.dot(onehot.T, node_sums, precision=lax.Precision.HIGHEST)
    grad_eps = -jnp.sum(act * resid, axis=(0, 1))
    grad_decay = jnp.sum(states * resid, axis=(0, 1))
    return (grad_w, grad_x, grad_table, grad_eps, grad_decay)


def solution(mesh):
    chips = mesh.shape["row"] // 2
    in_specs = (
        P("rep", None, "row"),
        P(("rep", "row"), None),
        P("rep", "row"),
        P(("rep", "row")),
        P(("rep", "row")),
        P("rep"),
    )
    out_specs = (
        P(("rep", "row"), None),
        P("rep", None, "row"),
        P("rep", "row"),
        P(("rep", "row")),
        P(("rep", "row")),
    )

    def run(states, *others):
        if states.shape[0] == 1 and chips <= LONGEST_RING:
            return ring_body(chips, states, *others)
        return plain_body(states, *others)

    return jax.shard_map(run, mesh=mesh, in_specs=in_specs, out_specs=out_specs, check_vma=False)
```

```python
import functools

import jax
import jax.numpy as jnp
import numpy as np
from jax import lax
from jax.experimental import pallas as pl
from jax.experimental.pallas import tpu as pltpu
from jax.sharding import PartitionSpec as P

SCALE = 2.0 / 1024.0
VMEM_LIMIT = 4 * 2**20
BANDS = 8
FIRST_BANDS = 5
LONGEST_RING = 16


def cheb_matrix(count):
    index = np.arange(count)
    points = np.cos(np.pi * index / (count - 1))
    signs = np.where(index % 2 == 0, 1.0, -1.0)
    weight_c = signs * np.where((index == 0) | (index == count - 1), 2.0, 1.0)
    same = index[:, None] == index[None, :]
    spread = np.where(same, 1.0, points[:, None] - points[None, :])
    off = np.where(same, 0.0, weight_c[:, None] / weight_c[None, :] / spread)
    return jnp.asarray((off - np.diag(np.sum(off, axis=1))).astype(np.float32))


def chip_ring(chips):
    rows = 4
    cols = chips // rows
    cells = [(0, col) for col in range(cols)]
    for row in range(1, rows):
        span = range(1, cols)
        cells += [(row, col) for col in (reversed(span) if row % 2 else span)]
    cells += [(row, 0) for row in range(rows - 1, 0, -1)]
    return [row * cols + col for row, col in cells]


VMEM_REF = pl.BlockSpec(memory_space=pltpu.VMEM)
SMEM_REF = pl.BlockSpec(memory_space=pltpu.SMEM)
ANY_REF = pl.BlockSpec(memory_space=pl.ANY)
HBM_REF = pl.BlockSpec(memory_space=pltpu.HBM)


def cost(products, nodes, slab, rows):
    return pl.CostEstimate(
        flops=2 * products * nodes * slab * rows // 16,
        bytes_accessed=2 * products * slab * rows // 16,
        transcendentals=0,
    )


def call(kernel, out_shape, out_specs, scratch, costs, aliases=None, more=0):
    def run(operands, in_specs):
        return pl.pallas_call(
            kernel,
            out_shape=out_shape,
            in_specs=in_specs,
            out_specs=out_specs,
            scratch_shapes=scratch,
            input_output_aliases=aliases or {},
            compiler_params=pltpu.CompilerParams(vmem_limit_bytes=VMEM_LIMIT + more),
            cost_estimate=costs,
        )(*operands)

    return run


def columns_of(offs_ref, at, slab):
    return pl.ds(pl.multiple_of(offs_ref[at] * slab, slab), slab)


def load_bands(w_ref, bands, sems, first):
    copies = []
    for at, band_ref in enumerate(bands):
        tile = band_ref.shape[0]
        rows = pl.ds((first + at) * tile, tile)
        copies.append(pltpu.make_async_copy(w_ref.at[rows, :], band_ref, sems.at[at]))
        copies[-1].start()
    return copies


def product(bands, here, x_ref):
    rows = [band_ref[:, here] for band_ref in bands]
    return lax.dot_general(
        rows[0] if len(rows) == 1 else jnp.concatenate(rows, axis=0),
        x_ref[...], (((1,), (1,)), ((), ())), preferred_element_type=jnp.float32,
    )


def first_kernel(base, offs_ref, w_ref, x_ref, out_ref, *refs):
    bands, sems = refs[:-1], refs[-1]
    here = columns_of(offs_ref, base, x_ref.shape[1])
    tile = bands[0].shape[0]
    for at, copy in enumerate(load_bands(w_ref, bands, sems, 0)):
        copy.wait()
        out_ref[pl.ds(at * tile, tile), :] = product(bands[at : at + 1], here, x_ref)


def second_kernel(base, count, early, *refs):
    offs_ref, w_ref, acc_ref = refs[:3]
    bands, refs = refs[3 : 3 + early], refs[3 + early :]
    xs, out_ref, late, sems = refs[:count], refs[count], refs[count + 1 : -1], refs[-1]
    slab, tile = xs[0].shape[1], bands[0].shape[0]
    copies = load_bands(w_ref, late, sems, early)
    places = [columns_of(offs_ref, base + at, slab) for at in range(count)]
    for low in range(0, early, 2):
        pair = bands[low : low + 2]
        rows = pl.ds(low * tile, len(pair) * tile)
        total = acc_ref[rows, :]
        for at in range(1, count):
            total += product(pair, places[at], xs[at])
        out_ref[rows, :] = total
    for at, copy in enumerate(copies):
        copy.wait()
        rows = pl.ds((early + at) * tile, tile)
        total = product(late[at : at + 1], places[0], xs[0])
        for index in range(1, count):
            total += product(late[at : at + 1], places[index], xs[index])
        out_ref[rows, :] = total


def pre_kernel(base, count, many, offs_ref, acc_ref, *refs):
    bands, xs, out_ref = refs[:many], refs[many:-1], refs[-1]
    slab, tile = xs[0].shape[1], bands[0].shape[0]
    for low in range(0, many, 2):
        rows = pl.ds(low * tile, 2 * tile)
        total = acc_ref[rows, :]
        for at in range(count):
            total += product(bands[low : low + 2], columns_of(offs_ref, base + at, slab), xs[at])
        out_ref[rows, :] = total


def band_shapes(count, weights):
    return [pltpu.VMEM((weights.shape[0] // BANDS, weights.shape[1]), weights.dtype)] * count


def first_products(offs, base, x, weights):
    (nodes, slab), rows = x.shape, weights.shape[0]
    acc, *bands = call(
        functools.partial(first_kernel, base),
        [jax.ShapeDtypeStruct((rows, nodes), jnp.float32)] + band_shapes(FIRST_BANDS, weights),
        [VMEM_REF] * (1 + FIRST_BANDS),
        [pltpu.SemaphoreType.DMA((FIRST_BANDS,))],
        cost(1, nodes, slab, rows),
    )([offs, weights, x], [SMEM_REF, HBM_REF, VMEM_REF])
    return acc, bands


def second_products(offs, base, xs, weights, acc, bands):
    (nodes, slab), rows = xs[0].shape, weights.shape[0]
    late = BANDS - len(bands)
    acc, *others = call(
        functools.partial(second_kernel, base, len(xs), len(bands)),
        [jax.ShapeDtypeStruct((rows, nodes), jnp.float32)] + band_shapes(late, weights),
        [VMEM_REF] * (1 + late),
        [pltpu.SemaphoreType.DMA((late,))],
        cost(len(xs), nodes, slab, rows),
    )(
        [offs, weights, acc, *bands, *xs],
        [SMEM_REF, HBM_REF] + [VMEM_REF] * (1 + len(bands) + len(xs)),
    )
    return acc, bands + others


def add_products(offs, base, xs, acc, bands):
    nodes, slab = xs[0].shape
    rows, count = acc.shape[0], len(xs)
    return call(
        functools.partial(pre_kernel, base, count, len(bands)),
        jax.ShapeDtypeStruct((rows, nodes), jnp.float32),
        VMEM_REF,
        [],
        cost(count, nodes, slab, rows),
    )([offs, acc, *bands, *xs], [SMEM_REF] + [VMEM_REF] * (1 + len(bands) + count))


def cheb_kernel(turned, cheb_ref, array_ref, out_ref):
    out_ref[...] = SCALE * lax.dot_general(
        cheb_ref[...], array_ref[...], (((0 if turned else 1,), (0,)), ((), ())),
        precision=lax.Precision.HIGHEST, preferred_element_type=jnp.float32,
    )


def cheb_product(turned, cheb, array):
    return call(
        functools.partial(cheb_kernel, turned),
        jax.ShapeDtypeStruct(array.shape, jnp.float32),
        VMEM_REF,
        [],
        cost(1, *array.shape, array.shape[0]),
    )([cheb, array], [VMEM_REF] * 2)


def middle_kernel(base, many, offs_ref, perts_ref, x_ref, *refs):
    bands = refs[:many]
    acc_ref, deriv_ref, states_ref, pert_ref, eps_ref, decay_ref = refs[many:-6]
    resid_ref, delta_ref, delta_t_ref, table_ref, sum_eps_ref, sum_decay_ref = refs[-6:]
    tile = 2 * bands[0].shape[0]
    here = columns_of(offs_ref, base, x_ref.shape[1])
    pert = perts_ref[0]
    chosen = lax.broadcasted_iota(jnp.int32, (pert_ref.shape[0], tile), 0) == pert
    for at in range(many // 2):
        band = pl.ds(at * tile, tile)
        part = acc_ref[band, :] + product(bands[2 * at : 2 * at + 2], here, x_ref)
        states = states_ref[:, band]
        act = jnp.tanh(part.T + pert_ref[pl.ds(pert, 1), band])
        eps = eps_ref[:, band]
        resid = deriv_ref[:, band] - (eps * act - decay_ref[:, band] * states)
        delta = (-eps * (1.0 - act * act) * resid).astype(jnp.bfloat16)
        wide = delta.astype(jnp.float32)
        resid_ref[:, band] = resid
        delta_ref[:, band] = delta
        delta_t_ref[band, :] = wide.T.astype(jnp.bfloat16)
        table_ref[:, band] = jnp.where(chosen, jnp.sum(wide, axis=0, keepdims=True), 0.0)
        sum_eps_ref[:, band] = -jnp.sum(act * resid, axis=0, keepdims=True)
        sum_decay_ref[:, band] = jnp.sum(states * resid, axis=0, keepdims=True)


def middle(offs, perts, base, x, bands, acc, deriv, states, pert_table, eps, decay):
    nodes, slab = x.shape
    rows = acc.shape[0]
    wide = functools.partial(jax.ShapeDtypeStruct, dtype=jnp.float32)
    return call(
        functools.partial(middle_kernel, base, len(bands)),
        [
            wide((nodes, rows)),
            jax.ShapeDtypeStruct((nodes, rows), jnp.bfloat16),
            jax.ShapeDtypeStruct((rows, nodes), jnp.bfloat16),
            wide(pert_table.shape),
            wide((1, rows)),
            wide((1, rows)),
        ],
        [VMEM_REF] * 6,
        [],
        cost(2, nodes, slab, rows),
    )(
        [offs, perts, x, *bands, acc, deriv, states, pert_table, eps, decay],
        [SMEM_REF] * 2 + [VMEM_REF] * (7 + len(bands)),
    )


def share_kernel(at_places, cuts, many, offs_ref, delta_ref, *refs):
    bands, outs = refs[:many], refs[many:]
    nodes = delta_ref.shape[0]
    count = cuts[-1] // nodes
    slab, depth = outs[0].shape[1], 2 * bands[0].shape[0]
    tile = max(slab // 2, 128)
    for at, place in enumerate(at_places):
        for col in range(0, slab, tile):
            here = pl.ds(col, tile)
            there = pl.ds(pl.multiple_of(offs_ref[place] * slab + col, tile), tile)
            part = None
            for low in range(0, many, 2):
                pair = jnp.concatenate([ref[:, there] for ref in bands[low : low + 2]], axis=0)
                more = jnp.dot(
                    delta_ref[:, low // 2 * depth : (low // 2 + 1) * depth], pair,
                    preferred_element_type=jnp.float32,
                )
                part = more if part is None else part + more
            if at >= count:
                outs[len(cuts) - 1 + at - count][:, here] = part
                continue
            for start, end, out_ref in zip(cuts[:-1], cuts[1:], outs):
                low, high = max(start, at * nodes), min(end, (at + 1) * nodes)
                if low < high:
                    rows = part[low - at * nodes : high - at * nodes]
                    out_ref[low - start : high - start, here] = rows.astype(out_ref.dtype)


def shares(offs, at_places, delta, bands, slab, cuts):
    nodes, rows = delta.shape
    own = len(at_places) // 2
    heights = [end - start for start, end in zip(cuts[:-1], cuts[1:])]
    outs = call(
        functools.partial(share_kernel, at_places, cuts, len(bands)),
        [jax.ShapeDtypeStruct((height, slab), jnp.bfloat16) for height in heights]
        + [jax.ShapeDtypeStruct((nodes, slab), jnp.float32)] * own,
        [VMEM_REF] * (len(heights) + own),
        [],
        cost(len(at_places), nodes, slab, rows),
    )([offs, delta, *bands], [SMEM_REF] + [VMEM_REF] * (1 + len(bands)))
    return outs[: len(heights)], outs[len(heights) :]


def grad_w_kernel(base, count, *refs):
    offs_ref, delta_ref, xs = refs[0], refs[1], refs[2 : 2 + count]
    out_ref, mark_ref, held, sems = refs[-4:]
    slab = xs[0].shape[1]
    slots, _, width = held.shape
    step = min(256, width)
    mark_ref[...] = jnp.zeros_like(mark_ref)
    copies = []
    for at in range(count):
        for start in range(0, slab, width):
            slot = len(copies) % slots
            if len(copies) >= slots:
                copies[-slots].wait()
            for col in range(0, width, step):
                held[slot, :, col : col + step] = jnp.dot(
                    delta_ref[...], xs[at][:, start + col : start + col + step],
                    preferred_element_type=jnp.float32,
                ).astype(held.dtype)
            there = pl.ds(pl.multiple_of(offs_ref[base + at] * slab + start, width), width)
            copy = pltpu.make_async_copy(held.at[slot], out_ref.at[:, there], sems.at[slot])
            copy.start()
            copies.append(copy)
    for copy in copies[-slots:]:
        copy.wait()


def grad_w_piece(offs, base, delta_t, xs, so_far, mark, shape):
    rows, nodes = delta_t.shape
    slab, count = xs[0].shape[1], len(xs)
    width = max(slab // 2, 128)
    first = so_far is None
    return call(
        functools.partial(grad_w_kernel, base, count),
        [jax.ShapeDtypeStruct(shape, jnp.bfloat16), jax.ShapeDtypeStruct((8, 128), jnp.float32)],
        [ANY_REF, VMEM_REF],
        [pltpu.VMEM((4, rows, width), jnp.bfloat16), pltpu.SemaphoreType.DMA((4,))],
        cost(count, nodes, slab, rows),
        {} if first else {2 + count: 0},
        4 * 2 * rows * width,
    )(
        [offs, delta_t, *xs] + ([] if first else [so_far, mark]),
        [SMEM_REF] + [VMEM_REF] * (1 + count) + ([] if first else [ANY_REF] * 2),
    )


def ring_body(chips, states, weights, pert_table, eps_gain, decay, perts):
    _, nodes, slab = states.shape
    rows = weights.shape[0]
    order = chip_ring(chips)
    place = np.argsort(order)
    half, cut = chips // 2, nodes // 2

    near = [0]
    for step in range(1, half):
        near += [-step, step]
    near.append(half)
    listing = [(0, 0)]
    for step in range(half):
        now = [0] if step == 0 else [-step, step]
        then = [half] if step == half - 1 else [-step - 1, step + 1]
        listing += [(at, 1) for at in now] + [(at, 0) for at in then]
    listing.append((half, 1))
    sides = {key: at for at, key in enumerate(listing)}
    table = np.array(
        [
            [
                2 * order[(place[device // 2] + step) % chips] + (device % 2 ^ side)
                for step, side in listing
            ]
            for device in range(2 * chips)
        ],
        dtype=np.int32,
    )
    me = lax.axis_index("row")
    offs = lax.dynamic_slice(jnp.asarray(table), (me, 0), (1, 2 * chips)).reshape(-1)

    def ring(array, way):
        pairs = []
        for at, chip in enumerate(order):
            to = order[(at + way) % chips]
            pairs += [(2 * chip, 2 * to), (2 * chip + 1, 2 * to + 1)]
        return lax.ppermute(array, "row", pairs)

    def swap(array):
        return lax.ppermute(array, "row", [(i, i ^ 1) for i in range(2 * chips)])

    weights = pltpu.with_memory_space_constraint(weights, pltpu.HBM)
    cheb = cheb_matrix(nodes)
    flat = states.reshape(nodes, slab)
    xb = flat.astype(jnp.bfloat16)

    x = {(0, 0): xb}
    behind, ahead, base = xb, xb, 0
    for step in range(1, half + 1):
        if step < half:
            behind, ahead = ring(behind, 1), ring(ahead, -1)
        else:
            behind, ahead = ring(behind[:cut], 1), ring(ahead[cut:], -1)
        for now in [0] if step == 1 else [1 - step, step - 1]:
            x[now, 1] = swap(x[now, 0])
        count = {1: 1, 2: 3}.get(step, 4)
        xs = [x[key] for key in listing[base : base + count]]
        if step == 1:
            acc, bands = first_products(offs, 0, xs[0], weights)
        elif step == 2:
            acc, bands = second_products(offs, 0, [x[0, 0], *xs], weights, acc, bands)
        else:
            acc = add_products(offs, base, xs, acc, bands)
        base += count
        behind, ahead, acc = lax.optimization_barrier((behind, ahead, acc))
        if step < half:
            x[-step, 0], x[step, 0] = behind, ahead
        else:
            x[half, 0] = jnp.concatenate([behind, ahead], axis=0)
    x[half, 1] = swap(x[half, 0])
    xs = [x[key] for key in listing[base : base + 3]]
    acc = add_products(offs, base, xs, acc, bands)
    base += 3

    resid, delta, delta_t, grad_table, grad_eps, grad_decay = middle(
        offs, perts, base, x[half, 1], bands, acc, cheb_product(False, cheb, flat), flat,
        pert_table, eps_gain.reshape(1, rows), decay.reshape(1, rows),
    )

    def share(steps):
        count = len(steps)
        parts = 2 if count == 1 else 3
        cuts = [0] + [count * nodes * at // parts // 16 * 16 for at in range(1, parts)]
        cuts.append(count * nodes)
        places = [sides[step, side] for side in (1, 0) for step in steps]
        others, owns = shares(offs, places, delta, bands, slab, cuts)
        swapped = jnp.concatenate([swap(other) for other in others], axis=0)
        return [
            own + swapped[at * nodes : (at + 1) * nodes].astype(jnp.float32)
            for at, own in enumerate(owns)
        ]

    gate = lax.optimization_barrier
    first = len(listing) // 8
    each = (len(listing) - first) // (half - 1)
    cuts = [0] + [first + each * at for at in range(half - 1)] + [len(listing)]
    pieces = [(base, listing[base:end]) for base, end in zip(cuts[:-1], cuts[1:])]
    grad_w, mark = None, None

    def next_piece(grad_w, mark):
        base, keys = pieces.pop(0)
        return grad_w_piece(
            offs, base, delta_t, [x[key] for key in keys], grad_w, mark, weights.shape
        )

    (far,) = share([half])
    far = far.astype(jnp.bfloat16)
    grad_w, mark = next_piece(grad_w, mark)
    far, offs, mark = gate((far, offs, mark))
    ahead, behind = ring(far[:cut], 1), ring(far[cut:], -1)
    for step in range(half - 1, -1, -1):
        if step > 0:
            own_ahead, own_behind = share([step, -step])
        else:
            (near_share,) = share([0])
        if step < half - 1:
            grad_w, mark = next_piece(grad_w, mark)
            ahead, behind, mark = gate((ahead, behind, mark))
        if step == 0:
            break
        ahead, behind = ahead.astype(jnp.float32), behind.astype(jnp.float32)
        if step == half - 1:
            ahead = jnp.concatenate([own_ahead[:cut] + ahead, own_ahead[cut:]], axis=0)
            behind = jnp.concatenate([own_behind[:cut], own_behind[cut:] + behind], axis=0)
        else:
            ahead, behind = own_ahead + ahead, own_behind + behind
        ahead, behind = ahead.astype(jnp.bfloat16), behind.astype(jnp.bfloat16)
        ahead, behind, offs = gate((ahead, behind, offs))
        ahead, behind = ring(ahead, 1), ring(behind, -1)

    local = gate(cheb_product(True, cheb, resid) + decay * resid)
    grad_x = local + near_share + ahead.astype(jnp.float32) + behind.astype(jnp.float32)
    grad_x = grad_x.reshape(states.shape)
    return (grad_w, grad_x, grad_table, grad_eps.reshape(rows), grad_decay.reshape(rows))


def plain_body(states, weights, pert_table, eps_gain, decay, perts):
    traj, nodes, slab = states.shape
    total = traj * nodes
    cheb = cheb_matrix(nodes)
    xb = states.astype(jnp.bfloat16).reshape(total, slab)
    full = lax.all_gather(xb, "row", axis=1, tiled=True)
    pre = lax.dot_general(
        full, weights, (((1,), (1,)), ((), ())), preferred_element_type=jnp.float32
    )
    onehot = (perts[:, None] == jnp.arange(pert_table.shape[0], dtype=jnp.int32)[None, :]).astype(
        jnp.float32
    )
    drive = jnp.dot(onehot, pert_table, precision=lax.Precision.HIGHEST)
    act = jnp.tanh(pre.reshape(traj, nodes, slab) + drive[:, None, :])
    deriv = SCALE * jnp.einsum("kl,clg->ckg", cheb, states, precision=lax.Precision.HIGHEST)
    resid = deriv - (eps_gain * act - decay * states)
    delta = (-eps_gain * (1.0 - act * act) * resid).astype(jnp.bfloat16)
    dflat = delta.reshape(total, slab)
    grad_w = lax.dot_general(
        dflat, full, (((0,), (0,)), ((), ())), preferred_element_type=jnp.float32
    ).astype(jnp.bfloat16)
    back = jnp.dot(dflat, weights, preferred_element_type=jnp.float32)
    back = lax.psum_scatter(back, "row", scatter_dimension=1, tiled=True)
    grad_x = (
        SCALE * jnp.einsum("lk,clg->ckg", cheb, resid, precision=lax.Precision.HIGHEST)
        + decay * resid
        + back.reshape(traj, nodes, slab)
    )
    node_sums = jnp.sum(delta.astype(jnp.float32), axis=1)
    grad_table = jnp.dot(onehot.T, node_sums, precision=lax.Precision.HIGHEST)
    grad_eps = -jnp.sum(act * resid, axis=(0, 1))
    grad_decay = jnp.sum(states * resid, axis=(0, 1))
    return (grad_w, grad_x, grad_table, grad_eps, grad_decay)


def solution(mesh):
    chips = mesh.shape["row"] // 2
    in_specs = (
        P("rep", None, "row"),
        P(("rep", "row"), None),
        P("rep", "row"),
        P(("rep", "row")),
        P(("rep", "row")),
        P("rep"),
    )
    out_specs = (
        P(("rep", "row"), None),
        P("rep", None, "row"),
        P("rep", "row"),
        P(("rep", "row")),
        P(("rep", "row")),
    )

    def run(states, *others):
        if states.shape[0] == 1 and chips <= LONGEST_RING:
            return ring_body(chips, states, *others)
        return plain_body(states, *others)

    return jax.shard_map(run, mesh=mesh, in_specs=in_specs, out_specs=out_specs, check_vma=False)
```

```python
import functools

import jax
import jax.numpy as jnp
import numpy as np
from jax import lax
from jax.experimental import pallas as pl
from jax.experimental.pallas import tpu as pltpu
from jax.sharding import PartitionSpec as P

SCALE = 2.0 / 1024.0
VMEM_LIMIT = 4 * 2**20
BANDS = 8
FIRST_BANDS = 5
LONGEST_RING = 16


def cheb_matrix(count):
    index = np.arange(count)
    points = np.cos(np.pi * index / (count - 1))
    signs = np.where(index % 2 == 0, 1.0, -1.0)
    weight_c = signs * np.where((index == 0) | (index == count - 1), 2.0, 1.0)
    same = index[:, None] == index[None, :]
    spread = np.where(same, 1.0, points[:, None] - points[None, :])
    off = np.where(same, 0.0, weight_c[:, None] / weight_c[None, :] / spread)
    return jnp.asarray((off - np.diag(np.sum(off, axis=1))).astype(np.float32))


def chip_ring(chips):
    rows = 4
    cols = chips // rows
    cells = [(0, col) for col in range(cols)]
    for row in range(1, rows):
        span = range(1, cols)
        cells += [(row, col) for col in (reversed(span) if row % 2 else span)]
    cells += [(row, 0) for row in range(rows - 1, 0, -1)]
    return [row * cols + col for row, col in cells]


VMEM_REF = pl.BlockSpec(memory_space=pltpu.VMEM)
SMEM_REF = pl.BlockSpec(memory_space=pltpu.SMEM)
ANY_REF = pl.BlockSpec(memory_space=pl.ANY)
HBM_REF = pl.BlockSpec(memory_space=pltpu.HBM)


def cost(products, nodes, slab, rows):
    return pl.CostEstimate(
        flops=2 * products * nodes * slab * rows // 16,
        bytes_accessed=2 * products * slab * rows // 16,
        transcendentals=0,
    )


def call(kernel, out_shape, out_specs, scratch, costs, aliases=None, more=0):
    def run(operands, in_specs):
        return pl.pallas_call(
            kernel,
            out_shape=out_shape,
            in_specs=in_specs,
            out_specs=out_specs,
            scratch_shapes=scratch,
            input_output_aliases=aliases or {},
            compiler_params=pltpu.CompilerParams(vmem_limit_bytes=VMEM_LIMIT + more),
            cost_estimate=costs,
        )(*operands)

    return run


def columns_of(offs_ref, at, slab):
    return pl.ds(pl.multiple_of(offs_ref[at] * slab, slab), slab)


def load_bands(w_ref, bands, sems, first):
    copies = []
    for at, band_ref in enumerate(bands):
        tile = band_ref.shape[0]
        rows = pl.ds((first + at) * tile, tile)
        copies.append(pltpu.make_async_copy(w_ref.at[rows, :], band_ref, sems.at[at]))
        copies[-1].start()
    return copies


def product(bands, here, x_ref):
    rows = [band_ref[:, here] for band_ref in bands]
    return lax.dot_general(
        rows[0] if len(rows) == 1 else jnp.concatenate(rows, axis=0),
        x_ref[...], (((1,), (1,)), ((), ())), preferred_element_type=jnp.float32,
    )


def first_kernel(base, offs_ref, w_ref, x_ref, out_ref, *refs):
    bands, sems = refs[:-1], refs[-1]
    here = columns_of(offs_ref, base, x_ref.shape[1])
    tile = bands[0].shape[0]
    for at, copy in enumerate(load_bands(w_ref, bands, sems, 0)):
        copy.wait()
        out_ref[pl.ds(at * tile, tile), :] = product(bands[at : at + 1], here, x_ref)


def second_kernel(base, count, early, *refs):
    offs_ref, w_ref, acc_ref = refs[:3]
    bands, refs = refs[3 : 3 + early], refs[3 + early :]
    xs, out_ref, late, sems = refs[:count], refs[count], refs[count + 1 : -1], refs[-1]
    slab, tile = xs[0].shape[1], bands[0].shape[0]
    copies = load_bands(w_ref, late, sems, early)
    places = [columns_of(offs_ref, base + at, slab) for at in range(count)]
    for low in range(0, early, 2):
        pair = bands[low : low + 2]
        rows = pl.ds(low * tile, len(pair) * tile)
        total = acc_ref[rows, :]
        for at in range(1, count):
            total += product(pair, places[at], xs[at])
        out_ref[rows, :] = total
    for at, copy in enumerate(copies):
        copy.wait()
        rows = pl.ds((early + at) * tile, tile)
        total = product(late[at : at + 1], places[0], xs[0])
        for index in range(1, count):
            total += product(late[at : at + 1], places[index], xs[index])
        out_ref[rows, :] = total


def pre_kernel(base, count, many, offs_ref, acc_ref, *refs):
    bands, xs, out_ref = refs[:many], refs[many:-1], refs[-1]
    slab, tile = xs[0].shape[1], bands[0].shape[0]
    for low in range(0, many, 2):
        rows = pl.ds(low * tile, 2 * tile)
        total = acc_ref[rows, :]
        for at in range(count):
            total += product(bands[low : low + 2], columns_of(offs_ref, base + at, slab), xs[at])
        out_ref[rows, :] = total


def band_shapes(count, weights):
    return [pltpu.VMEM((weights.shape[0] // BANDS, weights.shape[1]), weights.dtype)] * count


def first_products(offs, base, x, weights):
    (nodes, slab), rows = x.shape, weights.shape[0]
    acc, *bands = call(
        functools.partial(first_kernel, base),
        [jax.ShapeDtypeStruct((rows, nodes), jnp.float32)] + band_shapes(FIRST_BANDS, weights),
        [VMEM_REF] * (1 + FIRST_BANDS),
        [pltpu.SemaphoreType.DMA((FIRST_BANDS,))],
        cost(1, nodes, slab, rows),
    )([offs, weights, x], [SMEM_REF, HBM_REF, VMEM_REF])
    return acc, bands


def second_products(offs, base, xs, weights, acc, bands):
    (nodes, slab), rows = xs[0].shape, weights.shape[0]
    late = BANDS - len(bands)
    acc, *others = call(
        functools.partial(second_kernel, base, len(xs), len(bands)),
        [jax.ShapeDtypeStruct((rows, nodes), jnp.float32)] + band_shapes(late, weights),
        [VMEM_REF] * (1 + late),
        [pltpu.SemaphoreType.DMA((late,))],
        cost(len(xs), nodes, slab, rows),
    )(
        [offs, weights, acc, *bands, *xs],
        [SMEM_REF, HBM_REF] + [VMEM_REF] * (1 + len(bands) + len(xs)),
    )
    return acc, bands + others


def add_products(offs, base, xs, acc, bands):
    nodes, slab = xs[0].shape
    rows, count = acc.shape[0], len(xs)
    return call(
        functools.partial(pre_kernel, base, count, len(bands)),
        jax.ShapeDtypeStruct((rows, nodes), jnp.float32),
        VMEM_REF,
        [],
        cost(count, nodes, slab, rows),
    )([offs, acc, *bands, *xs], [SMEM_REF] + [VMEM_REF] * (1 + len(bands) + count))


def cheb_dot(turned, cheb_ref, array_ref):
    return SCALE * lax.dot_general(
        cheb_ref[...], array_ref[...], (((0 if turned else 1,), (0,)), ((), ())),
        precision=lax.Precision.HIGHEST, preferred_element_type=jnp.float32,
    )


def deriv_kernel(perts_ref, cheb_ref, states_ref, pert_ref, deriv_ref, drive_ref, chosen_ref):
    pert = perts_ref[0]
    deriv_ref[...] = cheb_dot(False, cheb_ref, states_ref)
    drive_ref[...] = pert_ref[pl.ds(pert, 1), :]
    rows = lax.broadcasted_iota(jnp.int32, chosen_ref.shape, 0)
    chosen_ref[...] = (rows == pert).astype(jnp.float32)


def derivatives(perts, cheb, states, pert_table):
    return call(
        deriv_kernel,
        [
            jax.ShapeDtypeStruct(states.shape, jnp.float32),
            jax.ShapeDtypeStruct((1, states.shape[1]), jnp.float32),
            jax.ShapeDtypeStruct(pert_table.shape, jnp.float32),
        ],
        [VMEM_REF] * 3,
        [],
        cost(1, *states.shape, states.shape[0]),
    )([perts, cheb, states, pert_table], [SMEM_REF] + [VMEM_REF] * 3)


def local_kernel(cheb_ref, resid_ref, decay_ref, out_ref):
    out_ref[...] = cheb_dot(True, cheb_ref, resid_ref) + decay_ref[...] * resid_ref[...]


def local_terms(cheb, resid, decay):
    return call(
        local_kernel,
        jax.ShapeDtypeStruct(resid.shape, jnp.float32),
        VMEM_REF,
        [],
        cost(1, *resid.shape, resid.shape[0]),
    )([cheb, resid, decay], [VMEM_REF] * 3)


def middle_kernel(base, many, offs_ref, x_ref, *refs):
    bands = refs[:many]
    acc_ref, deriv_ref, drive_ref, chosen_ref, states_ref, eps_ref, decay_ref = refs[many:-6]
    resid_ref, delta_ref, delta_t_ref, table_ref, sum_eps_ref, sum_decay_ref = refs[-6:]
    tile = 2 * bands[0].shape[0]
    here = columns_of(offs_ref, base, x_ref.shape[1])
    for at in range(many // 2):
        band = pl.ds(at * tile, tile)
        part = acc_ref[band, :] + product(bands[2 * at : 2 * at + 2], here, x_ref)
        states = states_ref[:, band]
        act = jnp.tanh(part.T + drive_ref[:, band])
        eps = eps_ref[:, band]
        resid = deriv_ref[:, band] - (eps * act - decay_ref[:, band] * states)
        delta = (-eps * (1.0 - act * act) * resid).astype(jnp.bfloat16)
        wide = delta.astype(jnp.float32)
        resid_ref[:, band] = resid
        delta_ref[:, band] = delta
        delta_t_ref[band, :] = wide.T.astype(jnp.bfloat16)
        table_ref[:, band] = chosen_ref[:, band] * jnp.sum(wide, axis=0, keepdims=True)
        sum_eps_ref[:, band] = -jnp.sum(act * resid, axis=0, keepdims=True)
        sum_decay_ref[:, band] = jnp.sum(states * resid, axis=0, keepdims=True)


def middle(offs, base, x, bands, acc, derivs, states, eps, decay):
    nodes, slab = x.shape
    rows = acc.shape[0]
    wide = functools.partial(jax.ShapeDtypeStruct, dtype=jnp.float32)
    return call(
        functools.partial(middle_kernel, base, len(bands)),
        [
            wide((nodes, rows)),
            jax.ShapeDtypeStruct((nodes, rows), jnp.bfloat16),
            jax.ShapeDtypeStruct((rows, nodes), jnp.bfloat16),
            wide(derivs[2].shape),
            wide((1, rows)),
            wide((1, rows)),
        ],
        [VMEM_REF] * 6,
        [],
        cost(2, nodes, slab, rows),
    )(
        [offs, x, *bands, acc, *derivs, states, eps, decay],
        [SMEM_REF] + [VMEM_REF] * (8 + len(bands)),
    )


def grad_w_part(base, offs_ref, delta_t_ref, xs, out_ref, held, sems):
    slab = xs[0].shape[1]
    slots, _, width = held.shape
    step = min(256, width)
    copies = []
    for at, x_ref in enumerate(xs):
        for start in range(0, slab, width):
            slot = len(copies) % slots
            if len(copies) >= slots:
                copies[-slots].wait()
            for col in range(0, width, step):
                held[slot, :, col : col + step] = jnp.dot(
                    delta_t_ref[...], x_ref[:, start + col : start + col + step],
                    preferred_element_type=jnp.float32,
                ).astype(held.dtype)
            there = pl.ds(pl.multiple_of(offs_ref[base + at] * slab + start, width), width)
            copy = pltpu.make_async_copy(held.at[slot], out_ref.at[:, there], sems.at[slot])
            copy.start()
            copies.append(copy)
    return copies[-slots:]


def share_part(places, offs_ref, delta_ref, bands, outs):
    depth = 2 * bands[0].shape[0]
    for place, out_ref in zip(places, outs):
        slab = out_ref.shape[1]
        tile = max(slab // 2, 128)
        for col in range(0, slab, tile):
            there = pl.ds(pl.multiple_of(offs_ref[place] * slab + col, tile), tile)
            part = None
            for low in range(0, len(bands), 2):
                pair = jnp.concatenate([ref[:, there] for ref in bands[low : low + 2]], axis=0)
                more = jnp.dot(
                    delta_ref[:, low // 2 * depth : (low // 2 + 1) * depth], pair,
                    preferred_element_type=jnp.float32,
                )
                part = more if part is None else part + more
            out_ref[:, pl.ds(col, tile)] = part.astype(out_ref.dtype)


def sums_kernel(base, count, places, many, first, *refs):
    offs_ref, delta_ref, delta_t_ref = refs[:3]
    xs, bands = refs[3 : 3 + count], refs[3 + count : 3 + count + many]
    refs = refs[3 + count + many + (0 if first else 1) :]
    outs, copies = refs[: len(places)], []
    if count:
        out_ref, mark_ref, held, sems = refs[len(places) :]
        mark_ref[...] = jnp.zeros_like(mark_ref)
        copies = grad_w_part(base, offs_ref, delta_t_ref, xs, out_ref, held, sems)
    share_part(places, offs_ref, delta_ref, bands, outs)
    for copy in copies:
        copy.wait()


def sums(offs, base, xs, places, delta, delta_t, bands, slab, so_far, shape):
    nodes, rows = delta.shape
    count, own = len(xs), len(places) // 2
    width = max(slab // 2, 128)
    first = so_far is None
    shapes = [jax.ShapeDtypeStruct((nodes, slab), jnp.bfloat16)] * own
    shapes += [jax.ShapeDtypeStruct((nodes, slab), jnp.float32)] * own
    specs, scratch, more = [VMEM_REF] * (2 * own), [], 0
    if count:
        shapes += [
            jax.ShapeDtypeStruct(shape, jnp.bfloat16),
            jax.ShapeDtypeStruct((8, 128), jnp.float32),
        ]
        specs += [ANY_REF, VMEM_REF]
        scratch = [pltpu.VMEM((4, rows, width), jnp.bfloat16), pltpu.SemaphoreType.DMA((4,))]
        more = 4 * 2 * rows * width
    operands = [offs, delta, delta_t, *xs, *bands] + ([] if first else [so_far])
    outs = call(
        functools.partial(sums_kernel, base, count, places, len(bands), first),
        shapes,
        specs,
        scratch,
        cost(count + 2 * own, nodes, slab, rows),
        {} if first else {len(operands) - 1: 2 * own},
        more,
    )(
        operands,
        [SMEM_REF] + [VMEM_REF] * (2 + count + len(bands)) + ([] if first else [ANY_REF]),
    )
    return outs[:own], outs[own : 2 * own], outs[2 * own :]


def ring_body(chips, states, weights, pert_table, eps_gain, decay, perts):
    _, nodes, slab = states.shape
    rows = weights.shape[0]
    order = chip_ring(chips)
    place = np.argsort(order)
    half, cut = chips // 2, nodes // 2

    near = [0]
    for step in range(1, half):
        near += [-step, step]
    near.append(half)
    listing = [(0, 0)]
    for step in range(half):
        now = [0] if step == 0 else [-step, step]
        then = [half] if step == half - 1 else [-step - 1, step + 1]
        listing += [(at, 1) for at in now] + [(at, 0) for at in then]
    listing.append((half, 1))
    sides = {key: at for at, key in enumerate(listing)}
    table = np.array(
        [
            [
                2 * order[(place[device // 2] + step) % chips] + (device % 2 ^ side)
                for step, side in listing
            ]
            for device in range(2 * chips)
        ],
        dtype=np.int32,
    )
    me = lax.axis_index("row")
    offs = lax.dynamic_slice(jnp.asarray(table), (me, 0), (1, 2 * chips)).reshape(-1)

    def ring(array, way):
        pairs = []
        for at, chip in enumerate(order):
            to = order[(at + way) % chips]
            pairs += [(2 * chip, 2 * to), (2 * chip + 1, 2 * to + 1)]
        return lax.ppermute(array, "row", pairs)

    def swap(array):
        return lax.ppermute(array, "row", [(i, i ^ 1) for i in range(2 * chips)])

    weights = pltpu.with_memory_space_constraint(weights, pltpu.HBM)
    cheb = cheb_matrix(nodes)
    flat = states.reshape(nodes, slab)
    xb = flat.astype(jnp.bfloat16)

    gate = lax.optimization_barrier

    x = {(0, 0): xb}
    behind, ahead, base = xb, xb, 0
    for step in range(1, half + 1):
        if step < half:
            behind, ahead = ring(behind, 1), ring(ahead, -1)
        else:
            behind, ahead = ring(behind[:cut], 1), ring(ahead[cut:], -1)
        for now in [0] if step == 1 else [1 - step, step - 1]:
            x[now, 1] = swap(x[now, 0])
        count = {1: 1, 2: 3}.get(step, 4)
        xs = [x[key] for key in listing[base : base + count]]
        if step == 1:
            acc, bands = first_products(offs, 0, xs[0], weights)
        elif step == 2:
            acc, bands = second_products(offs, 0, [x[0, 0], *xs], weights, acc, bands)
        else:
            acc = add_products(offs, base, xs, acc, bands)
        base += count
        if step == half - 1:
            derivs = derivatives(perts, cheb, flat, pert_table)
            acc, *derivs = gate((acc, *derivs))
        behind, ahead, acc = gate((behind, ahead, acc))
        if step < half:
            x[-step, 0], x[step, 0] = behind, ahead
        else:
            x[half, 0] = jnp.concatenate([behind, ahead], axis=0)
    x[half, 1] = swap(x[half, 0])
    xs = [x[key] for key in listing[base : base + 3]]
    acc = add_products(offs, base, xs, acc, bands)
    base += 3

    decay = decay.reshape(1, rows)
    resid, delta, delta_t, grad_table, grad_eps, grad_decay = middle(
        offs, base, x[half, 1], bands, acc, derivs, flat, eps_gain.reshape(1, rows), decay
    )

    grad_w, base = None, 0

    def work(offs, count, steps, grad_w, base):
        places = [sides[step, side] for side in (1, 0) for step in steps]
        xs = [x[key] for key in listing[base : base + count]]
        others, owns, rest = sums(
            offs, base, xs, places, delta, delta_t, bands, slab, grad_w, weights.shape
        )
        grad_w, mark = rest if count else (grad_w, None)
        return others, owns, grad_w, base + count, mark

    def joined(others, owns):
        return [own + swap(other).astype(jnp.float32) for other, own in zip(others, owns)]

    counts = [2, 5, 5]
    counts.append(len(listing) - sum(counts))
    others, owns, _, _, _ = work(offs, 0, [half], None, 0)
    (far,) = joined(others, owns)
    others, owns, _, _, _ = work(offs, 0, [half - 1, 1 - half], None, 0)
    far, offs, *owns = gate((far.astype(jnp.bfloat16), offs, *owns))
    own_ahead, own_behind = joined(others, owns)
    ahead, behind = ring(far[:cut], 1), ring(far[cut:], -1)
    for step in range(half - 1, -1, -1):
        steps = [] if step == 0 else [0] if step == 1 else [step - 1, 1 - step]
        others, owns, grad_w, base, mark = work(offs, counts.pop(0), steps, grad_w, base)
        if step == 0:
            break
        ahead, behind, *owns = gate((ahead, behind, *owns))
        ahead, behind = ahead.astype(jnp.float32), behind.astype(jnp.float32)
        if step == half - 1:
            ahead = jnp.concatenate([own_ahead[:cut] + ahead, own_ahead[cut:]], axis=0)
            behind = jnp.concatenate([own_behind[:cut], own_behind[cut:] + behind], axis=0)
        else:
            ahead, behind = own_ahead + ahead, own_behind + behind
        ahead, behind = ahead.astype(jnp.bfloat16), behind.astype(jnp.bfloat16)
        if step > 1:
            own_ahead, own_behind = joined(others, owns)
        else:
            (near_share,) = joined(others, owns)
        ahead, behind, offs = gate((ahead, behind, offs))
        ahead, behind = ring(ahead, 1), ring(behind, -1)

    local = local_terms(cheb, resid, decay)
    ahead, behind, local = gate((ahead, behind, local))
    grad_x = local + near_share + ahead.astype(jnp.float32) + behind.astype(jnp.float32)
    grad_x = grad_x.reshape(states.shape)
    return (grad_w, grad_x, grad_table, grad_eps.reshape(rows), grad_decay.reshape(rows))


def plain_body(states, weights, pert_table, eps_gain, decay, perts):
    traj, nodes, slab = states.shape
    total = traj * nodes
    cheb = cheb_matrix(nodes)
    xb = states.astype(jnp.bfloat16).reshape(total, slab)
    full = lax.all_gather(xb, "row", axis=1, tiled=True)
    pre = lax.dot_general(
        full, weights, (((1,), (1,)), ((), ())), preferred_element_type=jnp.float32
    )
    onehot = (perts[:, None] == jnp.arange(pert_table.shape[0], dtype=jnp.int32)[None, :]).astype(
        jnp.float32
    )
    drive = jnp.dot(onehot, pert_table, precision=lax.Precision.HIGHEST)
    act = jnp.tanh(pre.reshape(traj, nodes, slab) + drive[:, None, :])
    deriv = SCALE * jnp.einsum("kl,clg->ckg", cheb, states, precision=lax.Precision.HIGHEST)
    resid = deriv - (eps_gain * act - decay * states)
    delta = (-eps_gain * (1.0 - act * act) * resid).astype(jnp.bfloat16)
    dflat = delta.reshape(total, slab)
    grad_w = lax.dot_general(
        dflat, full, (((0,), (0,)), ((), ())), preferred_element_type=jnp.float32
    ).astype(jnp.bfloat16)
    back = jnp.dot(dflat, weights, preferred_element_type=jnp.float32)
    back = lax.psum_scatter(back, "row", scatter_dimension=1, tiled=True)
    grad_x = (
        SCALE * jnp.einsum("lk,clg->ckg", cheb, resid, precision=lax.Precision.HIGHEST)
        + decay * resid
        + back.reshape(traj, nodes, slab)
    )
    node_sums = jnp.sum(delta.astype(jnp.float32), axis=1)
    grad_table = jnp.dot(onehot.T, node_sums, precision=lax.Precision.HIGHEST)
    grad_eps = -jnp.sum(act * resid, axis=(0, 1))
    grad_decay = jnp.sum(states * resid, axis=(0, 1))
    return (grad_w, grad_x, grad_table, grad_eps, grad_decay)


def solution(mesh):
    chips = mesh.shape["row"] // 2
    in_specs = (
        P("rep", None, "row"),
        P(("rep", "row"), None),
        P("rep", "row"),
        P(("rep", "row")),
        P(("rep", "row")),
        P("rep"),
    )
    out_specs = (
        P(("rep", "row"), None),
        P("rep", None, "row"),
        P("rep", "row"),
        P(("rep", "row")),
        P(("rep", "row")),
    )

    def run(states, *others):
        if states.shape[0] == 1 and chips <= LONGEST_RING:
            return ring_body(chips, states, *others)
        return plain_body(states, *others)

    return jax.shard_map(run, mesh=mesh, in_specs=in_specs, out_specs=out_specs, check_vma=False)
```

```python
import functools

import jax
import jax.numpy as jnp
import numpy as np
from jax import lax
from jax.experimental import pallas as pl
from jax.experimental.pallas import tpu as pltpu
from jax.sharding import PartitionSpec as P

SCALE = 2.0 / 1024.0
VMEM_LIMIT = 4 * 2**20
BANDS = 8
FIRST_BANDS = 4
LONGEST_RING = 16


def cheb_matrix(count):
    index = np.arange(count)
    points = np.cos(np.pi * index / (count - 1))
    signs = np.where(index % 2 == 0, 1.0, -1.0)
    weight_c = signs * np.where((index == 0) | (index == count - 1), 2.0, 1.0)
    same = index[:, None] == index[None, :]
    spread = np.where(same, 1.0, points[:, None] - points[None, :])
    off = np.where(same, 0.0, weight_c[:, None] / weight_c[None, :] / spread)
    return jnp.asarray((off - np.diag(np.sum(off, axis=1))).astype(np.float32))


def chip_ring(chips):
    rows = 4
    cols = chips // rows
    cells = [(0, col) for col in range(cols)]
    for row in range(1, rows):
        span = range(1, cols)
        cells += [(row, col) for col in (reversed(span) if row % 2 else span)]
    cells += [(row, 0) for row in range(rows - 1, 0, -1)]
    return [row * cols + col for row, col in cells]


VMEM_REF = pl.BlockSpec(memory_space=pltpu.VMEM)
SMEM_REF = pl.BlockSpec(memory_space=pltpu.SMEM)
ANY_REF = pl.BlockSpec(memory_space=pl.ANY)
HBM_REF = pl.BlockSpec(memory_space=pltpu.HBM)


def cost(products, nodes, slab, rows):
    return pl.CostEstimate(
        flops=2 * products * nodes * slab * rows // 16,
        bytes_accessed=2 * products * slab * rows // 16,
        transcendentals=0,
    )


def call(kernel, out_shape, out_specs, scratch, costs, aliases=None, more=0):
    def run(operands, in_specs):
        return pl.pallas_call(
            kernel,
            out_shape=out_shape,
            in_specs=in_specs,
            out_specs=out_specs,
            scratch_shapes=scratch,
            input_output_aliases=aliases or {},
            compiler_params=pltpu.CompilerParams(vmem_limit_bytes=VMEM_LIMIT + more),
            cost_estimate=costs,
        )(*operands)

    return run


def columns_of(offs_ref, at, slab):
    return pl.ds(pl.multiple_of(offs_ref[at] * slab, slab), slab)


def load_bands(w_ref, bands, sems, first):
    copies = []
    for at, band_ref in enumerate(bands):
        tile = band_ref.shape[0]
        rows = pl.ds((first + at) * tile, tile)
        copies.append(pltpu.make_async_copy(w_ref.at[rows, :], band_ref, sems.at[at]))
        copies[-1].start()
    return copies


def product(bands, here, x_ref):
    rows = [band_ref[:, here] for band_ref in bands]
    return lax.dot_general(
        rows[0] if len(rows) == 1 else jnp.concatenate(rows, axis=0),
        x_ref[...], (((1,), (1,)), ((), ())), preferred_element_type=jnp.float32,
    )


def first_kernel(base, offs_ref, perts_ref, w_ref, x_ref, out_ref, *refs):
    bands, sems = refs[:-1], refs[-1]
    here = columns_of(offs_ref, base, x_ref.shape[1])
    tile = bands[0].shape[0]
    for at, copy in enumerate(load_bands(w_ref, bands, sems, 0)):
        copy.wait()
        out_ref[pl.ds(at * tile, tile), :] = product(bands[at : at + 1], here, x_ref)


def second_kernel(base, count, early, *refs):
    offs_ref, w_ref, acc_ref = refs[:3]
    bands, refs = refs[3 : 3 + early], refs[3 + early :]
    xs, out_ref, late, sems = refs[:count], refs[count], refs[count + 1 : -1], refs[-1]
    slab, tile = xs[0].shape[1], bands[0].shape[0]
    copies = load_bands(w_ref, late, sems, early)
    places = [columns_of(offs_ref, base + at, slab) for at in range(count)]
    rows = pl.ds(0, early * tile)
    total = acc_ref[rows, :]
    for at in range(1, count):
        total += product(bands, places[at], xs[at])
    out_ref[rows, :] = total
    for copy in copies:
        copy.wait()
    total = product(late, places[0], xs[0])
    for at in range(1, count):
        total += product(late, places[at], xs[at])
    out_ref[pl.ds(early * tile, len(late) * tile), :] = total


def pre_kernel(base, count, many, offs_ref, acc_ref, *refs):
    bands, xs, out_ref = refs[:many], refs[many:-1], refs[-1]
    slab, tile = xs[0].shape[1], bands[0].shape[0]
    for low in range(0, many, 4):
        rows = pl.ds(low * tile, 4 * tile)
        total = acc_ref[rows, :]
        for at in range(count):
            total += product(bands[low : low + 4], columns_of(offs_ref, base + at, slab), xs[at])
        out_ref[rows, :] = total


def band_shapes(count, weights):
    return [pltpu.VMEM((weights.shape[0] // BANDS, weights.shape[1]), weights.dtype)] * count


def first_products(offs, perts, base, x, weights):
    (nodes, slab), rows = x.shape, weights.shape[0]
    acc, *bands = call(
        functools.partial(first_kernel, base),
        [jax.ShapeDtypeStruct((rows, nodes), jnp.float32)] + band_shapes(FIRST_BANDS, weights),
        [VMEM_REF] * (1 + FIRST_BANDS),
        [pltpu.SemaphoreType.DMA((FIRST_BANDS,))],
        cost(1, nodes, slab, rows),
    )([offs, perts, weights, x], [SMEM_REF, SMEM_REF, HBM_REF, VMEM_REF])
    return acc, bands


def second_products(offs, base, xs, weights, acc, bands):
    (nodes, slab), rows = xs[0].shape, weights.shape[0]
    late = BANDS - len(bands)
    acc, *others = call(
        functools.partial(second_kernel, base, len(xs), len(bands)),
        [jax.ShapeDtypeStruct((rows, nodes), jnp.float32)] + band_shapes(late, weights),
        [VMEM_REF] * (1 + late),
        [pltpu.SemaphoreType.DMA((late,))],
        cost(len(xs), nodes, slab, rows),
    )(
        [offs, weights, acc, *bands, *xs],
        [SMEM_REF, HBM_REF] + [VMEM_REF] * (1 + len(bands) + len(xs)),
    )
    return acc, bands + others


def add_products(offs, base, xs, acc, bands):
    nodes, slab = xs[0].shape
    rows, count = acc.shape[0], len(xs)
    return call(
        functools.partial(pre_kernel, base, count, len(bands)),
        jax.ShapeDtypeStruct((rows, nodes), jnp.float32),
        VMEM_REF,
        [],
        cost(count, nodes, slab, rows),
    )([offs, acc, *bands, *xs], [SMEM_REF] + [VMEM_REF] * (1 + len(bands) + count))


def cheb_dot(turned, cheb_ref, array_ref):
    return SCALE * lax.dot_general(
        cheb_ref[...], array_ref[...], (((0 if turned else 1,), (0,)), ((), ())),
        precision=lax.Precision.HIGHEST, preferred_element_type=jnp.float32,
    )


def deriv_kernel(perts_ref, cheb_ref, states_ref, pert_ref, deriv_ref, drive_ref, chosen_ref):
    pert = perts_ref[0]
    deriv_ref[...] = cheb_dot(False, cheb_ref, states_ref)
    drive_ref[...] = pert_ref[pl.ds(pert, 1), :]
    rows = lax.broadcasted_iota(jnp.int32, chosen_ref.shape, 0)
    chosen_ref[...] = (rows == pert).astype(jnp.float32)


def derivatives(perts, cheb, states, pert_table):
    return call(
        deriv_kernel,
        [
            jax.ShapeDtypeStruct(states.shape, jnp.float32),
            jax.ShapeDtypeStruct((1, states.shape[1]), jnp.float32),
            jax.ShapeDtypeStruct(pert_table.shape, jnp.float32),
        ],
        [VMEM_REF] * 3,
        [],
        cost(1, *states.shape, states.shape[0]),
    )([perts, cheb, states, pert_table], [SMEM_REF] + [VMEM_REF] * 3)


def local_kernel(cheb_ref, resid_ref, decay_ref, out_ref):
    out_ref[...] = cheb_dot(True, cheb_ref, resid_ref) + decay_ref[...] * resid_ref[...]


def local_terms(cheb, resid, decay):
    return call(
        local_kernel,
        jax.ShapeDtypeStruct(resid.shape, jnp.float32),
        VMEM_REF,
        [],
        cost(1, *resid.shape, resid.shape[0]),
    )([cheb, resid, decay], [VMEM_REF] * 3)


def middle_kernel(base, many, offs_ref, x_ref, *refs):
    bands = refs[:many]
    acc_ref, deriv_ref, drive_ref, chosen_ref, states_ref, eps_ref, decay_ref = refs[many:-6]
    resid_ref, delta_ref, delta_t_ref, table_ref, sum_eps_ref, sum_decay_ref = refs[-6:]
    tile = 2 * bands[0].shape[0]
    here = columns_of(offs_ref, base, x_ref.shape[1])
    for at in range(many // 2):
        band = pl.ds(at * tile, tile)
        part = acc_ref[band, :] + product(bands[2 * at : 2 * at + 2], here, x_ref)
        states = states_ref[:, band]
        act = jnp.tanh(part.T + drive_ref[:, band])
        eps = eps_ref[:, band]
        resid = deriv_ref[:, band] - (eps * act - decay_ref[:, band] * states)
        delta = (-eps * (1.0 - act * act) * resid).astype(jnp.bfloat16)
        wide = delta.astype(jnp.float32)
        resid_ref[:, band] = resid
        delta_ref[:, band] = delta
        delta_t_ref[band, :] = wide.T.astype(jnp.bfloat16)
        table_ref[:, band] = chosen_ref[:, band] * jnp.sum(wide, axis=0, keepdims=True)
        sum_eps_ref[:, band] = -jnp.sum(act * resid, axis=0, keepdims=True)
        sum_decay_ref[:, band] = jnp.sum(states * resid, axis=0, keepdims=True)


def middle(offs, base, x, bands, acc, derivs, states, eps, decay):
    nodes, slab = x.shape
    rows = acc.shape[0]
    wide = functools.partial(jax.ShapeDtypeStruct, dtype=jnp.float32)
    return call(
        functools.partial(middle_kernel, base, len(bands)),
        [
            wide((nodes, rows)),
            jax.ShapeDtypeStruct((nodes, rows), jnp.bfloat16),
            jax.ShapeDtypeStruct((rows, nodes), jnp.bfloat16),
            wide(derivs[2].shape),
            wide((1, rows)),
            wide((1, rows)),
        ],
        [VMEM_REF] * 6,
        [],
        cost(2, nodes, slab, rows),
    )(
        [offs, x, *bands, acc, *derivs, states, eps, decay],
        [SMEM_REF] + [VMEM_REF] * (8 + len(bands)),
    )


def grad_w_part(base, offs_ref, delta_t_ref, xs, out_ref, held, sems):
    rows, slab = delta_t_ref.shape[0], xs[0].shape[1]
    slots, tile = held.shape[:2]
    step = min(256, slab)
    copies = []
    for at, x_ref in enumerate(xs):
        for start in range(0, rows, tile):
            slot, band = len(copies) % slots, pl.ds(start, tile)
            if len(copies) >= slots:
                copies[-slots].wait()
            for col in range(0, slab, step):
                held[slot, :, col : col + step] = jnp.dot(
                    delta_t_ref[band, :], x_ref[:, col : col + step],
                    preferred_element_type=jnp.float32,
                ).astype(held.dtype)
            there = columns_of(offs_ref, base + at, slab)
            copy = pltpu.make_async_copy(held.at[slot], out_ref.at[band, there], sems.at[slot])
            copy.start()
            copies.append(copy)
    return copies[-slots:]


def share_part(places, offs_ref, delta_ref, bands, outs):
    depth = 2 * bands[0].shape[0]
    for place, out_ref in zip(places, outs):
        slab = out_ref.shape[1]
        tile = max(slab // 2, 128)
        for col in range(0, slab, tile):
            there = pl.ds(pl.multiple_of(offs_ref[place] * slab + col, tile), tile)
            part = None
            for low in range(0, len(bands), 2):
                pair = jnp.concatenate([ref[:, there] for ref in bands[low : low + 2]], axis=0)
                more = jnp.dot(
                    delta_ref[:, low // 2 * depth : (low // 2 + 1) * depth], pair,
                    preferred_element_type=jnp.float32,
                )
                part = more if part is None else part + more
            out_ref[:, pl.ds(col, tile)] = part.astype(out_ref.dtype)


def sums_kernel(base, count, places, many, first, *refs):
    offs_ref, delta_ref, delta_t_ref = refs[:3]
    xs, bands = refs[3 : 3 + count], refs[3 + count : 3 + count + many]
    refs = refs[3 + count + many + (0 if first else 1) :]
    outs, copies = refs[: len(places)], []
    if count:
        out_ref, mark_ref, held, sems = refs[len(places) :]
        mark_ref[...] = jnp.zeros_like(mark_ref)
        copies = grad_w_part(base, offs_ref, delta_t_ref, xs, out_ref, held, sems)
    share_part(places, offs_ref, delta_ref, bands, outs)
    for copy in copies:
        copy.wait()


def sums(offs, base, xs, places, delta, delta_t, bands, slab, so_far, shape):
    nodes, rows = delta.shape
    count, own = len(xs), len(places) // 2
    tile = rows // 2
    first = so_far is None
    shapes = [jax.ShapeDtypeStruct((nodes, slab), jnp.bfloat16)] * own
    shapes += [jax.ShapeDtypeStruct((nodes, slab), jnp.float32)] * own
    specs, scratch, more = [VMEM_REF] * (2 * own), [], 0
    if count:
        shapes += [
            jax.ShapeDtypeStruct(shape, jnp.bfloat16),
            jax.ShapeDtypeStruct((8, 128), jnp.float32),
        ]
        specs += [ANY_REF, VMEM_REF]
        scratch = [pltpu.VMEM((4, tile, slab), jnp.bfloat16), pltpu.SemaphoreType.DMA((4,))]
        more = 4 * 2 * tile * slab
    operands = [offs, delta, delta_t, *xs, *bands] + ([] if first else [so_far])
    outs = call(
        functools.partial(sums_kernel, base, count, places, len(bands), first),
        shapes,
        specs,
        scratch,
        cost(count + 2 * own, nodes, slab, rows),
        {} if first else {len(operands) - 1: 2 * own},
        more,
    )(
        operands,
        [SMEM_REF] + [VMEM_REF] * (2 + count + len(bands)) + ([] if first else [ANY_REF]),
    )
    return outs[:own], outs[own : 2 * own], outs[2 * own :]


def ring_body(chips, states, weights, pert_table, eps_gain, decay, perts):
    _, nodes, slab = states.shape
    rows = weights.shape[0]
    order = chip_ring(chips)
    place = np.argsort(order)
    half, cut = chips // 2, nodes // 2

    near = [0]
    for step in range(1, half):
        near += [-step, step]
    near.append(half)
    listing = [(0, 0)]
    for step in range(half):
        now = [0] if step == 0 else [-step, step]
        then = [half] if step == half - 1 else [-step - 1, step + 1]
        listing += [(at, 1) for at in now] + [(at, 0) for at in then]
    listing.append((half, 1))
    sides = {key: at for at, key in enumerate(listing)}
    table = np.array(
        [
            [
                2 * order[(place[device // 2] + step) % chips] + (device % 2 ^ side)
                for step, side in listing
            ]
            for device in range(2 * chips)
        ],
        dtype=np.int32,
    )
    me = lax.axis_index("row")
    offs = lax.dynamic_slice(jnp.asarray(table), (me, 0), (1, 2 * chips)).reshape(-1)

    def ring(array, way):
        pairs = []
        for at, chip in enumerate(order):
            to = order[(at + way) % chips]
            pairs += [(2 * chip, 2 * to), (2 * chip + 1, 2 * to + 1)]
        return lax.ppermute(array, "row", pairs)

    def swap(array):
        return lax.ppermute(array, "row", [(i, i ^ 1) for i in range(2 * chips)])

    weights = pltpu.with_memory_space_constraint(weights, pltpu.HBM)
    cheb = cheb_matrix(nodes)
    flat = states.reshape(nodes, slab)
    xb = flat.astype(jnp.bfloat16)

    gate = lax.optimization_barrier

    x = {(0, 0): xb}
    behind, ahead, base = xb, xb, 0
    for step in range(1, half + 1):
        if step < half:
            behind, ahead = ring(behind, 1), ring(ahead, -1)
        else:
            behind, ahead = ring(behind[:cut], 1), ring(ahead[cut:], -1)
        for now in [0] if step == 1 else [1 - step, step - 1]:
            x[now, 1] = swap(x[now, 0])
        count = {1: 1, 2: 3}.get(step, 4)
        xs = [x[key] for key in listing[base : base + count]]
        if step == 1:
            acc, bands = first_products(offs, perts, 0, xs[0], weights)
        elif step == 2:
            acc, bands = second_products(offs, 0, [x[0, 0], *xs], weights, acc, bands)
        else:
            acc = add_products(offs, base, xs, acc, bands)
        base += count
        if step == half - 1:
            derivs = derivatives(perts, cheb, flat, pert_table)
            acc, *derivs = gate((acc, *derivs))
        behind, ahead, acc = gate((behind, ahead, acc))
        if step < half:
            x[-step, 0], x[step, 0] = behind, ahead
        else:
            x[half, 0] = jnp.concatenate([behind, ahead], axis=0)
    x[half, 1] = swap(x[half, 0])
    xs = [x[key] for key in listing[base : base + 3]]
    acc = add_products(offs, base, xs, acc, bands)
    base += 3

    decay = decay.reshape(1, rows)
    resid, delta, delta_t, grad_table, grad_eps, grad_decay = middle(
        offs, base, x[half, 1], bands, acc, derivs, flat, eps_gain.reshape(1, rows), decay
    )

    grad_w, base = None, 0

    def work(offs, count, steps, grad_w, base):
        places = [sides[step, side] for side in (1, 0) for step in steps]
        xs = [x[key] for key in listing[base : base + count]]
        others, owns, rest = sums(
            offs, base, xs, places, delta, delta_t, bands, slab, grad_w, weights.shape
        )
        grad_w, mark = rest if count else (grad_w, None)
        return others, owns, grad_w, base + count, mark

    def joined(others, owns):
        return [own + swap(other).astype(jnp.float32) for other, own in zip(others, owns)]

    counts = [2, 5, 5]
    counts.append(len(listing) - sum(counts))
    others, owns, _, _, _ = work(offs, 0, [half], None, 0)
    (far,) = joined(others, owns)
    others, owns, _, _, _ = work(offs, 0, [half - 1, 1 - half], None, 0)
    far, offs, *owns = gate((far.astype(jnp.bfloat16), offs, *owns))
    own_ahead, own_behind = joined(others, owns)
    ahead, behind = ring(far[:cut], 1), ring(far[cut:], -1)
    for step in range(half - 1, -1, -1):
        steps = [] if step == 0 else [0] if step == 1 else [step - 1, 1 - step]
        others, owns, grad_w, base, mark = work(offs, counts.pop(0), steps, grad_w, base)
        if step == 0:
            break
        ahead, behind, *owns = gate((ahead, behind, *owns))
        ahead, behind = ahead.astype(jnp.float32), behind.astype(jnp.float32)
        if step == half - 1:
            ahead = jnp.concatenate([own_ahead[:cut] + ahead, own_ahead[cut:]], axis=0)
            behind = jnp.concatenate([own_behind[:cut], own_behind[cut:] + behind], axis=0)
        else:
            ahead, behind = own_ahead + ahead, own_behind + behind
        ahead, behind = ahead.astype(jnp.bfloat16), behind.astype(jnp.bfloat16)
        if step > 1:
            own_ahead, own_behind = joined(others, owns)
        else:
            (near_share,) = joined(others, owns)
        ahead, behind, offs = gate((ahead, behind, offs))
        ahead, behind = ring(ahead, 1), ring(behind, -1)

    local = local_terms(cheb, resid, decay)
    ahead, behind, local = gate((ahead, behind, local))
    grad_x = local + near_share + ahead.astype(jnp.float32) + behind.astype(jnp.float32)
    grad_x = grad_x.reshape(states.shape)
    return (grad_w, grad_x, grad_table, grad_eps.reshape(rows), grad_decay.reshape(rows))


def plain_body(states, weights, pert_table, eps_gain, decay, perts):
    traj, nodes, slab = states.shape
    total = traj * nodes
    cheb = cheb_matrix(nodes)
    xb = states.astype(jnp.bfloat16).reshape(total, slab)
    full = lax.all_gather(xb, "row", axis=1, tiled=True)
    pre = lax.dot_general(
        full, weights, (((1,), (1,)), ((), ())), preferred_element_type=jnp.float32
    )
    onehot = (perts[:, None] == jnp.arange(pert_table.shape[0], dtype=jnp.int32)[None, :]).astype(
        jnp.float32
    )
    drive = jnp.dot(onehot, pert_table, precision=lax.Precision.HIGHEST)
    act = jnp.tanh(pre.reshape(traj, nodes, slab) + drive[:, None, :])
    deriv = SCALE * jnp.einsum("kl,clg->ckg", cheb, states, precision=lax.Precision.HIGHEST)
    resid = deriv - (eps_gain * act - decay * states)
    delta = (-eps_gain * (1.0 - act * act) * resid).astype(jnp.bfloat16)
    dflat = delta.reshape(total, slab)
    grad_w = lax.dot_general(
        dflat, full, (((0,), (0,)), ((), ())), preferred_element_type=jnp.float32
    ).astype(jnp.bfloat16)
    back = jnp.dot(dflat, weights, preferred_element_type=jnp.float32)
    back = lax.psum_scatter(back, "row", scatter_dimension=1, tiled=True)
    grad_x = (
        SCALE * jnp.einsum("lk,clg->ckg", cheb, resid, precision=lax.Precision.HIGHEST)
        + decay * resid
        + back.reshape(traj, nodes, slab)
    )
    node_sums = jnp.sum(delta.astype(jnp.float32), axis=1)
    grad_table = jnp.dot(onehot.T, node_sums, precision=lax.Precision.HIGHEST)
    grad_eps = -jnp.sum(act * resid, axis=(0, 1))
    grad_decay = jnp.sum(states * resid, axis=(0, 1))
    return (grad_w, grad_x, grad_table, grad_eps, grad_decay)


def solution(mesh):
    chips = mesh.shape["row"] // 2
    in_specs = (
        P("rep", None, "row"),
        P(("rep", "row"), None),
        P("rep", "row"),
        P(("rep", "row")),
        P(("rep", "row")),
        P("rep"),
    )
    out_specs = (
        P(("rep", "row"), None),
        P("rep", None, "row"),
        P("rep", "row"),
        P(("rep", "row")),
        P(("rep", "row")),
    )

    def run(states, *others):
        if states.shape[0] == 1 and chips <= LONGEST_RING:
            return ring_body(chips, states, *others)
        return plain_body(states, *others)

    return jax.shard_map(run, mesh=mesh, in_specs=in_specs, out_specs=out_specs, check_vma=False)
```

```python
import functools

import jax
import jax.numpy as jnp
import numpy as np
from jax import lax
from jax.experimental import pallas as pl
from jax.experimental.pallas import tpu as pltpu
from jax.sharding import PartitionSpec as P

SCALE = 2.0 / 1024.0
VMEM_LIMIT = 8 * 2**20
BANDS = 8
LOADS = (4, 2, 2)
LONGEST_RING = 16


def cheb_matrix(count):
    index = np.arange(count)
    points = np.cos(np.pi * index / (count - 1))
    signs = np.where(index % 2 == 0, 1.0, -1.0)
    weight_c = signs * np.where((index == 0) | (index == count - 1), 2.0, 1.0)
    same = index[:, None] == index[None, :]
    spread = np.where(same, 1.0, points[:, None] - points[None, :])
    off = np.where(same, 0.0, weight_c[:, None] / weight_c[None, :] / spread)
    return jnp.asarray((off - np.diag(np.sum(off, axis=1))).astype(np.float32))


def chip_ring(chips):
    rows = 4
    cols = chips // rows
    cells = [(0, col) for col in range(cols)]
    for row in range(1, rows):
        span = range(1, cols)
        cells += [(row, col) for col in (reversed(span) if row % 2 else span)]
    cells += [(row, 0) for row in range(rows - 1, 0, -1)]
    return [row * cols + col for row, col in cells]


VMEM_REF = pl.BlockSpec(memory_space=pltpu.VMEM)
SMEM_REF = pl.BlockSpec(memory_space=pltpu.SMEM)
ANY_REF = pl.BlockSpec(memory_space=pl.ANY)
HBM_REF = pl.BlockSpec(memory_space=pltpu.HBM)


def cost(products, nodes, slab, rows):
    return pl.CostEstimate(
        flops=2 * products * nodes * slab * rows // 16,
        bytes_accessed=2 * products * slab * rows // 16,
        transcendentals=0,
    )


def call(kernel, out_shape, out_specs, scratch, costs, aliases=None):
    def run(operands, in_specs):
        return pl.pallas_call(
            kernel,
            out_shape=out_shape,
            in_specs=in_specs,
            out_specs=out_specs,
            scratch_shapes=scratch,
            input_output_aliases=aliases or {},
            compiler_params=pltpu.CompilerParams(vmem_limit_bytes=VMEM_LIMIT),
            cost_estimate=costs,
        )(*operands)

    return run


def columns_of(offs_ref, at, slab):
    return pl.ds(pl.multiple_of(offs_ref[at] * slab, slab), slab)


def load_bands(w_ref, bands, sems, first):
    copies = []
    for at, band_ref in enumerate(bands):
        tile = band_ref.shape[0]
        rows = pl.ds((first + at) * tile, tile)
        copies.append(pltpu.make_async_copy(w_ref.at[rows, :], band_ref, sems.at[at]))
        copies[-1].start()
    return copies


def product(bands, here, x_ref):
    rows = [band_ref[:, here] for band_ref in bands]
    return lax.dot_general(
        rows[0] if len(rows) == 1 else jnp.concatenate(rows, axis=0),
        x_ref[...], (((1,), (1,)), ((), ())), preferred_element_type=jnp.float32,
    )


def pre_kernel(base, done, count, many, late, first, *refs):
    offs_ref, refs = refs[0], refs[1:]
    if first:
        refs = refs[1:]
    if late:
        w_ref, refs = refs[0], refs[1:]
    if many:
        acc_ref, refs = refs[0], refs[1:]
    bands, refs = refs[:many], refs[many:]
    xs, refs = refs[: count + (done if late else 0)], refs[count + (done if late else 0) :]
    out_ref, others, sems = refs[0], refs[1 : 1 + late], refs[-1]
    slab = xs[0].shape[1]
    tile = out_ref.shape[0] // BANDS
    copies = load_bands(w_ref, others, sems, many) if late else []
    places = [columns_of(offs_ref, base + at, slab) for at in range(done + count)]
    for low in range(0, many, 2):
        pair = bands[low : low + 2]
        rows = pl.ds(low * tile, len(pair) * tile)
        total = acc_ref[rows, :]
        for at, x_ref in enumerate(xs[-count:]):
            total += product(pair, places[done + at], x_ref)
        out_ref[rows, :] = total
    for copy in copies:
        copy.wait()
    for low in range(0, late, 2):
        pair = others[low : low + 2]
        rows = pl.ds((many + low) * tile, len(pair) * tile)
        total = product(pair, places[0], xs[0])
        for at in range(1, len(xs)):
            total += product(pair, places[at], xs[at])
        out_ref[rows, :] = total


def add_products(offs, perts, weights, acc, bands, before, xs, late):
    (nodes, slab), (rows, genes) = xs[0].shape, weights.shape
    first, many, done, count = acc is None, len(bands), len(before), len(xs)
    operands, specs = [offs], [SMEM_REF]
    if first:
        operands, specs = operands + [perts], specs + [SMEM_REF]
    if late:
        operands, specs = operands + [weights], specs + [HBM_REF]
    if many:
        operands, specs = operands + [acc], specs + [VMEM_REF]
    operands += [*bands, *(before if late else []), *xs]
    specs += [VMEM_REF] * (len(operands) - len(specs))
    acc, *others = call(
        functools.partial(pre_kernel, 0, done, count, many, late, first),
        [jax.ShapeDtypeStruct((rows, nodes), jnp.float32)]
        + [pltpu.VMEM((rows // BANDS, genes), weights.dtype)] * late,
        [VMEM_REF] * (1 + late),
        [pltpu.SemaphoreType.DMA((max(late, 1),))],
        cost(count, nodes, slab, rows),
    )(operands, specs)
    return acc, [*bands, *others]


def cheb_dot(turned, cheb_ref, array_ref):
    return SCALE * lax.dot_general(
        cheb_ref[...], array_ref[...], (((0 if turned else 1,), (0,)), ((), ())),
        precision=lax.Precision.HIGHEST, preferred_element_type=jnp.float32,
    )


def deriv_kernel(perts_ref, cheb_ref, states_ref, pert_ref, deriv_ref, drive_ref, chosen_ref):
    pert = perts_ref[0]
    deriv_ref[...] = cheb_dot(False, cheb_ref, states_ref)
    drive_ref[...] = pert_ref[pl.ds(pert, 1), :]
    rows = lax.broadcasted_iota(jnp.int32, chosen_ref.shape, 0)
    chosen_ref[...] = (rows == pert).astype(jnp.float32)


def derivatives(perts, cheb, states, pert_table):
    return call(
        deriv_kernel,
        [
            jax.ShapeDtypeStruct(states.shape, jnp.float32),
            jax.ShapeDtypeStruct((1, states.shape[1]), jnp.float32),
            jax.ShapeDtypeStruct(pert_table.shape, jnp.float32),
        ],
        [VMEM_REF] * 3,
        [],
        cost(1, *states.shape, states.shape[0]),
    )([perts, cheb, states, pert_table], [SMEM_REF] + [VMEM_REF] * 3)


def local_kernel(cheb_ref, resid_ref, decay_ref, out_ref):
    out_ref[...] = cheb_dot(True, cheb_ref, resid_ref) + decay_ref[...] * resid_ref[...]


def local_terms(cheb, resid, decay):
    return call(
        local_kernel,
        jax.ShapeDtypeStruct(resid.shape, jnp.float32),
        VMEM_REF,
        [],
        cost(1, *resid.shape, resid.shape[0]),
    )([cheb, resid, decay], [VMEM_REF] * 3)


def middle_kernel(base, many, offs_ref, x_ref, *refs):
    bands = refs[:many]
    acc_ref, deriv_ref, drive_ref, chosen_ref, states_ref, eps_ref, decay_ref = refs[many:-6]
    resid_ref, delta_ref, delta_t_ref, table_ref, sum_eps_ref, sum_decay_ref = refs[-6:]
    tile = 2 * bands[0].shape[0]
    here = columns_of(offs_ref, base, x_ref.shape[1])
    for at in range(many // 2):
        band = pl.ds(at * tile, tile)
        part = acc_ref[band, :] + product(bands[2 * at : 2 * at + 2], here, x_ref)
        states = states_ref[:, band]
        act = jnp.tanh(part.T + drive_ref[:, band])
        eps = eps_ref[:, band]
        resid = deriv_ref[:, band] - (eps * act - decay_ref[:, band] * states)
        delta = (-eps * (1.0 - act * act) * resid).astype(jnp.bfloat16)
        wide = delta.astype(jnp.float32)
        resid_ref[:, band] = resid
        delta_ref[:, band] = delta
        delta_t_ref[band, :] = wide.T.astype(jnp.bfloat16)
        table_ref[:, band] = chosen_ref[:, band] * jnp.sum(wide, axis=0, keepdims=True)
        sum_eps_ref[:, band] = -jnp.sum(act * resid, axis=0, keepdims=True)
        sum_decay_ref[:, band] = jnp.sum(states * resid, axis=0, keepdims=True)


def middle(offs, base, x, bands, acc, derivs, states, eps, decay):
    nodes, slab = x.shape
    rows = acc.shape[0]
    wide = functools.partial(jax.ShapeDtypeStruct, dtype=jnp.float32)
    return call(
        functools.partial(middle_kernel, base, len(bands)),
        [
            wide((nodes, rows)),
            jax.ShapeDtypeStruct((nodes, rows), jnp.bfloat16),
            jax.ShapeDtypeStruct((rows, nodes), jnp.bfloat16),
            wide(derivs[2].shape),
            wide((1, rows)),
            wide((1, rows)),
        ],
        [VMEM_REF] * 6,
        [],
        cost(2, nodes, slab, rows),
    )(
        [offs, x, *bands, acc, *derivs, states, eps, decay],
        [SMEM_REF] + [VMEM_REF] * (8 + len(bands)),
    )


def grad_w_part(base, offs_ref, delta_t_ref, xs, out_ref, held, sems):
    rows, slab = delta_t_ref.shape[0], xs[0].shape[1]
    slots, tile = held.shape[:2]
    step = min(256, slab)
    copies = []
    for at, x_ref in enumerate(xs):
        for start in range(0, rows, tile):
            slot, band = len(copies) % slots, pl.ds(start, tile)
            if len(copies) >= slots:
                copies[-slots].wait()
            for col in range(0, slab, step):
                held[slot, :, col : col + step] = jnp.dot(
                    delta_t_ref[band, :], x_ref[:, col : col + step],
                    preferred_element_type=jnp.float32,
                ).astype(held.dtype)
            there = columns_of(offs_ref, base + at, slab)
            copy = pltpu.make_async_copy(held.at[slot], out_ref.at[band, there], sems.at[slot])
            copy.start()
            copies.append(copy)
    return copies[-slots:]


def share_part(places, offs_ref, delta_ref, bands, outs):
    depth = 2 * bands[0].shape[0]
    for place, out_ref in zip(places, outs):
        slab = out_ref.shape[1]
        tile = max(slab // 2, 128)
        for col in range(0, slab, tile):
            there = pl.ds(pl.multiple_of(offs_ref[place] * slab + col, tile), tile)
            part = None
            for low in range(0, len(bands), 2):
                pair = jnp.concatenate([ref[:, there] for ref in bands[low : low + 2]], axis=0)
                more = jnp.dot(
                    delta_ref[:, low // 2 * depth : (low // 2 + 1) * depth], pair,
                    preferred_element_type=jnp.float32,
                )
                part = more if part is None else part + more
            out_ref[:, pl.ds(col, tile)] = part.astype(out_ref.dtype)


def sums_kernel(base, count, places, many, first, *refs):
    offs_ref, delta_ref, delta_t_ref = refs[:3]
    xs, bands = refs[3 : 3 + count], refs[3 + count : 3 + count + many]
    refs = refs[3 + count + many + (0 if first else 1) :]
    outs, copies = refs[: len(places)], []
    if count:
        out_ref, mark_ref, held, sems = refs[len(places) :]
        mark_ref[...] = jnp.zeros_like(mark_ref)
        copies = grad_w_part(base, offs_ref, delta_t_ref, xs, out_ref, held, sems)
    share_part(places, offs_ref, delta_ref, bands, outs)
    for copy in copies:
        copy.wait()


def sums(offs, base, xs, places, delta, delta_t, bands, slab, so_far, shape):
    nodes, rows = delta.shape
    count, own = len(xs), len(places) // 2
    tile = rows // 2
    first = so_far is None
    shapes = [jax.ShapeDtypeStruct((nodes, slab), jnp.bfloat16)] * own
    shapes += [jax.ShapeDtypeStruct((nodes, slab), jnp.float32)] * own
    specs, scratch = [VMEM_REF] * (2 * own), []
    if count:
        shapes += [
            jax.ShapeDtypeStruct(shape, jnp.bfloat16),
            jax.ShapeDtypeStruct((8, 128), jnp.float32),
        ]
        specs += [ANY_REF, VMEM_REF]
        scratch = [pltpu.VMEM((4, tile, slab), jnp.bfloat16), pltpu.SemaphoreType.DMA((4,))]
    operands = [offs, delta, delta_t, *xs, *bands] + ([] if first else [so_far])
    outs = call(
        functools.partial(sums_kernel, base, count, places, len(bands), first),
        shapes,
        specs,
        scratch,
        cost(count + 2 * own, nodes, slab, rows),
        {} if first else {len(operands) - 1: 2 * own},
    )(
        operands,
        [SMEM_REF] + [VMEM_REF] * (2 + count + len(bands)) + ([] if first else [ANY_REF]),
    )
    return outs[:own], outs[own : 2 * own], outs[2 * own :]


def ring_body(chips, states, weights, pert_table, eps_gain, decay, perts):
    _, nodes, slab = states.shape
    rows = weights.shape[0]
    order = chip_ring(chips)
    place = np.argsort(order)
    half, cut = chips // 2, nodes // 2

    near = [0]
    for step in range(1, half):
        near += [-step, step]
    near.append(half)
    listing = [(0, 0)]
    for step in range(half):
        now = [0] if step == 0 else [-step, step]
        then = [half] if step == half - 1 else [-step - 1, step + 1]
        listing += [(at, 1) for at in now] + [(at, 0) for at in then]
    listing.append((half, 1))
    sides = {key: at for at, key in enumerate(listing)}
    table = np.array(
        [
            [
                2 * order[(place[device // 2] + step) % chips] + (device % 2 ^ side)
                for step, side in listing
            ]
            for device in range(2 * chips)
        ],
        dtype=np.int32,
    )
    me = lax.axis_index("row")
    offs = lax.dynamic_slice(jnp.asarray(table), (me, 0), (1, 2 * chips)).reshape(-1)

    def ring(array, way):
        pairs = []
        for at, chip in enumerate(order):
            to = order[(at + way) % chips]
            pairs += [(2 * chip, 2 * to), (2 * chip + 1, 2 * to + 1)]
        return lax.ppermute(array, "row", pairs)

    def swap(array):
        return lax.ppermute(array, "row", [(i, i ^ 1) for i in range(2 * chips)])

    weights = pltpu.with_memory_space_constraint(weights, pltpu.HBM)
    cheb = cheb_matrix(nodes)
    flat = states.reshape(nodes, slab)
    xb = flat.astype(jnp.bfloat16)

    gate = lax.optimization_barrier

    x = {(0, 0): xb}
    behind, ahead, base = xb, xb, 0
    acc, bands, loads = None, [], list(LOADS)
    for step in range(1, half + 1):
        if step < half:
            behind, ahead = ring(behind, 1), ring(ahead, -1)
        else:
            behind, ahead = ring(behind[:cut], 1), ring(ahead[cut:], -1)
        for now in [0] if step == 1 else [1 - step, step - 1]:
            x[now, 1] = swap(x[now, 0])
        count = {1: 1, 2: 3}.get(step, 4)
        late = loads.pop(0) if loads else 0
        xs = [x[key] for key in listing[: base + count]]
        acc, bands = add_products(
            offs, perts, weights, acc, bands, xs[:base], xs[base:], late
        )
        base += count
        if step == half - 1:
            derivs = derivatives(perts, cheb, flat, pert_table)
            acc, *derivs = gate((acc, *derivs))
        behind, ahead, acc = gate((behind, ahead, acc))
        if step < half:
            x[-step, 0], x[step, 0] = behind, ahead
        else:
            x[half, 0] = jnp.concatenate([behind, ahead], axis=0)
    x[half, 1] = swap(x[half, 0])
    xs = [x[key] for key in listing[: base + 3]]
    acc, _ = add_products(offs, perts, weights, acc, bands, xs[:base], xs[base:], 0)
    base += 3

    decay = decay.reshape(1, rows)
    resid, delta, delta_t, grad_table, grad_eps, grad_decay = middle(
        offs, base, x[half, 1], bands, acc, derivs, flat, eps_gain.reshape(1, rows), decay
    )

    grad_w, base = None, 0

    def work(offs, count, steps, grad_w, base):
        places = [sides[step, side] for side in (1, 0) for step in steps]
        xs = [x[key] for key in listing[base : base + count]]
        others, owns, rest = sums(
            offs, base, xs, places, delta, delta_t, bands, slab, grad_w, weights.shape
        )
        grad_w, mark = rest if count else (grad_w, None)
        return others, owns, grad_w, base + count, mark

    def joined(others, owns):
        return [own + swap(other).astype(jnp.float32) for other, own in zip(others, owns)]

    counts = [2, 5, 5]
    counts.append(len(listing) - sum(counts))
    others, owns, _, _, _ = work(offs, 0, [half], None, 0)
    (far,) = joined(others, owns)
    others, owns, _, _, _ = work(offs, 0, [half - 1, 1 - half], None, 0)
    far, offs, *owns = gate((far.astype(jnp.bfloat16), offs, *owns))
    own_ahead, own_behind = joined(others, owns)
    ahead, behind = ring(far[:cut], 1), ring(far[cut:], -1)
    for step in range(half - 1, -1, -1):
        steps = [] if step == 0 else [0] if step == 1 else [step - 1, 1 - step]
        others, owns, grad_w, base, mark = work(offs, counts.pop(0), steps, grad_w, base)
        if step == 0:
            break
        ahead, behind, *owns = gate((ahead, behind, *owns))
        ahead, behind = ahead.astype(jnp.float32), behind.astype(jnp.float32)
        if step == half - 1:
            ahead = jnp.concatenate([own_ahead[:cut] + ahead, own_ahead[cut:]], axis=0)
            behind = jnp.concatenate([own_behind[:cut], own_behind[cut:] + behind], axis=0)
        else:
            ahead, behind = own_ahead + ahead, own_behind + behind
        ahead, behind = ahead.astype(jnp.bfloat16), behind.astype(jnp.bfloat16)
        if step > 1:
            own_ahead, own_behind = joined(others, owns)
        else:
            (near_share,) = joined(others, owns)
        ahead, behind, offs = gate((ahead, behind, offs))
        ahead, behind = ring(ahead, 1), ring(behind, -1)

    local = local_terms(cheb, resid, decay)
    ahead, behind, local = gate((ahead, behind, local))
    grad_x = local + near_share + ahead.astype(jnp.float32) + behind.astype(jnp.float32)
    grad_x = grad_x.reshape(states.shape)
    return (grad_w, grad_x, grad_table, grad_eps.reshape(rows), grad_decay.reshape(rows))


def plain_body(states, weights, pert_table, eps_gain, decay, perts):
    traj, nodes, slab = states.shape
    total = traj * nodes
    cheb = cheb_matrix(nodes)
    xb = states.astype(jnp.bfloat16).reshape(total, slab)
    full = lax.all_gather(xb, "row", axis=1, tiled=True)
    pre = lax.dot_general(
        full, weights, (((1,), (1,)), ((), ())), preferred_element_type=jnp.float32
    )
    onehot = (perts[:, None] == jnp.arange(pert_table.shape[0], dtype=jnp.int32)[None, :]).astype(
        jnp.float32
    )
    drive = jnp.dot(onehot, pert_table, precision=lax.Precision.HIGHEST)
    act = jnp.tanh(pre.reshape(traj, nodes, slab) + drive[:, None, :])
    deriv = SCALE * jnp.einsum("kl,clg->ckg", cheb, states, precision=lax.Precision.HIGHEST)
    resid = deriv - (eps_gain * act - decay * states)
    delta = (-eps_gain * (1.0 - act * act) * resid).astype(jnp.bfloat16)
    dflat = delta.reshape(total, slab)
    grad_w = lax.dot_general(
        dflat, full, (((0,), (0,)), ((), ())), preferred_element_type=jnp.float32
    ).astype(jnp.bfloat16)
    back = jnp.dot(dflat, weights, preferred_element_type=jnp.float32)
    back = lax.psum_scatter(back, "row", scatter_dimension=1, tiled=True)
    grad_x = (
        SCALE * jnp.einsum("lk,clg->ckg", cheb, resid, precision=lax.Precision.HIGHEST)
        + decay * resid
        + back.reshape(traj, nodes, slab)
    )
    node_sums = jnp.sum(delta.astype(jnp.float32), axis=1)
    grad_table = jnp.dot(onehot.T, node_sums, precision=lax.Precision.HIGHEST)
    grad_eps = -jnp.sum(act * resid, axis=(0, 1))
    grad_decay = jnp.sum(states * resid, axis=(0, 1))
    return (grad_w, grad_x, grad_table, grad_eps, grad_decay)


def solution(mesh):
    chips = mesh.shape["row"] // 2
    in_specs = (
        P("rep", None, "row"),
        P(("rep", "row"), None),
        P("rep", "row"),
        P(("rep", "row")),
        P(("rep", "row")),
        P("rep"),
    )
    out_specs = (
        P(("rep", "row"), None),
        P("rep", None, "row"),
        P("rep", "row"),
        P(("rep", "row")),
        P(("rep", "row")),
    )

    def run(states, *others):
        if states.shape[0] == 1 and chips <= LONGEST_RING:
            return ring_body(chips, states, *others)
        return plain_body(states, *others)

    return jax.shard_map(run, mesh=mesh, in_specs=in_specs, out_specs=out_specs, check_vma=False)
```

```python
import functools

import jax
import jax.numpy as jnp
import numpy as np
from jax import lax
from jax.experimental import pallas as pl
from jax.experimental.pallas import tpu as pltpu
from jax.sharding import PartitionSpec as P

SCALE = 2.0 / 1024.0
VMEM_LIMIT = 8 * 2**20
BANDS = 16
GROUP = 4
LOADS = (10, 6)
LONGEST_RING = 16


def cheb_matrix(count):
    index = np.arange(count)
    points = np.cos(np.pi * index / (count - 1))
    signs = np.where(index % 2 == 0, 1.0, -1.0)
    weight_c = signs * np.where((index == 0) | (index == count - 1), 2.0, 1.0)
    same = index[:, None] == index[None, :]
    spread = np.where(same, 1.0, points[:, None] - points[None, :])
    off = np.where(same, 0.0, weight_c[:, None] / weight_c[None, :] / spread)
    return jnp.asarray((off - np.diag(np.sum(off, axis=1))).astype(np.float32))


def chip_ring(chips):
    rows = 4
    cols = chips // rows
    cells = [(0, col) for col in range(cols)]
    for row in range(1, rows):
        span = range(1, cols)
        cells += [(row, col) for col in (reversed(span) if row % 2 else span)]
    cells += [(row, 0) for row in range(rows - 1, 0, -1)]
    return [row * cols + col for row, col in cells]


VMEM_REF = pl.BlockSpec(memory_space=pltpu.VMEM)
SMEM_REF = pl.BlockSpec(memory_space=pltpu.SMEM)
ANY_REF = pl.BlockSpec(memory_space=pl.ANY)
HBM_REF = pl.BlockSpec(memory_space=pltpu.HBM)


def cost(products, nodes, slab, rows):
    return pl.CostEstimate(
        flops=2 * products * nodes * slab * rows // 16,
        bytes_accessed=2 * products * slab * rows // 16,
        transcendentals=0,
    )


def call(kernel, out_shape, out_specs, scratch, costs, aliases=None):
    def run(operands, in_specs):
        return pl.pallas_call(
            kernel,
            out_shape=out_shape,
            in_specs=in_specs,
            out_specs=out_specs,
            scratch_shapes=scratch,
            input_output_aliases=aliases or {},
            compiler_params=pltpu.CompilerParams(vmem_limit_bytes=VMEM_LIMIT),
            cost_estimate=costs,
        )(*operands)

    return run


def columns_of(offs_ref, at, slab):
    return pl.ds(pl.multiple_of(offs_ref[at] * slab, slab), slab)


def load_bands(w_ref, bands, sems, first):
    copies = []
    for at, band_ref in enumerate(bands):
        tile = band_ref.shape[0]
        rows = pl.ds((first + at) * tile, tile)
        copies.append(pltpu.make_async_copy(w_ref.at[rows, :], band_ref, sems.at[at]))
        copies[-1].start()
    return copies


def product(bands, here, x_ref):
    rows = [band_ref[:, here] for band_ref in bands]
    return lax.dot_general(
        x_ref[...], rows[0] if len(rows) == 1 else jnp.concatenate(rows, axis=0),
        (((1,), (1,)), ((), ())), preferred_element_type=jnp.float32,
    )


def pre_kernel(base, done, count, many, late, first, *refs):
    offs_ref, refs = refs[0], refs[1:]
    if first:
        refs = refs[1:]
    if late:
        w_ref, refs = refs[0], refs[1:]
    if many:
        acc_ref, refs = refs[0], refs[1:]
    bands, refs = refs[:many], refs[many:]
    xs, refs = refs[: count + (done if late else 0)], refs[count + (done if late else 0) :]
    out_ref, others, sems = refs[0], refs[1 : 1 + late], refs[-1]
    slab = xs[0].shape[1]
    tile = out_ref.shape[1] // BANDS
    copies = load_bands(w_ref, others, sems, many) if late else []
    places = [columns_of(offs_ref, base + at, slab) for at in range(done + count)]
    for low in range(0, many, GROUP):
        group = bands[low : low + GROUP]
        rows = pl.ds(low * tile, len(group) * tile)
        total = acc_ref[:, rows]
        for at, x_ref in enumerate(xs[-count:]):
            total += product(group, places[done + at], x_ref)
        out_ref[:, rows] = total
    for low in range(0, late, GROUP):
        for copy in copies[low : low + GROUP]:
            copy.wait()
        group = others[low : low + GROUP]
        rows = pl.ds((many + low) * tile, len(group) * tile)
        total = product(group, places[0], xs[0])
        for at in range(1, len(xs)):
            total += product(group, places[at], xs[at])
        out_ref[:, rows] = total


def add_products(offs, perts, weights, acc, bands, before, xs, late):
    (nodes, slab), (rows, genes) = xs[0].shape, weights.shape
    first, many, done, count = acc is None, len(bands), len(before), len(xs)
    operands, specs = [offs], [SMEM_REF]
    if first:
        operands, specs = operands + [perts], specs + [SMEM_REF]
    if late:
        operands, specs = operands + [weights], specs + [HBM_REF]
    if many:
        operands, specs = operands + [acc], specs + [VMEM_REF]
    operands += [*bands, *(before if late else []), *xs]
    specs += [VMEM_REF] * (len(operands) - len(specs))
    acc, *others = call(
        functools.partial(pre_kernel, 0, done, count, many, late, first),
        [jax.ShapeDtypeStruct((nodes, rows), jnp.float32)]
        + [pltpu.VMEM((rows // BANDS, genes), weights.dtype)] * late,
        [VMEM_REF] * (1 + late),
        [pltpu.SemaphoreType.DMA((max(late, 1),))],
        cost(count, nodes, slab, rows),
    )(operands, specs)
    return acc, [*bands, *others]


def cheb_dot(turned, cheb_ref, array_ref):
    return SCALE * lax.dot_general(
        cheb_ref[...], array_ref[...], (((0 if turned else 1,), (0,)), ((), ())),
        precision=lax.Precision.HIGHEST, preferred_element_type=jnp.float32,
    )


def deriv_kernel(perts_ref, cheb_ref, states_ref, pert_ref, deriv_ref, drive_ref, chosen_ref):
    pert = perts_ref[0]
    deriv_ref[...] = cheb_dot(False, cheb_ref, states_ref)
    drive_ref[...] = pert_ref[pl.ds(pert, 1), :]
    rows = lax.broadcasted_iota(jnp.int32, chosen_ref.shape, 0)
    chosen_ref[...] = (rows == pert).astype(jnp.float32)


def derivatives(perts, cheb, states, pert_table):
    return call(
        deriv_kernel,
        [
            jax.ShapeDtypeStruct(states.shape, jnp.float32),
            jax.ShapeDtypeStruct((1, states.shape[1]), jnp.float32),
            jax.ShapeDtypeStruct(pert_table.shape, jnp.float32),
        ],
        [VMEM_REF] * 3,
        [],
        cost(1, *states.shape, states.shape[0]),
    )([perts, cheb, states, pert_table], [SMEM_REF] + [VMEM_REF] * 3)


def local_kernel(cheb_ref, resid_ref, decay_ref, out_ref):
    out_ref[...] = cheb_dot(True, cheb_ref, resid_ref) + decay_ref[...] * resid_ref[...]


def local_terms(cheb, resid, decay):
    return call(
        local_kernel,
        jax.ShapeDtypeStruct(resid.shape, jnp.float32),
        VMEM_REF,
        [],
        cost(1, *resid.shape, resid.shape[0]),
    )([cheb, resid, decay], [VMEM_REF] * 3)


def middle_kernel(base, many, offs_ref, x_ref, *refs):
    bands = refs[:many]
    acc_ref, deriv_ref, drive_ref, chosen_ref, states_ref, eps_ref, decay_ref = refs[many:-6]
    resid_ref, delta_ref, delta_t_ref, table_ref, sum_eps_ref, sum_decay_ref = refs[-6:]
    tile = GROUP * bands[0].shape[0]
    here = columns_of(offs_ref, base, x_ref.shape[1])
    for at in range(many // GROUP):
        band = pl.ds(at * tile, tile)
        part = acc_ref[:, band] + product(bands[at * GROUP : (at + 1) * GROUP], here, x_ref)
        states = states_ref[:, band]
        act = jnp.tanh(part + drive_ref[:, band])
        eps = eps_ref[:, band]
        resid = deriv_ref[:, band] - (eps * act - decay_ref[:, band] * states)
        delta = (-eps * (1.0 - act * act) * resid).astype(jnp.bfloat16)
        wide = delta.astype(jnp.float32)
        resid_ref[:, band] = resid
        delta_ref[:, band] = delta
        delta_t_ref[band, :] = wide.T.astype(jnp.bfloat16)
        table_ref[:, band] = chosen_ref[:, band] * jnp.sum(wide, axis=0, keepdims=True)
        sum_eps_ref[:, band] = -jnp.sum(act * resid, axis=0, keepdims=True)
        sum_decay_ref[:, band] = jnp.sum(states * resid, axis=0, keepdims=True)


def middle(offs, base, x, bands, acc, derivs, states, eps, decay):
    nodes, slab = x.shape
    rows = acc.shape[1]
    wide = functools.partial(jax.ShapeDtypeStruct, dtype=jnp.float32)
    return call(
        functools.partial(middle_kernel, base, len(bands)),
        [
            wide((nodes, rows)),
            jax.ShapeDtypeStruct((nodes, rows), jnp.bfloat16),
            jax.ShapeDtypeStruct((rows, nodes), jnp.bfloat16),
            wide(derivs[2].shape),
            wide((1, rows)),
            wide((1, rows)),
        ],
        [VMEM_REF] * 6,
        [],
        cost(2, nodes, slab, rows),
    )(
        [offs, x, *bands, acc, *derivs, states, eps, decay],
        [SMEM_REF] + [VMEM_REF] * (8 + len(bands)),
    )


def grad_w_part(base, offs_ref, delta_t_ref, xs, out_ref, held, sems):
    rows, slab = delta_t_ref.shape[0], xs[0].shape[1]
    slots, tile = held.shape[:2]
    step = min(256, slab)
    copies = []
    for at, x_ref in enumerate(xs):
        for start in range(0, rows, tile):
            slot, band = len(copies) % slots, pl.ds(start, tile)
            if len(copies) >= slots:
                copies[-slots].wait()
            for col in range(0, slab, step):
                held[slot, :, col : col + step] = jnp.dot(
                    delta_t_ref[band, :], x_ref[:, col : col + step],
                    preferred_element_type=jnp.float32,
                ).astype(held.dtype)
            there = columns_of(offs_ref, base + at, slab)
            copy = pltpu.make_async_copy(held.at[slot], out_ref.at[band, there], sems.at[slot])
            copy.start()
            copies.append(copy)
    return copies[-slots:]


def share_part(places, offs_ref, delta_ref, bands, outs):
    depth = GROUP * bands[0].shape[0]
    for place, out_ref in zip(places, outs):
        slab = out_ref.shape[1]
        tile = max(slab // 2, 128)
        for col in range(0, slab, tile):
            there = pl.ds(pl.multiple_of(offs_ref[place] * slab + col, tile), tile)
            part = None
            for at in range(len(bands) // GROUP):
                group = bands[at * GROUP : (at + 1) * GROUP]
                more = jnp.dot(
                    delta_ref[:, at * depth : (at + 1) * depth],
                    jnp.concatenate([ref[:, there] for ref in group], axis=0),
                    preferred_element_type=jnp.float32,
                )
                part = more if part is None else part + more
            out_ref[:, pl.ds(col, tile)] = part.astype(out_ref.dtype)


def sums_kernel(base, count, places, many, first, *refs):
    offs_ref, delta_ref, delta_t_ref = refs[:3]
    xs, bands = refs[3 : 3 + count], refs[3 + count : 3 + count + many]
    refs = refs[3 + count + many + (0 if first else 1) :]
    outs, copies = refs[: len(places)], []
    if count:
        out_ref, held, sems = refs[len(places) :]
        copies = grad_w_part(base, offs_ref, delta_t_ref, xs, out_ref, held, sems)
    share_part(places, offs_ref, delta_ref, bands, outs)
    for copy in copies:
        copy.wait()


def sums(offs, base, xs, places, delta, delta_t, bands, slab, so_far, shape):
    nodes, rows = delta.shape
    count, own = len(xs), len(places) // 2
    tile = rows // 2
    first = so_far is None
    shapes = [jax.ShapeDtypeStruct((nodes, slab), jnp.bfloat16)] * own
    shapes += [jax.ShapeDtypeStruct((nodes, slab), jnp.float32)] * own
    specs, scratch = [VMEM_REF] * (2 * own), []
    if count:
        shapes += [
            jax.ShapeDtypeStruct(shape, jnp.bfloat16),
        ]
        specs += [ANY_REF]
        scratch = [pltpu.VMEM((4, tile, slab), jnp.bfloat16), pltpu.SemaphoreType.DMA((4,))]
    operands = [offs, delta, delta_t, *xs, *bands] + ([] if first else [so_far])
    outs = call(
        functools.partial(sums_kernel, base, count, places, len(bands), first),
        shapes,
        specs,
        scratch,
        cost(count + 2 * own, nodes, slab, rows),
        {} if first else {len(operands) - 1: 2 * own},
    )(
        operands,
        [SMEM_REF] + [VMEM_REF] * (2 + count + len(bands)) + ([] if first else [ANY_REF]),
    )
    return outs[:own], outs[own : 2 * own], outs[2 * own :]


def ring_body(chips, states, weights, pert_table, eps_gain, decay, perts):
    _, nodes, slab = states.shape
    rows = weights.shape[0]
    order = chip_ring(chips)
    place = np.argsort(order)
    half, cut = chips // 2, nodes // 2

    near = [0]
    for step in range(1, half):
        near += [-step, step]
    near.append(half)
    listing = [(0, 0)]
    for step in range(half):
        now = [0] if step == 0 else [-step, step]
        then = [half] if step == half - 1 else [-step - 1, step + 1]
        listing += [(at, 1) for at in now] + [(at, 0) for at in then]
    listing.append((half, 1))
    sides = {key: at for at, key in enumerate(listing)}
    table = np.array(
        [
            [
                2 * order[(place[device // 2] + step) % chips] + (device % 2 ^ side)
                for step, side in listing
            ]
            for device in range(2 * chips)
        ],
        dtype=np.int32,
    )
    me = lax.axis_index("row")
    offs = lax.dynamic_slice(jnp.asarray(table), (me, 0), (1, 2 * chips)).reshape(-1)

    def ring(array, way):
        pairs = []
        for at, chip in enumerate(order):
            to = order[(at + way) % chips]
            pairs += [(2 * chip, 2 * to), (2 * chip + 1, 2 * to + 1)]
        return lax.ppermute(array, "row", pairs)

    def swap(array):
        return lax.ppermute(array, "row", [(i, i ^ 1) for i in range(2 * chips)])

    weights = pltpu.with_memory_space_constraint(weights, pltpu.HBM)
    cheb = cheb_matrix(nodes)
    flat = states.reshape(nodes, slab)
    xb = flat.astype(jnp.bfloat16)

    gate = lax.optimization_barrier

    x = {(0, 0): xb}
    behind, ahead, base = xb, xb, 0
    acc, bands, loads = None, [], list(LOADS)
    for step in range(1, half + 1):
        if step < half:
            behind, ahead = ring(behind, 1), ring(ahead, -1)
        else:
            behind, ahead = ring(behind[:cut], 1), ring(ahead[cut:], -1)
        for now in [0] if step == 1 else [1 - step, step - 1]:
            x[now, 1] = swap(x[now, 0])
        count = {1: 1, 2: 3}.get(step, 4)
        late = loads.pop(0) if loads else 0
        xs = [x[key] for key in listing[: base + count]]
        acc, bands = add_products(
            offs, perts, weights, acc, bands, xs[:base], xs[base:], late
        )
        base += count
        if step == half - 1:
            derivs = derivatives(perts, cheb, flat, pert_table)
            acc, *derivs = gate((acc, *derivs))
        behind, ahead, acc = gate((behind, ahead, acc))
        if step < half:
            x[-step, 0], x[step, 0] = behind, ahead
        else:
            x[half, 0] = jnp.concatenate([behind, ahead], axis=0)
    x[half, 1] = swap(x[half, 0])
    xs = [x[key] for key in listing[: base + 3]]
    acc, _ = add_products(offs, perts, weights, acc, bands, xs[:base], xs[base:], 0)
    base += 3

    decay = decay.reshape(1, rows)
    resid, delta, delta_t, grad_table, grad_eps, grad_decay = middle(
        offs, base, x[half, 1], bands, acc, derivs, flat, eps_gain.reshape(1, rows), decay
    )

    grad_w, base = None, 0

    def work(offs, count, steps, grad_w, base):
        places = [sides[step, side] for side in (1, 0) for step in steps]
        xs = [x[key] for key in listing[base : base + count]]
        others, owns, rest = sums(
            offs, base, xs, places, delta, delta_t, bands, slab, grad_w, weights.shape
        )
        if count:
            (grad_w,) = rest
        return others, owns, grad_w, base + count

    def joined(others, owns):
        return [own + swap(other).astype(jnp.float32) for other, own in zip(others, owns)]

    counts = [2, 4, 5]
    counts.append(len(listing) - sum(counts))
    others, owns, _, _ = work(offs, 0, [half], None, 0)
    (far,) = joined(others, owns)
    others, owns, _, _ = work(offs, 0, [half - 1, 1 - half], None, 0)
    far, offs, *owns = gate((far.astype(jnp.bfloat16), offs, *owns))
    own_ahead, own_behind = joined(others, owns)
    ahead, behind = ring(far[:cut], 1), ring(far[cut:], -1)
    for step in range(half - 1, -1, -1):
        steps = [] if step == 0 else [0] if step == 1 else [step - 1, 1 - step]
        others, owns, grad_w, base = work(offs, counts.pop(0), steps, grad_w, base)
        if step == 0:
            break
        ahead, behind, *owns = gate((ahead, behind, *owns))
        ahead, behind = ahead.astype(jnp.float32), behind.astype(jnp.float32)
        if step == half - 1:
            ahead = jnp.concatenate([own_ahead[:cut] + ahead, own_ahead[cut:]], axis=0)
            behind = jnp.concatenate([own_behind[:cut], own_behind[cut:] + behind], axis=0)
        else:
            ahead, behind = own_ahead + ahead, own_behind + behind
        ahead, behind = ahead.astype(jnp.bfloat16), behind.astype(jnp.bfloat16)
        if step > 1:
            own_ahead, own_behind = joined(others, owns)
        else:
            (near_share,) = joined(others, owns)
        ahead, behind, offs = gate((ahead, behind, offs))
        ahead, behind = ring(ahead, 1), ring(behind, -1)

    local = local_terms(cheb, resid, decay)
    ahead, behind, local = gate((ahead, behind, local))
    grad_x = local + near_share + ahead.astype(jnp.float32) + behind.astype(jnp.float32)
    grad_x = grad_x.reshape(states.shape)
    return (grad_w, grad_x, grad_table, grad_eps.reshape(rows), grad_decay.reshape(rows))


def plain_body(states, weights, pert_table, eps_gain, decay, perts):
    traj, nodes, slab = states.shape
    total = traj * nodes
    cheb = cheb_matrix(nodes)
    xb = states.astype(jnp.bfloat16).reshape(total, slab)
    full = lax.all_gather(xb, "row", axis=1, tiled=True)
    pre = lax.dot_general(
        full, weights, (((1,), (1,)), ((), ())), preferred_element_type=jnp.float32
    )
    onehot = (perts[:, None] == jnp.arange(pert_table.shape[0], dtype=jnp.int32)[None, :]).astype(
        jnp.float32
    )
    drive = jnp.dot(onehot, pert_table, precision=lax.Precision.HIGHEST)
    act = jnp.tanh(pre.reshape(traj, nodes, slab) + drive[:, None, :])
    deriv = SCALE * jnp.einsum("kl,clg->ckg", cheb, states, precision=lax.Precision.HIGHEST)
    resid = deriv - (eps_gain * act - decay * states)
    delta = (-eps_gain * (1.0 - act * act) * resid).astype(jnp.bfloat16)
    dflat = delta.reshape(total, slab)
    grad_w = lax.dot_general(
        dflat, full, (((0,), (0,)), ((), ())), preferred_element_type=jnp.float32
    ).astype(jnp.bfloat16)
    back = jnp.dot(dflat, weights, preferred_element_type=jnp.float32)
    back = lax.psum_scatter(back, "row", scatter_dimension=1, tiled=True)
    grad_x = (
        SCALE * jnp.einsum("lk,clg->ckg", cheb, resid, precision=lax.Precision.HIGHEST)
        + decay * resid
        + back.reshape(traj, nodes, slab)
    )
    node_sums = jnp.sum(delta.astype(jnp.float32), axis=1)
    grad_table = jnp.dot(onehot.T, node_sums, precision=lax.Precision.HIGHEST)
    grad_eps = -jnp.sum(act * resid, axis=(0, 1))
    grad_decay = jnp.sum(states * resid, axis=(0, 1))
    return (grad_w, grad_x, grad_table, grad_eps, grad_decay)


def solution(mesh):
    chips = mesh.shape["row"] // 2
    in_specs = (
        P("rep", None, "row"),
        P(("rep", "row"), None),
        P("rep", "row"),
        P(("rep", "row")),
        P(("rep", "row")),
        P("rep"),
    )
    out_specs = (
        P(("rep", "row"), None),
        P("rep", None, "row"),
        P("rep", "row"),
        P(("rep", "row")),
        P(("rep", "row")),
    )

    def run(states, *others):
        if states.shape[0] == 1 and chips <= LONGEST_RING:
            return ring_body(chips, states, *others)
        return plain_body(states, *others)

    return jax.shard_map(run, mesh=mesh, in_specs=in_specs, out_specs=out_specs, check_vma=False)
```

```python
import functools

import jax
import jax.numpy as jnp
import numpy as np
from jax import lax
from jax.experimental import pallas as pl
from jax.experimental.pallas import tpu as pltpu
from jax.sharding import PartitionSpec as P

SCALE = 2.0 / 1024.0
VMEM_LIMIT = 8 * 2**20
BANDS = 16
GROUP = 4
LOADS = (10, 6)
PIECES = (2, 4, 5)
LONGEST_RING = 16


def cheb_matrix(count):
    index = np.arange(count)
    points = np.cos(np.pi * index / (count - 1))
    signs = np.where(index % 2 == 0, 1.0, -1.0)
    weight_c = signs * np.where((index == 0) | (index == count - 1), 2.0, 1.0)
    same = index[:, None] == index[None, :]
    spread = np.where(same, 1.0, points[:, None] - points[None, :])
    off = np.where(same, 0.0, weight_c[:, None] / weight_c[None, :] / spread)
    return jnp.asarray((off - np.diag(np.sum(off, axis=1))).astype(np.float32))


def chip_ring(chips):
    rows = 4
    cols = chips // rows
    cells = [(0, col) for col in range(cols)]
    for row in range(1, rows):
        span = range(1, cols)
        cells += [(row, col) for col in (reversed(span) if row % 2 else span)]
    cells += [(row, 0) for row in range(rows - 1, 0, -1)]
    return [row * cols + col for row, col in cells]


VMEM_REF = pl.BlockSpec(memory_space=pltpu.VMEM)
SMEM_REF = pl.BlockSpec(memory_space=pltpu.SMEM)
ANY_REF = pl.BlockSpec(memory_space=pl.ANY)
HBM_REF = pl.BlockSpec(memory_space=pltpu.HBM)


def cost(products, nodes, slab, rows):
    return pl.CostEstimate(
        flops=2 * products * nodes * slab * rows // 16,
        bytes_accessed=2 * products * slab * rows // 16,
        transcendentals=0,
    )


def call(kernel, out_shape, out_specs, scratch, costs, aliases=None):
    def run(operands, in_specs):
        return pl.pallas_call(
            kernel,
            out_shape=out_shape,
            in_specs=in_specs,
            out_specs=out_specs,
            scratch_shapes=scratch,
            input_output_aliases=aliases or {},
            compiler_params=pltpu.CompilerParams(vmem_limit_bytes=VMEM_LIMIT),
            cost_estimate=costs,
        )(*operands)

    return run


def columns_of(offs_ref, at, slab):
    return pl.ds(pl.multiple_of(offs_ref[at] * slab, slab), slab)


def load_bands(w_ref, bands, sems, first):
    copies = []
    for at, band_ref in enumerate(bands):
        tile = band_ref.shape[0]
        rows = pl.ds((first + at) * tile, tile)
        copies.append(pltpu.make_async_copy(w_ref.at[rows, :], band_ref, sems.at[at]))
        copies[-1].start()
    return copies


def product(bands, here, x_ref):
    return lax.dot_general(
        jnp.concatenate([band_ref[:, here] for band_ref in bands], axis=0), x_ref[...],
        (((1,), (1,)), ((), ())), preferred_element_type=jnp.float32,
    )


def split_pieces(pieces):
    arrays, found = [], []
    for array, index in pieces:
        at = [place for place, other in enumerate(arrays) if other is array]
        if not at:
            arrays.append(array)
        found.append((at[0] if at else len(arrays) - 1, index))
    return arrays, found


def load_kernel(offs_ref, perts_ref, w_ref, mark_ref, *refs):
    mark_ref[...] = jnp.zeros_like(mark_ref)
    for copy in load_bands(w_ref, refs[:-1], refs[-1], 0):
        copy.wait()


def band_shapes(count, weights):
    return [pltpu.VMEM((weights.shape[0] // BANDS, weights.shape[1]), weights.dtype)] * count


def load_first(offs, perts, weights, count):
    mark, *bands = call(
        load_kernel,
        [jax.ShapeDtypeStruct((8, 128), jnp.float32)] + band_shapes(count, weights),
        [VMEM_REF] * (1 + count),
        [pltpu.SemaphoreType.DMA((count,))],
        cost(1, 128, 128, 1024),
    )([offs, perts, weights], [SMEM_REF, SMEM_REF, HBM_REF])
    return mark, bands


def pre_kernel(found, count, many, fresh, late, offs_ref, acc_ref, *refs):
    if late:
        w_ref, refs = refs[0], refs[1:]
    bands, refs = refs[:many], refs[many:]
    arrays = 1 + max(at for at, _ in found)
    xs, out_ref, others, sems = refs[:arrays], refs[arrays], refs[arrays + 1 : -1], refs[-1]
    slab = xs[0].shape[-1]
    tile = out_ref.shape[0] // BANDS
    copies = load_bands(w_ref, others, sems, many) if late else []
    for low in [*range(0, many - fresh, GROUP), *range(many - fresh, many, GROUP)]:
        old = low < many - fresh
        group = bands[low : min(low + GROUP, many - fresh if old else many)]
        rows = pl.ds(low * tile, len(group) * tile)
        total = acc_ref[rows, :] if old else None
        for place in range(len(found) - count if old else 0, len(found)):
            at, index = found[place]
            part = product(group, columns_of(offs_ref, place, slab), xs[at].at[index])
            total = part if total is None else total + part
        out_ref[rows, :] = total
    for copy in copies:
        copy.wait()


def add_products(offs, weights, acc, bands, pieces, count, fresh, late):
    arrays, found = split_pieces(pieces if fresh else pieces[-count:])
    if not fresh:
        found = [(0, 0)] * (len(pieces) - count) + found
    (_, nodes, slab), rows, many = arrays[0].shape, weights.shape[0], len(bands)
    operands = [offs, acc] + ([weights] if late else []) + [*bands, *arrays]
    acc, *others = call(
        functools.partial(pre_kernel, found, count, many, fresh, late),
        [jax.ShapeDtypeStruct((rows, nodes), jnp.float32)] + band_shapes(late, weights),
        [VMEM_REF] * (1 + late),
        [pltpu.SemaphoreType.DMA((max(late, 1),))],
        cost(count, nodes, slab, rows),
    )(
        operands,
        [SMEM_REF, VMEM_REF] + ([HBM_REF] if late else [])
        + [VMEM_REF] * (many + len(arrays)),
    )
    return acc, [*bands, *others]


def cheb_dot(turned, cheb_ref, array_ref):
    return SCALE * lax.dot_general(
        cheb_ref[...], array_ref[...], (((0 if turned else 1,), (0,)), ((), ())),
        precision=lax.Precision.HIGHEST, preferred_element_type=jnp.float32,
    )


def deriv_kernel(perts_ref, cheb_ref, states_ref, pert_ref, deriv_ref, drive_ref, chosen_ref):
    pert = perts_ref[0]
    deriv_ref[...] = cheb_dot(False, cheb_ref, states_ref)
    drive_ref[...] = pert_ref[pl.ds(pert, 1), :]
    rows = lax.broadcasted_iota(jnp.int32, chosen_ref.shape, 0)
    chosen_ref[...] = (rows == pert).astype(jnp.float32)


def derivatives(perts, cheb, states, pert_table):
    return call(
        deriv_kernel,
        [
            jax.ShapeDtypeStruct(states.shape, jnp.float32),
            jax.ShapeDtypeStruct((1, states.shape[1]), jnp.float32),
            jax.ShapeDtypeStruct(pert_table.shape, jnp.float32),
        ],
        [VMEM_REF] * 3,
        [],
        cost(1, *states.shape, states.shape[0]),
    )([perts, cheb, states, pert_table], [SMEM_REF] + [VMEM_REF] * 3)


def local_kernel(cheb_ref, resid_ref, decay_ref, out_ref):
    out_ref[...] = cheb_dot(True, cheb_ref, resid_ref) + decay_ref[...] * resid_ref[...]


def local_terms(cheb, resid, decay):
    return call(
        local_kernel,
        jax.ShapeDtypeStruct(resid.shape, jnp.float32),
        VMEM_REF,
        [],
        cost(1, *resid.shape, resid.shape[0]),
    )([cheb, resid, decay], [VMEM_REF] * 3)


def middle_kernel(base, many, offs_ref, x_ref, *refs):
    bands = refs[:many]
    acc_ref, deriv_ref, drive_ref, chosen_ref, states_ref, eps_ref, decay_ref = refs[many:-6]
    resid_ref, delta_ref, delta_t_ref, table_ref, sum_eps_ref, sum_decay_ref = refs[-6:]
    tile = GROUP * bands[0].shape[0]
    here = columns_of(offs_ref, base, x_ref.shape[-1])
    for at in range(many // GROUP):
        band = pl.ds(at * tile, tile)
        part = acc_ref[band, :] + product(bands[at * GROUP : (at + 1) * GROUP], here, x_ref.at[0])
        states = states_ref[:, band]
        act = jnp.tanh(part.T + drive_ref[:, band])
        eps = eps_ref[:, band]
        resid = deriv_ref[:, band] - (eps * act - decay_ref[:, band] * states)
        delta = (-eps * (1.0 - act * act) * resid).astype(jnp.bfloat16)
        wide = delta.astype(jnp.float32)
        resid_ref[:, band] = resid
        delta_ref[:, band] = delta
        delta_t_ref[band, :] = wide.T.astype(jnp.bfloat16)
        table_ref[:, band] = chosen_ref[:, band] * jnp.sum(wide, axis=0, keepdims=True)
        sum_eps_ref[:, band] = -jnp.sum(act * resid, axis=0, keepdims=True)
        sum_decay_ref[:, band] = jnp.sum(states * resid, axis=0, keepdims=True)


def middle(offs, base, x, bands, acc, derivs, states, eps, decay):
    _, nodes, slab = x.shape
    rows = acc.shape[0]
    wide = functools.partial(jax.ShapeDtypeStruct, dtype=jnp.float32)
    return call(
        functools.partial(middle_kernel, base, len(bands)),
        [
            wide((nodes, rows)),
            jax.ShapeDtypeStruct((nodes, rows), jnp.bfloat16),
            jax.ShapeDtypeStruct((rows, nodes), jnp.bfloat16),
            wide(derivs[2].shape),
            wide((1, rows)),
            wide((1, rows)),
        ],
        [VMEM_REF] * 6,
        [],
        cost(2, nodes, slab, rows),
    )(
        [offs, x, *bands, acc, *derivs, states, eps, decay],
        [SMEM_REF] + [VMEM_REF] * (8 + len(bands)),
    )


def grad_w_part(base, offs_ref, delta_t_ref, xs, out_ref, held, sems):
    rows, slab = delta_t_ref.shape[0], held.shape[2]
    slots, tile = held.shape[:2]
    step = min(256, slab)
    copies = []
    for at, x_ref in enumerate(xs):
        for start in range(0, rows, tile):
            slot, band = len(copies) % slots, pl.ds(start, tile)
            if len(copies) >= slots:
                copies[-slots].wait()
            for col in range(0, slab, step):
                held[slot, :, col : col + step] = jnp.dot(
                    delta_t_ref[band, :], x_ref[:, col : col + step],
                    preferred_element_type=jnp.float32,
                ).astype(held.dtype)
            there = columns_of(offs_ref, base + at, slab)
            copy = pltpu.make_async_copy(held.at[slot], out_ref.at[band, there], sems.at[slot])
            copy.start()
            copies.append(copy)
    return copies[-slots:]


def share_part(places, offs_ref, delta_ref, bands, out_ref):
    depth, slab = GROUP * bands[0].shape[0], out_ref.shape[2]
    tile = max(slab // 2, 128)
    for index, place in enumerate(places):
        for col in range(0, slab, tile):
            there = pl.ds(pl.multiple_of(offs_ref[place] * slab + col, tile), tile)
            part = None
            for at in range(len(bands) // GROUP):
                group = bands[at * GROUP : (at + 1) * GROUP]
                more = jnp.dot(
                    delta_ref[:, at * depth : (at + 1) * depth],
                    jnp.concatenate([ref[:, there] for ref in group], axis=0),
                    preferred_element_type=jnp.float32,
                )
                part = more if part is None else part + more
            out_ref[index, :, pl.ds(col, tile)] = part.astype(out_ref.dtype)


def sums_kernel(base, found, arrays, sent, kept, many, first, *refs):
    offs_ref, delta_ref, delta_t_ref = refs[:3]
    xs, bands = refs[3 : 3 + arrays], refs[3 + arrays : 3 + arrays + many]
    refs = refs[3 + arrays + many + (0 if first else 1) :]
    copies = []
    if found:
        out_ref, held, sems = refs[-3:]
        views = [xs[at].at[index] for at, index in found]
        copies = grad_w_part(base, offs_ref, delta_t_ref, views, out_ref, held, sems)
    if sent:
        share_part(sent, offs_ref, delta_ref, bands, refs[0])
        share_part(kept, offs_ref, delta_ref, bands, refs[1])
    for copy in copies:
        copy.wait()


def sums(offs, base, pieces, sent, kept, delta, delta_t, bands, slab, so_far, shape):
    nodes, rows = delta.shape
    arrays, found = split_pieces(pieces)
    first = so_far is None
    tile = rows // 2
    shapes, scratch = [], []
    if sent:
        shapes = [
            jax.ShapeDtypeStruct((len(sent), nodes, slab), jnp.bfloat16),
            jax.ShapeDtypeStruct((len(kept), nodes, slab), jnp.float32),
        ]
    specs = [VMEM_REF] * len(shapes)
    if found:
        shapes, specs = shapes + [jax.ShapeDtypeStruct(shape, jnp.bfloat16)], specs + [ANY_REF]
        scratch = [pltpu.VMEM((4, tile, slab), jnp.bfloat16), pltpu.SemaphoreType.DMA((4,))]
    operands = [offs, delta, delta_t, *arrays, *bands] + ([] if first else [so_far])
    outs = call(
        functools.partial(
            sums_kernel, base, found, len(arrays), sent, kept, len(bands), first
        ),
        shapes,
        specs,
        scratch,
        cost(len(found) + len(sent) + len(kept), nodes, slab, rows),
        {} if first else {len(operands) - 1: len(shapes) - 1},
    )(
        operands,
        [SMEM_REF] + [VMEM_REF] * (2 + len(arrays) + len(bands))
        + ([] if first else [ANY_REF]),
    )
    others, owns = outs[:2] if sent else (None, None)
    return others, owns, outs[-1] if found else so_far


def ring_body(chips, states, weights, pert_table, eps_gain, decay, perts):
    _, nodes, slab = states.shape
    rows = weights.shape[0]
    order = chip_ring(chips)
    place = np.argsort(order)
    half = chips // 2

    listing = [(0, 0), (0, 1)]
    for step in range(1, half):
        listing += [(step, 0), (step, 1), (-step, 1), (-step, 0)]
    listing += [(half, 0), (half, 1)]
    sides = {key: at for at, key in enumerate(listing)}
    table = np.array(
        [
            [
                2 * order[(place[device // 2] + (step if device % 2 else -step)) % chips]
                + (device % 2 ^ side)
                for step, side in listing
            ]
            for device in range(2 * chips)
        ],
        dtype=np.int32,
    )
    me = lax.axis_index("row")
    offs = lax.dynamic_slice(jnp.asarray(table), (me, 0), (1, 2 * chips)).reshape(-1)

    def passed(array, way=1, cross=0):
        pairs = []
        for at, chip in enumerate(order):
            pairs.append((2 * chip, 2 * order[(at + way) % chips] + cross))
            pairs.append((2 * chip + 1, 2 * order[(at - way) % chips] + 1 - cross))
        return lax.ppermute(array, "row", pairs)

    def swap(array):
        return lax.ppermute(array, "row", [(i, i ^ 1) for i in range(2 * chips)])

    gate = lax.optimization_barrier
    weights = pltpu.with_memory_space_constraint(weights, pltpu.HBM)
    cheb = cheb_matrix(nodes)
    flat = states.reshape(nodes, slab)
    xb = states.astype(jnp.bfloat16)

    near, over = passed(xb), passed(xb, -1, 1)
    other = swap(xb)
    mark, bands = load_first(offs, perts, weights, LOADS[0])
    near, over, other, mark = gate((near, over, other, mark))
    x = {(0, 0): (xb, 0), (0, 1): (other, 0)}
    flow = jnp.concatenate([near, over], axis=0)
    acc, seen = mark, 0
    for step in range(1, half + 1):
        if step < half:
            x[step, 0], x[step, 1] = (flow, 0), (flow, 1)
            other = flow
        else:
            x[half, 0], other = (flow, 0), flow
        if step < half:
            flow = passed(flow if step < half - 1 else flow[:1])
        other = swap(other)
        if step < half:
            x[-step, 1], x[-step, 0] = (other, 0), (other, 1)
        else:
            x[half, 1] = (other, 0)
        count = 3 if step == half else 4
        late = LOADS[1] if step == 1 else 0
        acc, bands = add_products(
            offs, weights, acc, bands, [x[key] for key in listing[: seen + count]], count,
            LOADS[1] if step == 2 else len(bands) if step == 1 else 0, late,
        )
        seen += count
        if step == half - 2:
            derivs = derivatives(perts, cheb, flat, pert_table)
            acc, *derivs = gate((acc, *derivs))
        if step < half:
            flow, acc = gate((flow, acc))

    decay = decay.reshape(1, rows)
    resid, delta, delta_t, grad_table, grad_eps, grad_decay = middle(
        offs, seen, x[half, 1][0], bands, acc, derivs, flat, eps_gain.reshape(1, rows), decay
    )

    grad_w, base = None, 0

    def work(offs, count, step, grad_w, base):
        if step is None:
            sent, kept = [], []
        elif step in (0, half):
            sent, kept = [sides[step, 1]], [sides[step, 0]]
        else:
            sent = [sides[step, 1], sides[step, 0]]
            kept = [sides[-step, 0], sides[-step, 1]]
        others, owns, grad_w = sums(
            offs, base, [x[key] for key in listing[base : base + count]], sent, kept,
            delta, delta_t, bands, slab, grad_w, weights.shape,
        )
        return others, owns, grad_w, base + count

    def joined(others, owns):
        return owns + swap(others).astype(jnp.float32)

    counts = list(PIECES)
    others, owns, _, _ = work(offs, 0, half, None, 0)
    far = joined(others, owns).astype(jnp.bfloat16)
    others, owns, _, _ = work(offs, 0, half - 1, None, 0)
    far, offs, owns = gate((far, offs, owns))
    share = joined(others, owns)
    flow = passed(far)
    for step in range(half - 1, 0, -1):
        others, owns, grad_w, base = work(offs, counts.pop(0), step - 1, grad_w, base)
        flow, owns = gate((flow, owns))
        flow = flow.astype(jnp.float32)
        if step == half - 1:
            total = jnp.concatenate([share[:1] + flow, share[1:]], axis=0)
        else:
            total = share + flow
        total = total.astype(jnp.bfloat16)
        share = joined(others, owns)
        total, offs = gate((total, offs))
        if step > 1:
            flow = passed(total)
        else:
            near, over = passed(total[:1]), passed(total[1:], 1, 1)
    _, _, grad_w, base = work(offs, len(listing) - base, None, grad_w, base)
    local = local_terms(cheb, resid, decay)
    near, over, local = gate((near, over, local))
    grad_x = local + share[0] + near[0].astype(jnp.float32) + over[0].astype(jnp.float32)
    grad_x = grad_x.reshape(states.shape)
    return (grad_w, grad_x, grad_table, grad_eps.reshape(rows), grad_decay.reshape(rows))


def plain_body(states, weights, pert_table, eps_gain, decay, perts):
    traj, nodes, slab = states.shape
    total = traj * nodes
    cheb = cheb_matrix(nodes)
    xb = states.astype(jnp.bfloat16).reshape(total, slab)
    full = lax.all_gather(xb, "row", axis=1, tiled=True)
    pre = lax.dot_general(
        full, weights, (((1,), (1,)), ((), ())), preferred_element_type=jnp.float32
    )
    onehot = (perts[:, None] == jnp.arange(pert_table.shape[0], dtype=jnp.int32)[None, :]).astype(
        jnp.float32
    )
    drive = jnp.dot(onehot, pert_table, precision=lax.Precision.HIGHEST)
    act = jnp.tanh(pre.reshape(traj, nodes, slab) + drive[:, None, :])
    deriv = SCALE * jnp.einsum("kl,clg->ckg", cheb, states, precision=lax.Precision.HIGHEST)
    resid = deriv - (eps_gain * act - decay * states)
    delta = (-eps_gain * (1.0 - act * act) * resid).astype(jnp.bfloat16)
    dflat = delta.reshape(total, slab)
    grad_w = lax.dot_general(
        dflat, full, (((0,), (0,)), ((), ())), preferred_element_type=jnp.float32
    ).astype(jnp.bfloat16)
    back = jnp.dot(dflat, weights, preferred_element_type=jnp.float32)
    back = lax.psum_scatter(back, "row", scatter_dimension=1, tiled=True)
    grad_x = (
        SCALE * jnp.einsum("lk,clg->ckg", cheb, resid, precision=lax.Precision.HIGHEST)
        + decay * resid
        + back.reshape(traj, nodes, slab)
    )
    node_sums = jnp.sum(delta.astype(jnp.float32), axis=1)
    grad_table = jnp.dot(onehot.T, node_sums, precision=lax.Precision.HIGHEST)
    grad_eps = -jnp.sum(act * resid, axis=(0, 1))
    grad_decay = jnp.sum(states * resid, axis=(0, 1))
    return (grad_w, grad_x, grad_table, grad_eps, grad_decay)


def solution(mesh):
    chips = mesh.shape["row"] // 2
    in_specs = (
        P("rep", None, "row"),
        P(("rep", "row"), None),
        P("rep", "row"),
        P(("rep", "row")),
        P(("rep", "row")),
        P("rep"),
    )
    out_specs = (
        P(("rep", "row"), None),
        P("rep", None, "row"),
        P("rep", "row"),
        P(("rep", "row")),
        P(("rep", "row")),
    )

    def run(states, *others):
        if states.shape[0] == 1 and chips <= LONGEST_RING:
            return ring_body(chips, states, *others)
        return plain_body(states, *others)

    return jax.shard_map(run, mesh=mesh, in_specs=in_specs, out_specs=out_specs, check_vma=False)
```

```python
import functools

import jax
import jax.numpy as jnp
import numpy as np
from jax import lax
from jax.experimental import pallas as pl
from jax.experimental.pallas import tpu as pltpu
from jax.sharding import PartitionSpec as P

SCALE = 2.0 / 1024.0
VMEM_LIMIT = 8 * 2**20
BANDS = 16
GROUP = 4
LOADS = (8, 6, 2)
PIECES = (0, 5, 6)


def cheb_matrix(count):
    index = np.arange(count)
    points = np.cos(np.pi * index / (count - 1))
    signs = np.where(index % 2 == 0, 1.0, -1.0)
    weight_c = signs * np.where((index == 0) | (index == count - 1), 2.0, 1.0)
    same = index[:, None] == index[None, :]
    spread = np.where(same, 1.0, points[:, None] - points[None, :])
    off = np.where(same, 0.0, weight_c[:, None] / weight_c[None, :] / spread)
    return jnp.asarray((off - np.diag(np.sum(off, axis=1))).astype(np.float32))


def chip_ring(chips):
    rows = 4
    cols = chips // rows
    cells = [(0, col) for col in range(cols)]
    for row in range(1, rows):
        span = range(1, cols)
        cells += [(row, col) for col in (reversed(span) if row % 2 else span)]
    cells += [(row, 0) for row in range(rows - 1, 0, -1)]
    return [row * cols + col for row, col in cells]


VMEM_REF = pl.BlockSpec(memory_space=pltpu.VMEM)
SMEM_REF = pl.BlockSpec(memory_space=pltpu.SMEM)
ANY_REF = pl.BlockSpec(memory_space=pl.ANY)
HBM_REF = pl.BlockSpec(memory_space=pltpu.HBM)


def cost(products, nodes, slab, rows):
    return pl.CostEstimate(
        flops=2 * products * nodes * slab * rows // 16,
        bytes_accessed=2 * products * slab * rows // 16,
        transcendentals=0,
    )


def call(kernel, out_shape, out_specs, scratch, costs, aliases=None):
    def run(operands, in_specs):
        return pl.pallas_call(
            kernel,
            out_shape=out_shape,
            in_specs=in_specs,
            out_specs=out_specs,
            scratch_shapes=scratch,
            input_output_aliases=aliases or {},
            compiler_params=pltpu.CompilerParams(vmem_limit_bytes=VMEM_LIMIT),
            cost_estimate=costs,
        )(*operands)

    return run


def columns_of(offs_ref, at, slab):
    return pl.ds(pl.multiple_of(offs_ref[at] * slab, slab), slab)


def load_bands(w_ref, bands, sems, first):
    copies = []
    for at, band_ref in enumerate(bands):
        tile = band_ref.shape[0]
        rows = pl.ds((first + at) * tile, tile)
        copies.append(pltpu.make_async_copy(w_ref.at[rows, :], band_ref, sems.at[at]))
        copies[-1].start()
    return copies


def product(bands, here, x_ref):
    return lax.dot_general(
        jnp.concatenate([band_ref[:, here] for band_ref in bands], axis=0), x_ref[...],
        (((1,), (1,)), ((), ())), preferred_element_type=jnp.float32,
    )


def split_pieces(pieces):
    arrays, found = [], []
    for array, index in pieces:
        at = [place for place, other in enumerate(arrays) if other is array]
        if not at:
            arrays.append(array)
        found.append((at[0] if at else len(arrays) - 1, index))
    return arrays, found


def load_kernel(offs_ref, perts_ref, w_ref, mark_ref, *refs):
    mark_ref[...] = jnp.zeros_like(mark_ref)
    for copy in load_bands(w_ref, refs[:-1], refs[-1], 0):
        copy.wait()


def band_shapes(count, weights):
    return [pltpu.VMEM((weights.shape[0] // BANDS, weights.shape[1]), weights.dtype)] * count


def load_first(offs, perts, weights, count):
    mark, *bands = call(
        load_kernel,
        [jax.ShapeDtypeStruct((8, 128), jnp.float32)] + band_shapes(count, weights),
        [VMEM_REF] * (1 + count),
        [pltpu.SemaphoreType.DMA((count,))],
        cost(1, 128, 128, 1024),
    )([offs, perts, weights], [SMEM_REF, SMEM_REF, HBM_REF])
    return mark, bands


def pre_kernel(found, count, many, fresh, late, ripe, offs_ref, acc_ref, *refs):
    if late:
        w_ref, refs = refs[0], refs[1:]
    bands, refs = refs[:many], refs[many:]
    arrays = 1 + max(at for at, _ in found)
    xs, out_ref, others, sems = refs[:arrays], refs[arrays], refs[arrays + 1 : -1], refs[-1]
    slab = xs[0].shape[-1]
    tile = out_ref.shape[0] // BANDS
    copies = load_bands(w_ref, others, sems, many) if late else []
    for low in [*range(0, many - fresh, GROUP), *range(many - fresh, many, GROUP)]:
        old = low < many - fresh
        group = bands[low : min(low + GROUP, many - fresh if old else many)]
        rows = pl.ds(low * tile, len(group) * tile)
        total = acc_ref[rows, :] if old else None
        for place in range(len(found) - count if old else 0, len(found)):
            at, index = found[place]
            part = product(group, columns_of(offs_ref, place, slab), xs[at].at[index])
            total = part if total is None else total + part
        out_ref[rows, :] = total
    for copy in copies:
        copy.wait()
    if ripe:
        rows, total = pl.ds(many * tile, late * tile), None
        for place, (at, index) in enumerate(found):
            part = product(others, columns_of(offs_ref, place, slab), xs[at].at[index])
            total = part if total is None else total + part
        out_ref[rows, :] = total


def add_products(offs, weights, acc, bands, pieces, count, fresh, late, ripe):
    arrays, found = split_pieces(pieces if fresh else pieces[-count:])
    if not fresh:
        found = [(0, 0)] * (len(pieces) - count) + found
    (_, nodes, slab), rows, many = arrays[0].shape, weights.shape[0], len(bands)
    operands = [offs, acc] + ([weights] if late else []) + [*bands, *arrays]
    acc, *others = call(
        functools.partial(pre_kernel, found, count, many, fresh, late, ripe),
        [jax.ShapeDtypeStruct((rows, nodes), jnp.float32)] + band_shapes(late, weights),
        [VMEM_REF] * (1 + late),
        [pltpu.SemaphoreType.DMA((max(late, 1),))],
        cost(count, nodes, slab, rows),
    )(
        operands,
        [SMEM_REF, VMEM_REF] + ([HBM_REF] if late else [])
        + [VMEM_REF] * (many + len(arrays)),
    )
    return acc, [*bands, *others]


def cheb_dot(turned, cheb_ref, array_ref):
    return SCALE * lax.dot_general(
        cheb_ref[...], array_ref[...], (((0 if turned else 1,), (0,)), ((), ())),
        precision=lax.Precision.HIGHEST, preferred_element_type=jnp.float32,
    )


def deriv_kernel(perts_ref, cheb_ref, states_ref, pert_ref, deriv_ref, drive_ref, chosen_ref):
    pert = perts_ref[0]
    deriv_ref[...] = cheb_dot(False, cheb_ref, states_ref)
    drive_ref[...] = pert_ref[pl.ds(pert, 1), :]
    rows = lax.broadcasted_iota(jnp.int32, chosen_ref.shape, 0)
    chosen_ref[...] = (rows == pert).astype(jnp.float32)


def derivatives(perts, cheb, states, pert_table):
    return call(
        deriv_kernel,
        [
            jax.ShapeDtypeStruct(states.shape, jnp.float32),
            jax.ShapeDtypeStruct((1, states.shape[1]), jnp.float32),
            jax.ShapeDtypeStruct(pert_table.shape, jnp.float32),
        ],
        [VMEM_REF] * 3,
        [],
        cost(1, *states.shape, states.shape[0]),
    )([perts, cheb, states, pert_table], [SMEM_REF] + [VMEM_REF] * 3)


def local_kernel(cheb_ref, resid_ref, decay_ref, out_ref):
    out_ref[...] = cheb_dot(True, cheb_ref, resid_ref) + decay_ref[...] * resid_ref[...]


def local_terms(cheb, resid, decay):
    return call(
        local_kernel,
        jax.ShapeDtypeStruct(resid.shape, jnp.float32),
        VMEM_REF,
        [],
        cost(1, *resid.shape, resid.shape[0]),
    )([cheb, resid, decay], [VMEM_REF] * 3)


def middle_kernel(base, many, offs_ref, x_ref, *refs):
    bands = refs[:many]
    acc_ref, deriv_ref, drive_ref, chosen_ref, states_ref, eps_ref, decay_ref = refs[many:-6]
    resid_ref, delta_ref, delta_t_ref, table_ref, sum_eps_ref, sum_decay_ref = refs[-6:]
    tile = GROUP * bands[0].shape[0]
    here = columns_of(offs_ref, base, x_ref.shape[-1])
    for at in range(many // GROUP):
        band = pl.ds(at * tile, tile)
        part = acc_ref[band, :] + product(bands[at * GROUP : (at + 1) * GROUP], here, x_ref.at[0])
        states = states_ref[:, band]
        act = jnp.tanh(part.T + drive_ref[:, band])
        eps = eps_ref[:, band]
        resid = deriv_ref[:, band] - (eps * act - decay_ref[:, band] * states)
        delta = (-eps * (1.0 - act * act) * resid).astype(jnp.bfloat16)
        wide = delta.astype(jnp.float32)
        resid_ref[:, band] = resid
        delta_ref[:, band] = delta
        delta_t_ref[band, :] = wide.T.astype(jnp.bfloat16)
        table_ref[:, band] = chosen_ref[:, band] * jnp.sum(wide, axis=0, keepdims=True)
        sum_eps_ref[:, band] = -jnp.sum(act * resid, axis=0, keepdims=True)
        sum_decay_ref[:, band] = jnp.sum(states * resid, axis=0, keepdims=True)


def middle(offs, base, x, bands, acc, derivs, states, eps, decay):
    _, nodes, slab = x.shape
    rows = acc.shape[0]
    wide = functools.partial(jax.ShapeDtypeStruct, dtype=jnp.float32)
    return call(
        functools.partial(middle_kernel, base, len(bands)),
        [
            wide((nodes, rows)),
            jax.ShapeDtypeStruct((nodes, rows), jnp.bfloat16),
            jax.ShapeDtypeStruct((rows, nodes), jnp.bfloat16),
            wide(derivs[2].shape),
            wide((1, rows)),
            wide((1, rows)),
        ],
        [VMEM_REF] * 6,
        [],
        cost(2, nodes, slab, rows),
    )(
        [offs, x, *bands, acc, *derivs, states, eps, decay],
        [SMEM_REF] + [VMEM_REF] * (8 + len(bands)),
    )


def grad_w_part(base, offs_ref, delta_t_ref, xs, out_ref, held, sems):
    rows, slab = delta_t_ref.shape[0], held.shape[2]
    slots, tile = held.shape[:2]
    step = min(256, slab)
    copies = []
    for at, x_ref in enumerate(xs):
        for start in range(0, rows, tile):
            slot, band = len(copies) % slots, pl.ds(start, tile)
            if len(copies) >= slots:
                copies[-slots].wait()
            for col in range(0, slab, step):
                held[slot, :, col : col + step] = jnp.dot(
                    delta_t_ref[band, :], x_ref[:, col : col + step],
                    preferred_element_type=jnp.float32,
                ).astype(held.dtype)
            there = columns_of(offs_ref, base + at, slab)
            copy = pltpu.make_async_copy(held.at[slot], out_ref.at[band, there], sems.at[slot])
            copy.start()
            copies.append(copy)
    return copies[-slots:]


def share_part(places, offs_ref, delta_ref, bands, out_ref):
    depth, slab = GROUP * bands[0].shape[0], out_ref.shape[2]
    tile = max(slab // 2, 128)
    for index, place in enumerate(places):
        for col in range(0, slab, tile):
            there = pl.ds(pl.multiple_of(offs_ref[place] * slab + col, tile), tile)
            part = None
            for at in range(len(bands) // GROUP):
                group = bands[at * GROUP : (at + 1) * GROUP]
                more = jnp.dot(
                    delta_ref[:, at * depth : (at + 1) * depth],
                    jnp.concatenate([ref[:, there] for ref in group], axis=0),
                    preferred_element_type=jnp.float32,
                )
                part = more if part is None else part + more
            out_ref[index, :, pl.ds(col, tile)] = part.astype(out_ref.dtype)


def sums_kernel(base, found, arrays, sent, kept, many, first, *refs):
    offs_ref, delta_ref, delta_t_ref = refs[:3]
    xs, bands = refs[3 : 3 + arrays], refs[3 + arrays : 3 + arrays + many]
    refs = refs[3 + arrays + many + (0 if first else 1) :]
    copies = []
    if found:
        out_ref, held, sems = refs[-3:]
        views = [xs[at].at[index] for at, index in found]
        copies = grad_w_part(base, offs_ref, delta_t_ref, views, out_ref, held, sems)
    if sent:
        share_part(sent, offs_ref, delta_ref, bands, refs[0])
    if kept:
        share_part(kept, offs_ref, delta_ref, bands, refs[1])
    for copy in copies:
        copy.wait()


def sums(offs, base, pieces, sent, kept, delta, delta_t, bands, slab, so_far, shape):
    nodes, rows = delta.shape
    arrays, found = split_pieces(pieces)
    first = so_far is None
    tile = rows // 2
    shapes, scratch = [], []
    if sent:
        shapes.append(jax.ShapeDtypeStruct((len(sent), nodes, slab), jnp.bfloat16))
    if kept:
        shapes.append(jax.ShapeDtypeStruct((len(kept), nodes, slab), jnp.float32))
    specs = [VMEM_REF] * len(shapes)
    if found:
        shapes, specs = shapes + [jax.ShapeDtypeStruct(shape, jnp.bfloat16)], specs + [ANY_REF]
        scratch = [pltpu.VMEM((4, tile, slab), jnp.bfloat16), pltpu.SemaphoreType.DMA((4,))]
    operands = [offs, delta, delta_t, *arrays, *bands] + ([] if first else [so_far])
    outs = call(
        functools.partial(
            sums_kernel, base, found, len(arrays), sent, kept, len(bands), first
        ),
        shapes,
        specs,
        scratch,
        cost(len(found) + len(sent) + len(kept), nodes, slab, rows),
        {} if first else {len(operands) - 1: len(shapes) - 1},
    )(
        operands,
        [SMEM_REF] + [VMEM_REF] * (2 + len(arrays) + len(bands))
        + ([] if first else [ANY_REF]),
    )
    others, owns = outs[0] if sent else None, outs[1] if kept else None
    return others, owns, outs[-1] if found else so_far


def ring_body(chips, states, weights, pert_table, eps_gain, decay, perts):
    _, nodes, slab = states.shape
    rows = weights.shape[0]
    order = chip_ring(chips)
    place = np.argsort(order)
    half = chips // 2

    listing = [(0, 0), (0, 1)]
    for step in range(1, half):
        listing += [(step, 0), (step, 1), (-step, 1), (-step, 0)]
    listing += [(half, 0), (half, 1)]
    sides = {key: at for at, key in enumerate(listing)}
    table = np.array(
        [
            [
                2 * order[(place[device // 2] + (step if device % 2 else -step)) % chips]
                + (device % 2 ^ side)
                for step, side in listing
            ]
            for device in range(2 * chips)
        ],
        dtype=np.int32,
    )
    me = lax.axis_index("row")
    offs = lax.dynamic_slice(jnp.asarray(table), (me, 0), (1, 2 * chips)).reshape(-1)

    def passed(array, way=1, cross=0):
        pairs = []
        for at, chip in enumerate(order):
            pairs.append((2 * chip, 2 * order[(at + way) % chips] + cross))
            pairs.append((2 * chip + 1, 2 * order[(at - way) % chips] + 1 - cross))
        return lax.ppermute(array, "row", pairs)

    def swap(array):
        return lax.ppermute(array, "row", [(i, i ^ 1) for i in range(2 * chips)])

    gate = lax.optimization_barrier
    weights = pltpu.with_memory_space_constraint(weights, pltpu.HBM)
    cheb = cheb_matrix(nodes)
    flat = states.reshape(nodes, slab)
    xb = states.astype(jnp.bfloat16)

    near, over = passed(xb), passed(xb, -1, 1)
    other = swap(xb)
    mark, bands = load_first(offs, perts, weights, LOADS[0])
    near, over, other, mark = gate((near, over, other, mark))
    x = {(0, 0): (xb, 0), (0, 1): (other, 0)}
    flow = jnp.concatenate([near, over], axis=0)
    acc, seen = mark, 0
    for step in range(1, half + 1):
        if step < half:
            x[step, 0], x[step, 1] = (flow, 0), (flow, 1)
            other = flow
        else:
            x[half, 0], other = (flow, 0), flow
        if step < half:
            flow = passed(flow if step < half - 1 else flow[:1])
        other = swap(other)
        if step < half:
            x[-step, 1], x[-step, 0] = (other, 0), (other, 1)
        else:
            x[half, 1] = (other, 0)
        count = 1 if step == half else 6 if step == half - 1 else 4
        fresh = [LOADS[0], LOADS[1], 0][min(step, 3) - 1]
        late = [LOADS[1], LOADS[2], 0][min(step, 3) - 1]
        acc, bands = add_products(
            offs, weights, acc, bands, [x[key] for key in listing[: seen + count]], count,
            fresh, late, step == 2,
        )
        seen += count
        if step == half - 2:
            derivs = derivatives(perts, cheb, flat, pert_table)
            acc, *derivs = gate((acc, *derivs))
        if step < half:
            flow, acc = gate((flow, acc))

    decay = decay.reshape(1, rows)
    resid, delta, delta_t, grad_table, grad_eps, grad_decay = middle(
        offs, seen, x[half, 1][0], bands, acc, derivs, flat, eps_gain.reshape(1, rows), decay
    )

    grad_w, base = None, 0

    def sent(step):
        return [sides[step, 1]] if step in (0, half) else [sides[step, 1], sides[step, 0]]

    def kept(step):
        return [sides[step, 0]] if step in (0, half) else [sides[-step, 0], sides[-step, 1]]

    def work(offs, count, sent, kept, grad_w, base):
        others, owns, grad_w = sums(
            offs, base, [x[key] for key in listing[base : base + count]], sent, kept,
            delta, delta_t, bands, slab, grad_w, weights.shape,
        )
        return others, owns, grad_w, base + count

    def joined(others, owns):
        return owns + swap(others).astype(jnp.float32)

    counts = list(PIECES)
    others, owns, _, _ = work(offs, 0, sent(half), kept(half), None, 0)
    far = joined(others, owns).astype(jnp.bfloat16)
    others, _, _, _ = work(offs, 0, sent(half - 1), [], None, 0)
    far, offs, others = gate((far, offs, others))
    ready, flow = swap(others), passed(far)
    for step in range(half - 1, 0, -1):
        late = kept(step) if step == half - 1 else []
        others, owns, grad_w, base = work(
            offs, counts.pop(0), sent(step - 1), late + kept(step - 1), grad_w, base
        )
        flow, owns = gate((flow, owns))
        flow = flow.astype(jnp.float32)
        if late:
            share, owns = owns[:2] + ready.astype(jnp.float32), owns[2:]
            total = jnp.concatenate([share[:1] + flow, share[1:]], axis=0)
        else:
            total = share + flow
        total = total.astype(jnp.bfloat16)
        share = joined(others, owns)
        total, offs = gate((total, offs))
        if step > 1:
            flow = passed(total)
        else:
            near, over = passed(total[:1]), passed(total[1:], 1, 1)
    _, _, grad_w, base = work(offs, len(listing) - base, [], [], grad_w, base)
    local = local_terms(cheb, resid, decay)
    near, over, local = gate((near, over, local))
    grad_x = local + share[0] + near[0].astype(jnp.float32) + over[0].astype(jnp.float32)
    grad_x = grad_x.reshape(states.shape)
    return (grad_w, grad_x, grad_table, grad_eps.reshape(rows), grad_decay.reshape(rows))


def plain_body(states, weights, pert_table, eps_gain, decay, perts):
    traj, nodes, slab = states.shape
    total = traj * nodes
    cheb = cheb_matrix(nodes)
    xb = states.astype(jnp.bfloat16).reshape(total, slab)
    full = lax.all_gather(xb, "row", axis=1, tiled=True)
    pre = lax.dot_general(
        full, weights, (((1,), (1,)), ((), ())), preferred_element_type=jnp.float32
    )
    onehot = (perts[:, None] == jnp.arange(pert_table.shape[0], dtype=jnp.int32)[None, :]).astype(
        jnp.float32
    )
    drive = jnp.dot(onehot, pert_table, precision=lax.Precision.HIGHEST)
    act = jnp.tanh(pre.reshape(traj, nodes, slab) + drive[:, None, :])
    deriv = SCALE * jnp.einsum("kl,clg->ckg", cheb, states, precision=lax.Precision.HIGHEST)
    resid = deriv - (eps_gain * act - decay * states)
    delta = (-eps_gain * (1.0 - act * act) * resid).astype(jnp.bfloat16)
    dflat = delta.reshape(total, slab)
    grad_w = lax.dot_general(
        dflat, full, (((0,), (0,)), ((), ())), preferred_element_type=jnp.float32
    ).astype(jnp.bfloat16)
    back = jnp.dot(dflat, weights, preferred_element_type=jnp.float32)
    back = lax.psum_scatter(back, "row", scatter_dimension=1, tiled=True)
    grad_x = (
        SCALE * jnp.einsum("lk,clg->ckg", cheb, resid, precision=lax.Precision.HIGHEST)
        + decay * resid
        + back.reshape(traj, nodes, slab)
    )
    node_sums = jnp.sum(delta.astype(jnp.float32), axis=1)
    grad_table = jnp.dot(onehot.T, node_sums, precision=lax.Precision.HIGHEST)
    grad_eps = -jnp.sum(act * resid, axis=(0, 1))
    grad_decay = jnp.sum(states * resid, axis=(0, 1))
    return (grad_w, grad_x, grad_table, grad_eps, grad_decay)


def solution(mesh):
    chips = mesh.shape["row"] // 2
    in_specs = (
        P("rep", None, "row"),
        P(("rep", "row"), None),
        P("rep", "row"),
        P(("rep", "row")),
        P(("rep", "row")),
        P("rep"),
    )
    out_specs = (
        P(("rep", "row"), None),
        P("rep", None, "row"),
        P("rep", "row"),
        P(("rep", "row")),
        P(("rep", "row")),
    )

    def run(states, *others):
        if states.shape[0] == 1 and chips // 2 == len(PIECES) + 1:
            return ring_body(chips, states, *others)
        return plain_body(states, *others)

    return jax.shard_map(run, mesh=mesh, in_specs=in_specs, out_specs=out_specs, check_vma=False)
```

```python
import functools

import jax
import jax.numpy as jnp
import numpy as np
from jax import lax
from jax.experimental import pallas as pl
from jax.experimental.pallas import tpu as pltpu
from jax.sharding import PartitionSpec as P

SCALE = 2.0 / 1024.0
VMEM_LIMIT = 8 * 2**20
BANDS = 16
GROUP = 4
LOADS = (7, 6, 3)
PIECES = (2, 5, 6)


def cheb_matrix(count):
    index = np.arange(count)
    points = np.cos(np.pi * index / (count - 1))
    signs = np.where(index % 2 == 0, 1.0, -1.0)
    weight_c = signs * np.where((index == 0) | (index == count - 1), 2.0, 1.0)
    same = index[:, None] == index[None, :]
    spread = np.where(same, 1.0, points[:, None] - points[None, :])
    off = np.where(same, 0.0, weight_c[:, None] / weight_c[None, :] / spread)
    return jnp.asarray((off - np.diag(np.sum(off, axis=1))).astype(np.float32))


def chip_ring(chips):
    rows = 4
    cols = chips // rows
    cells = [(0, col) for col in range(cols)]
    for row in range(1, rows):
        span = range(1, cols)
        cells += [(row, col) for col in (reversed(span) if row % 2 else span)]
    cells += [(row, 0) for row in range(rows - 1, 0, -1)]
    return [row * cols + col for row, col in cells]


VMEM_REF = pl.BlockSpec(memory_space=pltpu.VMEM)
SMEM_REF = pl.BlockSpec(memory_space=pltpu.SMEM)
ANY_REF = pl.BlockSpec(memory_space=pl.ANY)
HBM_REF = pl.BlockSpec(memory_space=pltpu.HBM)


def cost(products, nodes, slab, rows):
    return pl.CostEstimate(
        flops=2 * products * nodes * slab * rows // 16,
        bytes_accessed=2 * products * slab * rows // 16,
        transcendentals=0,
    )


def call(kernel, out_shape, out_specs, scratch, costs, aliases=None):
    def run(operands, in_specs):
        return pl.pallas_call(
            kernel,
            out_shape=out_shape,
            in_specs=in_specs,
            out_specs=out_specs,
            scratch_shapes=scratch,
            input_output_aliases=aliases or {},
            compiler_params=pltpu.CompilerParams(vmem_limit_bytes=VMEM_LIMIT),
            cost_estimate=costs,
        )(*operands)

    return run


def columns_of(offs_ref, at, slab):
    return pl.ds(pl.multiple_of(offs_ref[at] * slab, slab), slab)


def load_bands(w_ref, bands, sems, first):
    copies = []
    for at, band_ref in enumerate(bands):
        tile = band_ref.shape[0]
        rows = pl.ds((first + at) * tile, tile)
        copies.append(pltpu.make_async_copy(w_ref.at[rows, :], band_ref, sems.at[at]))
        copies[-1].start()
    return copies


def product(bands, here, x_ref):
    return lax.dot_general(
        jnp.concatenate([band_ref[:, here] for band_ref in bands], axis=0), x_ref[...],
        (((1,), (1,)), ((), ())), preferred_element_type=jnp.float32,
    )


def split_pieces(pieces):
    arrays, found = [], []
    for array, index in pieces:
        at = [place for place, other in enumerate(arrays) if other is array]
        if not at:
            arrays.append(array)
        found.append((at[0] if at else len(arrays) - 1, index))
    return arrays, found


def load_kernel(offs_ref, perts_ref, w_ref, mark_ref, *refs):
    mark_ref[...] = jnp.zeros_like(mark_ref)
    for copy in load_bands(w_ref, refs[:-1], refs[-1], 0):
        copy.wait()


def band_shapes(count, weights):
    return [pltpu.VMEM((weights.shape[0] // BANDS, weights.shape[1]), weights.dtype)] * count


def load_first(offs, perts, weights, count):
    mark, *bands = call(
        load_kernel,
        [jax.ShapeDtypeStruct((8, 128), jnp.float32)] + band_shapes(count, weights),
        [VMEM_REF] * (1 + count),
        [pltpu.SemaphoreType.DMA((count,))],
        cost(1, 128, 128, 1024),
    )([offs, perts, weights], [SMEM_REF, SMEM_REF, HBM_REF])
    return mark, bands


def pre_kernel(found, count, many, fresh, late, ripe, offs_ref, acc_ref, *refs):
    if late:
        w_ref, refs = refs[0], refs[1:]
    bands, refs = refs[:many], refs[many:]
    arrays = 1 + max(at for at, _ in found)
    xs, out_ref, others, sems = refs[:arrays], refs[arrays], refs[arrays + 1 : -1], refs[-1]
    slab = xs[0].shape[-1]
    tile = out_ref.shape[0] // BANDS
    copies = load_bands(w_ref, others, sems, many) if late else []
    rest = fresh % GROUP if ripe else 0
    for low in [*range(0, many - fresh, GROUP), *range(many - fresh, many - rest, GROUP)]:
        old = low < many - fresh
        group = bands[low : min(low + GROUP, many - fresh if old else many - rest)]
        rows = pl.ds(low * tile, len(group) * tile)
        total = acc_ref[rows, :] if old else None
        for place in range(len(found) - count if old else 0, len(found)):
            at, index = found[place]
            part = product(group, columns_of(offs_ref, place, slab), xs[at].at[index])
            total = part if total is None else total + part
        out_ref[rows, :] = total
    for copy in copies:
        copy.wait()
    if ripe:
        group, total = [*bands[many - rest :], *others], None
        for place, (at, index) in enumerate(found):
            part = product(group, columns_of(offs_ref, place, slab), xs[at].at[index])
            total = part if total is None else total + part
        out_ref[pl.ds((many - rest) * tile, len(group) * tile), :] = total


def add_products(offs, weights, acc, bands, pieces, count, fresh, late, ripe):
    arrays, found = split_pieces(pieces if fresh else pieces[-count:])
    if not fresh:
        found = [(0, 0)] * (len(pieces) - count) + found
    (_, nodes, slab), rows, many = arrays[0].shape, weights.shape[0], len(bands)
    operands = [offs, acc] + ([weights] if late else []) + [*bands, *arrays]
    acc, *others = call(
        functools.partial(pre_kernel, found, count, many, fresh, late, ripe),
        [jax.ShapeDtypeStruct((rows, nodes), jnp.float32)] + band_shapes(late, weights),
        [VMEM_REF] * (1 + late),
        [pltpu.SemaphoreType.DMA((max(late, 1),))],
        cost(count, nodes, slab, rows),
    )(
        operands,
        [SMEM_REF, VMEM_REF] + ([HBM_REF] if late else [])
        + [VMEM_REF] * (many + len(arrays)),
    )
    return acc, [*bands, *others]


def cheb_dot(turned, cheb_ref, array_ref):
    return SCALE * lax.dot_general(
        cheb_ref[...], array_ref[...], (((0 if turned else 1,), (0,)), ((), ())),
        precision=lax.Precision.HIGHEST, preferred_element_type=jnp.float32,
    )


def deriv_kernel(perts_ref, cheb_ref, states_ref, pert_ref, deriv_ref, drive_ref, chosen_ref):
    pert = perts_ref[0]
    deriv_ref[...] = cheb_dot(False, cheb_ref, states_ref)
    drive_ref[...] = pert_ref[pl.ds(pert, 1), :]
    rows = lax.broadcasted_iota(jnp.int32, chosen_ref.shape, 0)
    chosen_ref[...] = (rows == pert).astype(jnp.float32)


def derivatives(perts, cheb, states, pert_table):
    return call(
        deriv_kernel,
        [
            jax.ShapeDtypeStruct(states.shape, jnp.float32),
            jax.ShapeDtypeStruct((1, states.shape[1]), jnp.float32),
            jax.ShapeDtypeStruct(pert_table.shape, jnp.float32),
        ],
        [VMEM_REF] * 3,
        [],
        cost(1, *states.shape, states.shape[0]),
    )([perts, cheb, states, pert_table], [SMEM_REF] + [VMEM_REF] * 3)


def local_kernel(cheb_ref, resid_ref, decay_ref, out_ref):
    out_ref[...] = cheb_dot(True, cheb_ref, resid_ref) + decay_ref[...] * resid_ref[...]


def local_terms(cheb, resid, decay):
    return call(
        local_kernel,
        jax.ShapeDtypeStruct(resid.shape, jnp.float32),
        VMEM_REF,
        [],
        cost(1, *resid.shape, resid.shape[0]),
    )([cheb, resid, decay], [VMEM_REF] * 3)


def middle_kernel(base, sent, many, offs_ref, x_ref, *refs):
    bands = refs[:many]
    acc_ref, deriv_ref, drive_ref, chosen_ref, states_ref, eps_ref, decay_ref = refs[many:-7]
    resid_ref, delta_ref, delta_t_ref, table_ref, sum_eps_ref, sum_decay_ref = refs[-7:-1]
    tile = GROUP * bands[0].shape[0]
    here = columns_of(offs_ref, base, x_ref.shape[-1])
    for at in range(many // GROUP):
        band = pl.ds(at * tile, tile)
        part = acc_ref[band, :] + product(bands[at * GROUP : (at + 1) * GROUP], here, x_ref.at[0])
        states = states_ref[:, band]
        act = jnp.tanh(part.T + drive_ref[:, band])
        eps = eps_ref[:, band]
        resid = deriv_ref[:, band] - (eps * act - decay_ref[:, band] * states)
        delta = (-eps * (1.0 - act * act) * resid).astype(jnp.bfloat16)
        wide = delta.astype(jnp.float32)
        resid_ref[:, band] = resid
        delta_ref[:, band] = delta
        delta_t_ref[band, :] = wide.T.astype(jnp.bfloat16)
        table_ref[:, band] = chosen_ref[:, band] * jnp.sum(wide, axis=0, keepdims=True)
        sum_eps_ref[:, band] = -jnp.sum(act * resid, axis=0, keepdims=True)
        sum_decay_ref[:, band] = jnp.sum(states * resid, axis=0, keepdims=True)
    share_part(sent, offs_ref, delta_ref, bands, refs[-1])


def middle(offs, base, sent, x, bands, acc, derivs, states, eps, decay):
    _, nodes, slab = x.shape
    rows = acc.shape[0]
    wide = functools.partial(jax.ShapeDtypeStruct, dtype=jnp.float32)
    return call(
        functools.partial(middle_kernel, base, sent, len(bands)),
        [
            wide((nodes, rows)),
            jax.ShapeDtypeStruct((nodes, rows), jnp.bfloat16),
            jax.ShapeDtypeStruct((rows, nodes), jnp.bfloat16),
            wide(derivs[2].shape),
            wide((1, rows)),
            wide((1, rows)),
            jax.ShapeDtypeStruct((len(sent), nodes, slab), jnp.bfloat16),
        ],
        [VMEM_REF] * 7,
        [],
        cost(2, nodes, slab, rows),
    )(
        [offs, x, *bands, acc, *derivs, states, eps, decay],
        [SMEM_REF] + [VMEM_REF] * (8 + len(bands)),
    )


def grad_w_part(base, offs_ref, delta_t_ref, xs, out_ref, held, sems):
    rows, slab = delta_t_ref.shape[0], held.shape[2]
    slots, tile = held.shape[:2]
    step = min(256, slab)
    copies = []
    for at, x_ref in enumerate(xs):
        for start in range(0, rows, tile):
            slot, band = len(copies) % slots, pl.ds(start, tile)
            if len(copies) >= slots:
                copies[-slots].wait()
            for col in range(0, slab, step):
                held[slot, :, col : col + step] = jnp.dot(
                    delta_t_ref[band, :], x_ref[:, col : col + step],
                    preferred_element_type=jnp.float32,
                ).astype(held.dtype)
            there = columns_of(offs_ref, base + at, slab)
            copy = pltpu.make_async_copy(held.at[slot], out_ref.at[band, there], sems.at[slot])
            copy.start()
            copies.append(copy)
    return copies[-slots:]


def share_part(places, offs_ref, delta_ref, bands, out_ref):
    depth, slab = GROUP * bands[0].shape[0], out_ref.shape[2]
    tile = max(slab // 2, 128)
    for index, place in enumerate(places):
        for col in range(0, slab, tile):
            there = pl.ds(pl.multiple_of(offs_ref[place] * slab + col, tile), tile)
            part = None
            for at in range(len(bands) // GROUP):
                group = bands[at * GROUP : (at + 1) * GROUP]
                more = jnp.dot(
                    delta_ref[:, at * depth : (at + 1) * depth],
                    jnp.concatenate([ref[:, there] for ref in group], axis=0),
                    preferred_element_type=jnp.float32,
                )
                part = more if part is None else part + more
            out_ref[index, :, pl.ds(col, tile)] = part.astype(out_ref.dtype)


def sums_kernel(base, found, arrays, sent, kept, many, first, *refs):
    offs_ref, delta_ref, delta_t_ref = refs[:3]
    xs, bands = refs[3 : 3 + arrays], refs[3 + arrays : 3 + arrays + many]
    refs = refs[3 + arrays + many + (0 if first else 1) :]
    copies = []
    if found:
        out_ref, held, sems = refs[-3:]
        views = [xs[at].at[index] for at, index in found]
        copies = grad_w_part(base, offs_ref, delta_t_ref, views, out_ref, held, sems)
    if sent:
        share_part(sent, offs_ref, delta_ref, bands, refs[0])
    if kept:
        share_part(kept, offs_ref, delta_ref, bands, refs[1])
    for copy in copies:
        copy.wait()


def sums(offs, base, pieces, sent, kept, delta, delta_t, bands, slab, so_far, shape):
    nodes, rows = delta.shape
    arrays, found = split_pieces(pieces)
    first = so_far is None
    tile = rows // 2
    shapes, scratch = [], []
    if sent:
        shapes.append(jax.ShapeDtypeStruct((len(sent), nodes, slab), jnp.bfloat16))
    if kept:
        shapes.append(jax.ShapeDtypeStruct((len(kept), nodes, slab), jnp.float32))
    specs = [VMEM_REF] * len(shapes)
    if found:
        shapes, specs = shapes + [jax.ShapeDtypeStruct(shape, jnp.bfloat16)], specs + [ANY_REF]
        scratch = [pltpu.VMEM((4, tile, slab), jnp.bfloat16), pltpu.SemaphoreType.DMA((4,))]
    operands = [offs, delta, delta_t, *arrays, *bands] + ([] if first else [so_far])
    outs = call(
        functools.partial(
            sums_kernel, base, found, len(arrays), sent, kept, len(bands), first
        ),
        shapes,
        specs,
        scratch,
        cost(len(found) + len(sent) + len(kept), nodes, slab, rows),
        {} if first else {len(operands) - 1: len(shapes) - 1},
    )(
        operands,
        [SMEM_REF] + [VMEM_REF] * (2 + len(arrays) + len(bands))
        + ([] if first else [ANY_REF]),
    )
    others, owns = outs[0] if sent else None, outs[1] if kept else None
    return others, owns, outs[-1] if found else so_far


def ring_body(chips, states, weights, pert_table, eps_gain, decay, perts):
    _, nodes, slab = states.shape
    rows = weights.shape[0]
    order = chip_ring(chips)
    place = np.argsort(order)
    half = chips // 2

    listing = [(0, 0), (0, 1)]
    for step in range(1, half):
        listing += [(step, 0), (step, 1), (-step, 1), (-step, 0)]
    listing += [(half, 0), (half, 1)]
    sides = {key: at for at, key in enumerate(listing)}
    table = np.array(
        [
            [
                2 * order[(place[device // 2] + (step if device % 2 else -step)) % chips]
                + (device % 2 ^ side)
                for step, side in listing
            ]
            for device in range(2 * chips)
        ],
        dtype=np.int32,
    )
    me = lax.axis_index("row")
    offs = lax.dynamic_slice(jnp.asarray(table), (me, 0), (1, 2 * chips)).reshape(-1)

    def passed(array, way=1, cross=0):
        pairs = []
        for at, chip in enumerate(order):
            pairs.append((2 * chip, 2 * order[(at + way) % chips] + cross))
            pairs.append((2 * chip + 1, 2 * order[(at - way) % chips] + 1 - cross))
        return lax.ppermute(array, "row", pairs)

    def swap(array):
        return lax.ppermute(array, "row", [(i, i ^ 1) for i in range(2 * chips)])

    gate = lax.optimization_barrier
    weights = pltpu.with_memory_space_constraint(weights, pltpu.HBM)
    cheb = cheb_matrix(nodes)
    flat = states.reshape(nodes, slab)
    xb = states.astype(jnp.bfloat16)

    near, over = passed(xb), passed(xb, -1, 1)
    other = swap(xb)
    mark, bands = load_first(offs, perts, weights, LOADS[0])
    near, over, other, mark = gate((near, over, other, mark))
    x = {(0, 0): (xb, 0), (0, 1): (other, 0)}
    flow = jnp.concatenate([near, over], axis=0)
    acc, seen = mark, 0
    for step in range(1, half + 1):
        if step < half:
            x[step, 0], x[step, 1] = (flow, 0), (flow, 1)
            other = flow
        else:
            x[half, 0], other = (flow, 0), flow
        if step < half:
            flow = passed(flow if step < half - 1 else flow[:1])
        other = swap(other)
        if step < half:
            x[-step, 1], x[-step, 0] = (other, 0), (other, 1)
        else:
            x[half, 1] = (other, 0)
        count = 1 if step == half else 6 if step == half - 1 else 4
        fresh = [LOADS[0], LOADS[1], 0][min(step, 3) - 1]
        late = [LOADS[1], LOADS[2], 0][min(step, 3) - 1]
        acc, bands = add_products(
            offs, weights, acc, bands, [x[key] for key in listing[: seen + count]], count,
            fresh, late, step == 2,
        )
        seen += count
        if step == half - 2:
            derivs = derivatives(perts, cheb, flat, pert_table)
            acc, *derivs = gate((acc, *derivs))
        if step < half:
            flow, acc = gate((flow, acc))

    decay = decay.reshape(1, rows)
    resid, delta, delta_t, grad_table, grad_eps, grad_decay, others = middle(
        offs, seen, [sides[half, 1]], x[half, 1][0], bands, acc, derivs, flat,
        eps_gain.reshape(1, rows), decay,
    )

    grad_w, base = None, 0

    def sent(step):
        return [sides[step, 1]] if step in (0, half) else [sides[step, 1], sides[step, 0]]

    def kept(step):
        return [sides[step, 0]] if step in (0, half) else [sides[-step, 0], sides[-step, 1]]

    def work(offs, count, sent, kept, grad_w, base):
        others, owns, grad_w = sums(
            offs, base, [x[key] for key in listing[base : base + count]], sent, kept,
            delta, delta_t, bands, slab, grad_w, weights.shape,
        )
        return others, owns, grad_w, base + count

    def joined(others, owns):
        return owns + swap(others).astype(jnp.float32)

    counts = list(PIECES)
    others, offs = gate((others, offs))
    far = swap(others)
    others, owns, _, _ = work(offs, 0, sent(half - 1), kept(half), None, 0)
    far = (owns + far.astype(jnp.float32)).astype(jnp.bfloat16)
    far, offs, others = gate((far, offs, others))
    ready, flow = swap(others), passed(far)
    for step in range(half - 1, 0, -1):
        late = kept(step) if step == half - 1 else []
        others, owns, grad_w, base = work(
            offs, counts.pop(0), sent(step - 1), late + kept(step - 1), grad_w, base
        )
        if late:
            local = local_terms(cheb, resid, decay)
            owns, local = gate((owns, local))
        flow, owns = gate((flow, owns))
        flow = flow.astype(jnp.float32)
        if late:
            share, owns = owns[:2] + ready.astype(jnp.float32), owns[2:]
            total = jnp.concatenate([share[:1] + flow, share[1:]], axis=0)
        else:
            total = share + flow
        total = total.astype(jnp.bfloat16)
        share = joined(others, owns)
        total, offs = gate((total, offs))
        if step > 1:
            flow = passed(total)
        else:
            near, over = passed(total[:1]), passed(total[1:], 1, 1)
    _, _, grad_w, base = work(offs, len(listing) - base, [], [], grad_w, base)
    grad_x = local + share[0] + near[0].astype(jnp.float32) + over[0].astype(jnp.float32)
    grad_x = grad_x.reshape(states.shape)
    return (grad_w, grad_x, grad_table, grad_eps.reshape(rows), grad_decay.reshape(rows))


def plain_body(states, weights, pert_table, eps_gain, decay, perts):
    traj, nodes, slab = states.shape
    total = traj * nodes
    cheb = cheb_matrix(nodes)
    xb = states.astype(jnp.bfloat16).reshape(total, slab)
    full = lax.all_gather(xb, "row", axis=1, tiled=True)
    pre = lax.dot_general(
        full, weights, (((1,), (1,)), ((), ())), preferred_element_type=jnp.float32
    )
    onehot = (perts[:, None] == jnp.arange(pert_table.shape[0], dtype=jnp.int32)[None, :]).astype(
        jnp.float32
    )
    drive = jnp.dot(onehot, pert_table, precision=lax.Precision.HIGHEST)
    act = jnp.tanh(pre.reshape(traj, nodes, slab) + drive[:, None, :])
    deriv = SCALE * jnp.einsum("kl,clg->ckg", cheb, states, precision=lax.Precision.HIGHEST)
    resid = deriv - (eps_gain * act - decay * states)
    delta = (-eps_gain * (1.0 - act * act) * resid).astype(jnp.bfloat16)
    dflat = delta.reshape(total, slab)
    grad_w = lax.dot_general(
        dflat, full, (((0,), (0,)), ((), ())), preferred_element_type=jnp.float32
    ).astype(jnp.bfloat16)
    back = jnp.dot(dflat, weights, preferred_element_type=jnp.float32)
    back = lax.psum_scatter(back, "row", scatter_dimension=1, tiled=True)
    grad_x = (
        SCALE * jnp.einsum("lk,clg->ckg", cheb, resid, precision=lax.Precision.HIGHEST)
        + decay * resid
        + back.reshape(traj, nodes, slab)
    )
    node_sums = jnp.sum(delta.astype(jnp.float32), axis=1)
    grad_table = jnp.dot(onehot.T, node_sums, precision=lax.Precision.HIGHEST)
    grad_eps = -jnp.sum(act * resid, axis=(0, 1))
    grad_decay = jnp.sum(states * resid, axis=(0, 1))
    return (grad_w, grad_x, grad_table, grad_eps, grad_decay)


def solution(mesh):
    chips = mesh.shape["row"] // 2
    in_specs = (
        P("rep", None, "row"),
        P(("rep", "row"), None),
        P("rep", "row"),
        P(("rep", "row")),
        P(("rep", "row")),
        P("rep"),
    )
    out_specs = (
        P(("rep", "row"), None),
        P("rep", None, "row"),
        P("rep", "row"),
        P(("rep", "row")),
        P(("rep", "row")),
    )

    def run(states, *others):
        if states.shape[0] == 1 and chips // 2 == len(PIECES) + 1:
            return ring_body(chips, states, *others)
        return plain_body(states, *others)

    return jax.shard_map(run, mesh=mesh, in_specs=in_specs, out_specs=out_specs, check_vma=False)
```

```python
import functools

import jax
import jax.numpy as jnp
import numpy as np
from jax import lax
from jax.experimental import pallas as pl
from jax.experimental.pallas import tpu as pltpu
from jax.sharding import PartitionSpec as P

SCALE = 2.0 / 1024.0
VMEM_LIMIT = 8 * 2**20
BANDS = 16
GROUP = 4
LOADS = (8, 8)
PIECES = (2, 4, 5)


def cheb_matrix(count):
    index = np.arange(count)
    points = np.cos(np.pi * index / (count - 1))
    signs = np.where(index % 2 == 0, 1.0, -1.0)
    weight_c = signs * np.where((index == 0) | (index == count - 1), 2.0, 1.0)
    same = index[:, None] == index[None, :]
    spread = np.where(same, 1.0, points[:, None] - points[None, :])
    off = np.where(same, 0.0, weight_c[:, None] / weight_c[None, :] / spread)
    return jnp.asarray((off - np.diag(np.sum(off, axis=1))).astype(np.float32))


def chip_ring(chips):
    rows = 4
    cols = chips // rows
    cells = [(0, col) for col in range(cols)]
    for row in range(1, rows):
        span = range(1, cols)
        cells += [(row, col) for col in (reversed(span) if row % 2 else span)]
    cells += [(row, 0) for row in range(rows - 1, 0, -1)]
    return [row * cols + col for row, col in cells]


VMEM_REF = pl.BlockSpec(memory_space=pltpu.VMEM)
SMEM_REF = pl.BlockSpec(memory_space=pltpu.SMEM)
ANY_REF = pl.BlockSpec(memory_space=pl.ANY)
HBM_REF = pl.BlockSpec(memory_space=pltpu.HBM)


def cost(products, nodes, slab, rows):
    return pl.CostEstimate(
        flops=2 * products * nodes * slab * rows // 16,
        bytes_accessed=2 * products * slab * rows // 16,
        transcendentals=0,
    )


def call(kernel, out_shape, out_specs, scratch, costs, aliases=None):
    def run(operands, in_specs):
        return pl.pallas_call(
            kernel,
            out_shape=out_shape,
            in_specs=in_specs,
            out_specs=out_specs,
            scratch_shapes=scratch,
            input_output_aliases=aliases or {},
            compiler_params=pltpu.CompilerParams(vmem_limit_bytes=VMEM_LIMIT),
            cost_estimate=costs,
        )(*operands)

    return run


def columns_of(offs_ref, at, slab):
    return pl.ds(pl.multiple_of(offs_ref[at] * slab, slab), slab)


def band_copies(w_ref, bands, sems, first):
    copies = []
    for at, band_ref in enumerate(bands):
        tile = band_ref.shape[0]
        rows = pl.ds((first + at) * tile, tile)
        copies.append(pltpu.make_async_copy(w_ref.at[rows, :], band_ref, sems.at[at]))
    return copies


def product(bands, here, x_ref):
    return lax.dot_general(
        jnp.concatenate([band_ref[:, here] for band_ref in bands], axis=0), x_ref[...],
        (((1,), (1,)), ((), ())), preferred_element_type=jnp.float32,
    )


def split_pieces(pieces):
    arrays, found = [], []
    for array, index in pieces:
        at = [place for place, other in enumerate(arrays) if other is array]
        if not at:
            arrays.append(array)
        found.append((at[0] if at else len(arrays) - 1, index))
    return arrays, found


def load_kernel(offs_ref, perts_ref, w_ref, mark_ref, *refs):
    mark_ref[...] = jnp.zeros_like(mark_ref)
    copies = band_copies(w_ref, refs[:-1], refs[-1], 0)
    for copy in copies:
        copy.start()
    for copy in copies:
        copy.wait()


def band_shapes(count, weights):
    return [pltpu.VMEM((weights.shape[0] // BANDS, weights.shape[1]), weights.dtype)] * count


def load_first(offs, perts, weights, count):
    mark, *bands = call(
        load_kernel,
        [jax.ShapeDtypeStruct((8, 128), jnp.float32)] + band_shapes(count, weights),
        [VMEM_REF] * (1 + count),
        [pltpu.SemaphoreType.DMA((count,))],
        cost(1, 128, 128, 1024),
    )([offs, perts, weights], [SMEM_REF, SMEM_REF, HBM_REF])
    return mark, bands


def pre_kernel(found, count, many, fresh, late, offs_ref, acc_ref, *refs):
    if late:
        w_ref, refs = refs[0], refs[1:]
    bands, refs = refs[:many], refs[many:]
    arrays = 1 + max(at for at, _ in found)
    xs, out_ref, others, sems = refs[:arrays], refs[arrays], refs[arrays + 1 : -1], refs[-1]
    slab = xs[0].shape[-1]
    tile = out_ref.shape[0] // BANDS
    copies = band_copies(w_ref, others, sems, many) if late else []
    waiting = list(copies)
    for low in [*range(0, many - fresh, GROUP), *range(many - fresh, many, GROUP)]:
        old = low < many - fresh
        group = bands[low : min(low + GROUP, many - fresh if old else many)]
        rows = pl.ds(low * tile, len(group) * tile)
        total = acc_ref[rows, :] if old else None
        for place in range(len(found) - count if old else 0, len(found)):
            if waiting:
                waiting.pop(0).start()
            at, index = found[place]
            part = product(group, columns_of(offs_ref, place, slab), xs[at].at[index])
            total = part if total is None else total + part
        out_ref[rows, :] = total
    for copy in waiting:
        copy.start()
    for copy in copies:
        copy.wait()


def add_products(offs, weights, acc, bands, pieces, count, fresh, late):
    arrays, found = split_pieces(pieces if fresh else pieces[-count:])
    if not fresh:
        found = [(0, 0)] * (len(pieces) - count) + found
    (_, nodes, slab), rows, many = arrays[0].shape, weights.shape[0], len(bands)
    operands = [offs, acc] + ([weights] if late else []) + [*bands, *arrays]
    acc, *others = call(
        functools.partial(pre_kernel, found, count, many, fresh, late),
        [jax.ShapeDtypeStruct((rows, nodes), jnp.float32)] + band_shapes(late, weights),
        [VMEM_REF] * (1 + late),
        [pltpu.SemaphoreType.DMA((max(late, 1),))],
        cost(count, nodes, slab, rows),
    )(
        operands,
        [SMEM_REF, VMEM_REF] + ([HBM_REF] if late else [])
        + [VMEM_REF] * (many + len(arrays)),
    )
    return acc, [*bands, *others]


def cheb_dot(turned, cheb_ref, array_ref):
    return SCALE * lax.dot_general(
        cheb_ref[...], array_ref[...], (((0 if turned else 1,), (0,)), ((), ())),
        precision=lax.Precision.HIGHEST, preferred_element_type=jnp.float32,
    )


def deriv_kernel(perts_ref, cheb_ref, states_ref, pert_ref, deriv_ref, drive_ref, chosen_ref):
    pert = perts_ref[0]
    deriv_ref[...] = cheb_dot(False, cheb_ref, states_ref)
    drive_ref[...] = pert_ref[pl.ds(pert, 1), :]
    rows = lax.broadcasted_iota(jnp.int32, chosen_ref.shape, 0)
    chosen_ref[...] = (rows == pert).astype(jnp.float32)


def derivatives(perts, cheb, states, pert_table):
    return call(
        deriv_kernel,
        [
            jax.ShapeDtypeStruct(states.shape, jnp.float32),
            jax.ShapeDtypeStruct((1, states.shape[1]), jnp.float32),
            jax.ShapeDtypeStruct(pert_table.shape, jnp.float32),
        ],
        [VMEM_REF] * 3,
        [],
        cost(1, *states.shape, states.shape[0]),
    )([perts, cheb, states, pert_table], [SMEM_REF] + [VMEM_REF] * 3)


def local_kernel(cheb_ref, resid_ref, decay_ref, out_ref):
    out_ref[...] = cheb_dot(True, cheb_ref, resid_ref) + decay_ref[...] * resid_ref[...]


def local_terms(cheb, resid, decay):
    return call(
        local_kernel,
        jax.ShapeDtypeStruct(resid.shape, jnp.float32),
        VMEM_REF,
        [],
        cost(1, *resid.shape, resid.shape[0]),
    )([cheb, resid, decay], [VMEM_REF] * 3)


def middle_kernel(base, sent, many, offs_ref, x_ref, *refs):
    bands = refs[:many]
    acc_ref, deriv_ref, drive_ref, chosen_ref, states_ref, eps_ref, decay_ref = refs[many:-7]
    resid_ref, delta_ref, delta_t_ref, table_ref, sum_eps_ref, sum_decay_ref = refs[-7:-1]
    tile = GROUP * bands[0].shape[0]
    here = columns_of(offs_ref, base, x_ref.shape[-1])
    for at in range(many // GROUP):
        band = pl.ds(at * tile, tile)
        part = acc_ref[band, :] + product(bands[at * GROUP : (at + 1) * GROUP], here, x_ref.at[0])
        states = states_ref[:, band]
        act = jnp.tanh(part.T + drive_ref[:, band])
        eps = eps_ref[:, band]
        resid = deriv_ref[:, band] - (eps * act - decay_ref[:, band] * states)
        delta = (-eps * (1.0 - act * act) * resid).astype(jnp.bfloat16)
        wide = delta.astype(jnp.float32)
        resid_ref[:, band] = resid
        delta_ref[:, band] = delta
        delta_t_ref[band, :] = wide.T.astype(jnp.bfloat16)
        table_ref[:, band] = chosen_ref[:, band] * jnp.sum(wide, axis=0, keepdims=True)
        sum_eps_ref[:, band] = -jnp.sum(act * resid, axis=0, keepdims=True)
        sum_decay_ref[:, band] = jnp.sum(states * resid, axis=0, keepdims=True)
    share_part(sent, offs_ref, delta_ref, bands, refs[-1])


def middle(offs, base, sent, x, bands, acc, derivs, states, eps, decay):
    _, nodes, slab = x.shape
    rows = acc.shape[0]
    wide = functools.partial(jax.ShapeDtypeStruct, dtype=jnp.float32)
    return call(
        functools.partial(middle_kernel, base, sent, len(bands)),
        [
            wide((nodes, rows)),
            jax.ShapeDtypeStruct((nodes, rows), jnp.bfloat16),
            jax.ShapeDtypeStruct((rows, nodes), jnp.bfloat16),
            wide(derivs[2].shape),
            wide((1, rows)),
            wide((1, rows)),
            jax.ShapeDtypeStruct((len(sent), nodes, slab), jnp.bfloat16),
        ],
        [VMEM_REF] * 7,
        [],
        cost(2, nodes, slab, rows),
    )(
        [offs, x, *bands, acc, *derivs, states, eps, decay],
        [SMEM_REF] + [VMEM_REF] * (8 + len(bands)),
    )


def grad_w_part(base, offs_ref, delta_t_ref, xs, out_ref, held, sems):
    rows, slab = delta_t_ref.shape[0], held.shape[2]
    slots, tile = held.shape[:2]
    step = min(256, slab)
    copies = []
    for at, x_ref in enumerate(xs):
        for start in range(0, rows, tile):
            slot, band = len(copies) % slots, pl.ds(start, tile)
            if len(copies) >= slots:
                copies[-slots].wait()
            for col in range(0, slab, step):
                held[slot, :, col : col + step] = jnp.dot(
                    delta_t_ref[band, :], x_ref[:, col : col + step],
                    preferred_element_type=jnp.float32,
                ).astype(held.dtype)
            there = columns_of(offs_ref, base + at, slab)
            copy = pltpu.make_async_copy(held.at[slot], out_ref.at[band, there], sems.at[slot])
            copy.start()
            copies.append(copy)
    return copies[-slots:]


def share_part(places, offs_ref, delta_ref, bands, out_ref):
    depth, slab = GROUP * bands[0].shape[0], out_ref.shape[2]
    tile = max(slab // 2, 128)
    for index, place in enumerate(places):
        for col in range(0, slab, tile):
            there = pl.ds(pl.multiple_of(offs_ref[place] * slab + col, tile), tile)
            part = None
            for at in range(len(bands) // GROUP):
                group = bands[at * GROUP : (at + 1) * GROUP]
                more = jnp.dot(
                    delta_ref[:, at * depth : (at + 1) * depth],
                    jnp.concatenate([ref[:, there] for ref in group], axis=0),
                    preferred_element_type=jnp.float32,
                )
                part = more if part is None else part + more
            out_ref[index, :, pl.ds(col, tile)] = part.astype(out_ref.dtype)


def sums_kernel(base, found, arrays, sent, kept, many, first, *refs):
    offs_ref, delta_ref, delta_t_ref = refs[:3]
    xs, bands = refs[3 : 3 + arrays], refs[3 + arrays : 3 + arrays + many]
    refs = refs[3 + arrays + many + (0 if first else 1) :]
    copies = []
    if found:
        out_ref, held, sems = refs[-3:]
        views = [xs[at].at[index] for at, index in found]
        copies = grad_w_part(base, offs_ref, delta_t_ref, views, out_ref, held, sems)
    if sent:
        share_part(sent, offs_ref, delta_ref, bands, refs[0])
    if kept:
        share_part(kept, offs_ref, delta_ref, bands, refs[1])
    for copy in copies:
        copy.wait()


def sums(offs, base, pieces, sent, kept, delta, delta_t, bands, slab, so_far, shape):
    nodes, rows = delta.shape
    arrays, found = split_pieces(pieces)
    first = so_far is None
    tile = rows // 2
    shapes, scratch = [], []
    if sent:
        shapes.append(jax.ShapeDtypeStruct((len(sent), nodes, slab), jnp.bfloat16))
    if kept:
        shapes.append(jax.ShapeDtypeStruct((len(kept), nodes, slab), jnp.float32))
    specs = [VMEM_REF] * len(shapes)
    if found:
        shapes, specs = shapes + [jax.ShapeDtypeStruct(shape, jnp.bfloat16)], specs + [ANY_REF]
        scratch = [pltpu.VMEM((4, tile, slab), jnp.bfloat16), pltpu.SemaphoreType.DMA((4,))]
    operands = [offs, delta, delta_t, *arrays, *bands] + ([] if first else [so_far])
    outs = call(
        functools.partial(
            sums_kernel, base, found, len(arrays), sent, kept, len(bands), first
        ),
        shapes,
        specs,
        scratch,
        cost(len(found) + len(sent) + len(kept), nodes, slab, rows),
        {} if first else {len(operands) - 1: len(shapes) - 1},
    )(
        operands,
        [SMEM_REF] + [VMEM_REF] * (2 + len(arrays) + len(bands))
        + ([] if first else [ANY_REF]),
    )
    others, owns = outs[0] if sent else None, outs[1] if kept else None
    return others, owns, outs[-1] if found else so_far


def ring_body(chips, states, weights, pert_table, eps_gain, decay, perts):
    _, nodes, slab = states.shape
    rows = weights.shape[0]
    order = chip_ring(chips)
    place = np.argsort(order)
    half = chips // 2

    listing = [(0, 0), (0, 1)]
    for step in range(1, half):
        listing += [(step, 0), (step, 1), (-step, 1), (-step, 0)]
    listing += [(half, 0), (half, 1)]
    sides = {key: at for at, key in enumerate(listing)}
    table = np.array(
        [
            [
                2 * order[(place[device // 2] + (step if device % 2 else -step)) % chips]
                + (device % 2 ^ side)
                for step, side in listing
            ]
            for device in range(2 * chips)
        ],
        dtype=np.int32,
    )
    me = lax.axis_index("row")
    offs = lax.dynamic_slice(jnp.asarray(table), (me, 0), (1, 2 * chips)).reshape(-1)

    def passed(array, way=1, cross=0):
        pairs = []
        for at, chip in enumerate(order):
            pairs.append((2 * chip, 2 * order[(at + way) % chips] + cross))
            pairs.append((2 * chip + 1, 2 * order[(at - way) % chips] + 1 - cross))
        return lax.ppermute(array, "row", pairs)

    def swap(array):
        return lax.ppermute(array, "row", [(i, i ^ 1) for i in range(2 * chips)])

    gate = lax.optimization_barrier
    weights = pltpu.with_memory_space_constraint(weights, pltpu.HBM)
    cheb = cheb_matrix(nodes)
    flat = states.reshape(nodes, slab)
    xb = states.astype(jnp.bfloat16)

    near, over = passed(xb), passed(xb, -1, 1)
    other = swap(xb)
    mark, bands = load_first(offs, perts, weights, LOADS[0])
    near, over, other, mark = gate((near, over, other, mark))
    x = {(0, 0): (xb, 0), (0, 1): (other, 0)}
    flow = jnp.concatenate([near, over], axis=0)
    acc, seen = mark, 0
    for step in range(1, half + 1):
        if step < half:
            x[step, 0], x[step, 1] = (flow, 0), (flow, 1)
            other = flow
        else:
            x[half, 0], other = (flow, 0), flow
        if step < half:
            flow = passed(flow if step < half - 1 else flow[:1])
        other = swap(other)
        if step < half:
            x[-step, 1], x[-step, 0] = (other, 0), (other, 1)
        else:
            x[half, 1] = (other, 0)
        count = 1 if step == half else 6 if step == half - 1 else 4
        fresh = LOADS[step - 1] if step <= 2 else 0
        late = LOADS[1] if step == 1 else 0
        acc, bands = add_products(
            offs, weights, acc, bands, [x[key] for key in listing[: seen + count]], count,
            fresh, late,
        )
        seen += count
        if step == half - 2:
            derivs = derivatives(perts, cheb, flat, pert_table)
            acc, *derivs = gate((acc, *derivs))
        if step < half:
            flow, acc = gate((flow, acc))

    decay = decay.reshape(1, rows)
    resid, delta, delta_t, grad_table, grad_eps, grad_decay, others = middle(
        offs, seen, [sides[half, 1]], x[half, 1][0], bands, acc, derivs, flat,
        eps_gain.reshape(1, rows), decay,
    )

    grad_w, base = None, 0

    def sent(step):
        return [sides[step, 1]] if step in (0, half) else [sides[step, 1], sides[step, 0]]

    def kept(step):
        return [sides[step, 0]] if step in (0, half) else [sides[-step, 0], sides[-step, 1]]

    def work(offs, count, sent, kept, grad_w, base):
        others, owns, grad_w = sums(
            offs, base, [x[key] for key in listing[base : base + count]], sent, kept,
            delta, delta_t, bands, slab, grad_w, weights.shape,
        )
        return others, owns, grad_w, base + count

    def joined(others, owns):
        return owns + swap(others).astype(jnp.float32)

    counts = list(PIECES)
    others, offs = gate((others, offs))
    far = swap(others)
    others, owns, _, _ = work(offs, 0, sent(half - 1), kept(half), None, 0)
    far = (owns + far.astype(jnp.float32)).astype(jnp.bfloat16)
    far, offs, others = gate((far, offs, others))
    ready, flow = swap(others), passed(far)
    for step in range(half - 1, 0, -1):
        late = kept(step) if step == half - 1 else []
        others, owns, grad_w, base = work(
            offs, counts.pop(0), sent(step - 1), late + kept(step - 1), grad_w, base
        )
        if late:
            local = local_terms(cheb, resid, decay)
            owns, local = gate((owns, local))
        flow, owns = gate((flow, owns))
        flow = flow.astype(jnp.float32)
        if late:
            share, owns = owns[:2] + ready.astype(jnp.float32), owns[2:]
            total = jnp.concatenate([share[:1] + flow, share[1:]], axis=0)
        else:
            total = share + flow
        total = total.astype(jnp.bfloat16)
        share = joined(others, owns)
        total, offs = gate((total, offs))
        if step > 1:
            flow = passed(total)
        else:
            near, over = passed(total[:1]), passed(total[1:], 1, 1)
    _, _, grad_w, base = work(offs, len(listing) - base, [], [], grad_w, base)
    grad_x = local + share[0] + near[0].astype(jnp.float32) + over[0].astype(jnp.float32)
    grad_x = grad_x.reshape(states.shape)
    return (grad_w, grad_x, grad_table, grad_eps.reshape(rows), grad_decay.reshape(rows))


def plain_body(states, weights, pert_table, eps_gain, decay, perts):
    traj, nodes, slab = states.shape
    total = traj * nodes
    cheb = cheb_matrix(nodes)
    xb = states.astype(jnp.bfloat16).reshape(total, slab)
    full = lax.all_gather(xb, "row", axis=1, tiled=True)
    pre = lax.dot_general(
        full, weights, (((1,), (1,)), ((), ())), preferred_element_type=jnp.float32
    )
    onehot = (perts[:, None] == jnp.arange(pert_table.shape[0], dtype=jnp.int32)[None, :]).astype(
        jnp.float32
    )
    drive = jnp.dot(onehot, pert_table, precision=lax.Precision.HIGHEST)
    act = jnp.tanh(pre.reshape(traj, nodes, slab) + drive[:, None, :])
    deriv = SCALE * jnp.einsum("kl,clg->ckg", cheb, states, precision=lax.Precision.HIGHEST)
    resid = deriv - (eps_gain * act - decay * states)
    delta = (-eps_gain * (1.0 - act * act) * resid).astype(jnp.bfloat16)
    dflat = delta.reshape(total, slab)
    grad_w = lax.dot_general(
        dflat, full, (((0,), (0,)), ((), ())), preferred_element_type=jnp.float32
    ).astype(jnp.bfloat16)
    back = jnp.dot(dflat, weights, preferred_element_type=jnp.float32)
    back = lax.psum_scatter(back, "row", scatter_dimension=1, tiled=True)
    grad_x = (
        SCALE * jnp.einsum("lk,clg->ckg", cheb, resid, precision=lax.Precision.HIGHEST)
        + decay * resid
        + back.reshape(traj, nodes, slab)
    )
    node_sums = jnp.sum(delta.astype(jnp.float32), axis=1)
    grad_table = jnp.dot(onehot.T, node_sums, precision=lax.Precision.HIGHEST)
    grad_eps = -jnp.sum(act * resid, axis=(0, 1))
    grad_decay = jnp.sum(states * resid, axis=(0, 1))
    return (grad_w, grad_x, grad_table, grad_eps, grad_decay)


def solution(mesh):
    chips = mesh.shape["row"] // 2
    in_specs = (
        P("rep", None, "row"),
        P(("rep", "row"), None),
        P("rep", "row"),
        P(("rep", "row")),
        P(("rep", "row")),
        P("rep"),
    )
    out_specs = (
        P(("rep", "row"), None),
        P("rep", None, "row"),
        P("rep", "row"),
        P(("rep", "row")),
        P(("rep", "row")),
    )

    def run(states, *others):
        if states.shape[0] == 1 and chips // 2 == len(PIECES) + 1:
            return ring_body(chips, states, *others)
        return plain_body(states, *others)

    return jax.shard_map(run, mesh=mesh, in_specs=in_specs, out_specs=out_specs, check_vma=False)
```

```python
import functools

import jax
import jax.numpy as jnp
import numpy as np
from jax import lax
from jax.experimental import pallas as pl
from jax.experimental.pallas import tpu as pltpu
from jax.sharding import PartitionSpec as P

SCALE = 2.0 / 1024.0
VMEM_LIMIT = 8 * 2**20
BANDS = 16
GROUP = 4
LOADS = (8, 8)
COUNTS = (2, 6, 6, 1)
PIECES = (1, 5, 5)


def cheb_matrix(count):
    index = np.arange(count)
    points = np.cos(np.pi * index / (count - 1))
    signs = np.where(index % 2 == 0, 1.0, -1.0)
    weight_c = signs * np.where((index == 0) | (index == count - 1), 2.0, 1.0)
    same = index[:, None] == index[None, :]
    spread = np.where(same, 1.0, points[:, None] - points[None, :])
    off = np.where(same, 0.0, weight_c[:, None] / weight_c[None, :] / spread)
    return jnp.asarray((off - np.diag(np.sum(off, axis=1))).astype(np.float32))


def chip_ring(chips):
    rows = 4
    cols = chips // rows
    cells = [(0, col) for col in range(cols)]
    for row in range(1, rows):
        span = range(1, cols)
        cells += [(row, col) for col in (reversed(span) if row % 2 else span)]
    cells += [(row, 0) for row in range(rows - 1, 0, -1)]
    return [row * cols + col for row, col in cells]


VMEM_REF = pl.BlockSpec(memory_space=pltpu.VMEM)
SMEM_REF = pl.BlockSpec(memory_space=pltpu.SMEM)
ANY_REF = pl.BlockSpec(memory_space=pl.ANY)
HBM_REF = pl.BlockSpec(memory_space=pltpu.HBM)


def cost(products, nodes, slab, rows):
    return pl.CostEstimate(
        flops=2 * products * nodes * slab * rows // 16,
        bytes_accessed=2 * products * slab * rows // 16,
        transcendentals=0,
    )


def call(kernel, out_shape, out_specs, scratch, costs, aliases=None):
    def run(operands, in_specs):
        return pl.pallas_call(
            kernel,
            out_shape=out_shape,
            in_specs=in_specs,
            out_specs=out_specs,
            scratch_shapes=scratch,
            input_output_aliases=aliases or {},
            compiler_params=pltpu.CompilerParams(vmem_limit_bytes=VMEM_LIMIT),
            cost_estimate=costs,
        )(*operands)

    return run


def columns_of(offs_ref, at, slab):
    return pl.ds(pl.multiple_of(offs_ref[at] * slab, slab), slab)


def band_copies(w_ref, bands, sems, first):
    copies = []
    for at, band_ref in enumerate(bands):
        tile = band_ref.shape[0]
        rows = pl.ds((first + at) * tile, tile)
        copies.append(pltpu.make_async_copy(w_ref.at[rows, :], band_ref, sems.at[at]))
    return copies


def product(bands, here, x_ref):
    return lax.dot_general(
        jnp.concatenate([band_ref[:, here] for band_ref in bands], axis=0), x_ref[...],
        (((1,), (1,)), ((), ())), preferred_element_type=jnp.float32,
    )


def split_pieces(pieces):
    arrays, found = [], []
    for array, index in pieces:
        at = [place for place, other in enumerate(arrays) if other is array]
        if not at:
            arrays.append(array)
        found.append((at[0] if at else len(arrays) - 1, index))
    return arrays, found


def load_kernel(offs_ref, perts_ref, w_ref, mark_ref, *refs):
    mark_ref[...] = jnp.zeros_like(mark_ref)
    copies = band_copies(w_ref, refs[:-1], refs[-1], 0)
    for copy in copies:
        copy.start()
    for copy in copies:
        copy.wait()


def band_shapes(count, weights):
    return [pltpu.VMEM((weights.shape[0] // BANDS, weights.shape[1]), weights.dtype)] * count


def load_first(offs, perts, weights, count):
    mark, *bands = call(
        load_kernel,
        [jax.ShapeDtypeStruct((8, 128), jnp.float32)] + band_shapes(count, weights),
        [VMEM_REF] * (1 + count),
        [pltpu.SemaphoreType.DMA((count,))],
        cost(1, 128, 128, 1024),
    )([offs, perts, weights], [SMEM_REF, SMEM_REF, HBM_REF])
    return mark, bands


def pre_kernel(found, count, many, fresh, late, offs_ref, acc_ref, *refs):
    if late:
        w_ref, refs = refs[0], refs[1:]
    bands, refs = refs[:many], refs[many:]
    arrays = 1 + max(at for at, _ in found)
    xs, out_ref, others, sems = refs[:arrays], refs[arrays], refs[arrays + 1 : -1], refs[-1]
    slab = xs[0].shape[-1]
    tile = out_ref.shape[0] // BANDS
    copies = band_copies(w_ref, others, sems, many) if late else []
    waiting = list(copies)
    for low in [*range(0, many - fresh, GROUP), *range(many - fresh, many, GROUP)]:
        old = low < many - fresh
        group = bands[low : min(low + GROUP, many - fresh if old else many)]
        rows = pl.ds(low * tile, len(group) * tile)
        total = acc_ref[rows, :] if old else None
        for place in range(len(found) - count if old else 0, len(found)):
            if waiting:
                waiting.pop(0).start()
            at, index = found[place]
            part = product(group, columns_of(offs_ref, place, slab), xs[at].at[index])
            total = part if total is None else total + part
        out_ref[rows, :] = total
    for copy in waiting:
        copy.start()
    for copy in copies:
        copy.wait()


def add_products(offs, weights, acc, bands, pieces, count, fresh, late):
    arrays, found = split_pieces(pieces if fresh else pieces[-count:])
    if not fresh:
        found = [(0, 0)] * (len(pieces) - count) + found
    (_, nodes, slab), rows, many = arrays[0].shape, weights.shape[0], len(bands)
    operands = [offs, acc] + ([weights] if late else []) + [*bands, *arrays]
    acc, *others = call(
        functools.partial(pre_kernel, found, count, many, fresh, late),
        [jax.ShapeDtypeStruct((rows, nodes), jnp.float32)] + band_shapes(late, weights),
        [VMEM_REF] * (1 + late),
        [pltpu.SemaphoreType.DMA((max(late, 1),))],
        cost(count, nodes, slab, rows),
    )(
        operands,
        [SMEM_REF, VMEM_REF] + ([HBM_REF] if late else [])
        + [VMEM_REF] * (many + len(arrays)),
    )
    return acc, [*bands, *others]


def cheb_dot(turned, cheb_ref, array_ref):
    return SCALE * lax.dot_general(
        cheb_ref[...], array_ref[...], (((0 if turned else 1,), (0,)), ((), ())),
        precision=lax.Precision.HIGHEST, preferred_element_type=jnp.float32,
    )


def deriv_kernel(perts_ref, cheb_ref, states_ref, pert_ref, deriv_ref, drive_ref, chosen_ref):
    pert = perts_ref[0]
    deriv_ref[...] = cheb_dot(False, cheb_ref, states_ref)
    drive_ref[...] = pert_ref[pl.ds(pert, 1), :]
    rows = lax.broadcasted_iota(jnp.int32, chosen_ref.shape, 0)
    chosen_ref[...] = (rows == pert).astype(jnp.float32)


def derivatives(perts, cheb, states, pert_table):
    return call(
        deriv_kernel,
        [
            jax.ShapeDtypeStruct(states.shape, jnp.float32),
            jax.ShapeDtypeStruct((1, states.shape[1]), jnp.float32),
            jax.ShapeDtypeStruct(pert_table.shape, jnp.float32),
        ],
        [VMEM_REF] * 3,
        [],
        cost(1, *states.shape, states.shape[0]),
    )([perts, cheb, states, pert_table], [SMEM_REF] + [VMEM_REF] * 3)


def local_kernel(cheb_ref, resid_ref, decay_ref, out_ref):
    out_ref[...] = cheb_dot(True, cheb_ref, resid_ref) + decay_ref[...] * resid_ref[...]


def local_terms(cheb, resid, decay):
    return call(
        local_kernel,
        jax.ShapeDtypeStruct(resid.shape, jnp.float32),
        VMEM_REF,
        [],
        cost(1, *resid.shape, resid.shape[0]),
    )([cheb, resid, decay], [VMEM_REF] * 3)


def middle_kernel(base, sent, many, offs_ref, x_ref, *refs):
    bands = refs[:many]
    acc_ref, deriv_ref, drive_ref, chosen_ref, states_ref, eps_ref, decay_ref = refs[many:-7]
    resid_ref, delta_ref, delta_t_ref, table_ref, sum_eps_ref, sum_decay_ref = refs[-7:-1]
    tile = GROUP * bands[0].shape[0]
    here = columns_of(offs_ref, base, x_ref.shape[-1])
    for at in range(many // GROUP):
        band = pl.ds(at * tile, tile)
        part = acc_ref[band, :] + product(bands[at * GROUP : (at + 1) * GROUP], here, x_ref.at[0])
        states = states_ref[:, band]
        act = jnp.tanh(part.T + drive_ref[:, band])
        eps = eps_ref[:, band]
        resid = deriv_ref[:, band] - (eps * act - decay_ref[:, band] * states)
        delta = (-eps * (1.0 - act * act) * resid).astype(jnp.bfloat16)
        wide = delta.astype(jnp.float32)
        resid_ref[:, band] = resid
        delta_ref[:, band] = delta
        delta_t_ref[band, :] = wide.T.astype(jnp.bfloat16)
        table_ref[:, band] = chosen_ref[:, band] * jnp.sum(wide, axis=0, keepdims=True)
        sum_eps_ref[:, band] = -jnp.sum(act * resid, axis=0, keepdims=True)
        sum_decay_ref[:, band] = jnp.sum(states * resid, axis=0, keepdims=True)
    share_part(sent, offs_ref, delta_ref, bands, refs[-1])


def middle(offs, base, sent, x, bands, acc, derivs, states, eps, decay):
    _, nodes, slab = x.shape
    rows = acc.shape[0]
    wide = functools.partial(jax.ShapeDtypeStruct, dtype=jnp.float32)
    return call(
        functools.partial(middle_kernel, base, sent, len(bands)),
        [
            wide((nodes, rows)),
            jax.ShapeDtypeStruct((nodes, rows), jnp.bfloat16),
            jax.ShapeDtypeStruct((rows, nodes), jnp.bfloat16),
            wide(derivs[2].shape),
            wide((1, rows)),
            wide((1, rows)),
            jax.ShapeDtypeStruct((len(sent), nodes, slab), jnp.bfloat16),
        ],
        [VMEM_REF] * 7,
        [],
        cost(2, nodes, slab, rows),
    )(
        [offs, x, *bands, acc, *derivs, states, eps, decay],
        [SMEM_REF] + [VMEM_REF] * (8 + len(bands)),
    )


def grad_w_part(base, offs_ref, delta_t_ref, xs, out_ref, held, sems):
    rows, slab = delta_t_ref.shape[0], held.shape[2]
    slots, tile = held.shape[:2]
    step = min(256, slab)
    copies = []
    for at, x_ref in enumerate(xs):
        for start in range(0, rows, tile):
            slot, band = len(copies) % slots, pl.ds(start, tile)
            if len(copies) >= slots:
                copies[-slots].wait()
            for col in range(0, slab, step):
                held[slot, :, col : col + step] = jnp.dot(
                    delta_t_ref[band, :], x_ref[:, col : col + step],
                    preferred_element_type=jnp.float32,
                ).astype(held.dtype)
            there = columns_of(offs_ref, base + at, slab)
            copy = pltpu.make_async_copy(held.at[slot], out_ref.at[band, there], sems.at[slot])
            copy.start()
            copies.append(copy)
    return copies[-slots:]


def share_part(places, offs_ref, delta_ref, bands, out_ref):
    depth, slab = GROUP * bands[0].shape[0], out_ref.shape[2]
    tile = max(slab // 2, 128)
    for index, place in enumerate(places):
        for col in range(0, slab, tile):
            there = pl.ds(pl.multiple_of(offs_ref[place] * slab + col, tile), tile)
            part = None
            for at in range(len(bands) // GROUP):
                group = bands[at * GROUP : (at + 1) * GROUP]
                more = jnp.dot(
                    delta_ref[:, at * depth : (at + 1) * depth],
                    jnp.concatenate([ref[:, there] for ref in group], axis=0),
                    preferred_element_type=jnp.float32,
                )
                part = more if part is None else part + more
            out_ref[index, :, pl.ds(col, tile)] = part.astype(out_ref.dtype)


def sums_kernel(base, found, arrays, sent, kept, many, first, *refs):
    offs_ref, delta_ref, delta_t_ref = refs[:3]
    xs, bands = refs[3 : 3 + arrays], refs[3 + arrays : 3 + arrays + many]
    refs = refs[3 + arrays + many + (0 if first else 1) :]
    copies = []
    if found:
        out_ref, held, sems = refs[-3:]
        views = [xs[at].at[index] for at, index in found]
        copies = grad_w_part(base, offs_ref, delta_t_ref, views, out_ref, held, sems)
    if sent:
        share_part(sent, offs_ref, delta_ref, bands, refs[0])
    if kept:
        share_part(kept, offs_ref, delta_ref, bands, refs[1])
    for copy in copies:
        copy.wait()


def sums(offs, base, pieces, sent, kept, delta, delta_t, bands, slab, so_far, shape):
    nodes, rows = delta.shape
    arrays, found = split_pieces(pieces)
    first = so_far is None
    tile = rows // 2
    shapes, scratch = [], []
    if sent:
        shapes.append(jax.ShapeDtypeStruct((len(sent), nodes, slab), jnp.bfloat16))
    if kept:
        shapes.append(jax.ShapeDtypeStruct((len(kept), nodes, slab), jnp.float32))
    specs = [VMEM_REF] * len(shapes)
    if found:
        shapes, specs = shapes + [jax.ShapeDtypeStruct(shape, jnp.bfloat16)], specs + [ANY_REF]
        scratch = [pltpu.VMEM((4, tile, slab), jnp.bfloat16), pltpu.SemaphoreType.DMA((4,))]
    operands = [offs, delta, delta_t, *arrays, *bands] + ([] if first else [so_far])
    outs = call(
        functools.partial(
            sums_kernel, base, found, len(arrays), sent, kept, len(bands), first
        ),
        shapes,
        specs,
        scratch,
        cost(len(found) + len(sent) + len(kept), nodes, slab, rows),
        {} if first else {len(operands) - 1: len(shapes) - 1},
    )(
        operands,
        [SMEM_REF] + [VMEM_REF] * (2 + len(arrays) + len(bands))
        + ([] if first else [ANY_REF]),
    )
    others, owns = outs[0] if sent else None, outs[1] if kept else None
    return others, owns, outs[-1] if found else so_far


def ring_body(chips, states, weights, pert_table, eps_gain, decay, perts):
    _, nodes, slab = states.shape
    rows = weights.shape[0]
    order = chip_ring(chips)
    place = np.argsort(order)
    half = chips // 2

    listing = [(0, 0), (0, 1)]
    for step in range(1, half):
        listing += [(step, 0), (step, 1), (-step, 1), (-step, 0)]
    listing += [(half, 0), (half, 1)]
    sides = {key: at for at, key in enumerate(listing)}
    table = np.array(
        [
            [
                2 * order[(place[device // 2] + (step if device % 2 else -step)) % chips]
                + (device % 2 ^ side)
                for step, side in listing
            ]
            for device in range(2 * chips)
        ],
        dtype=np.int32,
    )
    me = lax.axis_index("row")
    offs = lax.dynamic_slice(jnp.asarray(table), (me, 0), (1, 2 * chips)).reshape(-1)

    def passed(array, way=1, cross=0):
        pairs = []
        for at, chip in enumerate(order):
            pairs.append((2 * chip, 2 * order[(at + way) % chips] + cross))
            pairs.append((2 * chip + 1, 2 * order[(at - way) % chips] + 1 - cross))
        return lax.ppermute(array, "row", pairs)

    def swap(array):
        return lax.ppermute(array, "row", [(i, i ^ 1) for i in range(2 * chips)])

    gate = lax.optimization_barrier
    weights = pltpu.with_memory_space_constraint(weights, pltpu.HBM)
    cheb = cheb_matrix(nodes)
    flat = states.reshape(nodes, slab)
    xb = states.astype(jnp.bfloat16)

    near, over = passed(xb), passed(xb, -1, 1)
    other = swap(xb)
    mark, bands = load_first(offs, perts, weights, LOADS[0])
    near, over, other, mark = gate((near, over, other, mark))
    x = {(0, 0): (xb, 0), (0, 1): (other, 0)}
    flow = jnp.concatenate([near, over], axis=0)
    acc, seen = mark, 0
    for step in range(1, half + 1):
        if step < half:
            x[step, 0], x[step, 1] = (flow, 0), (flow, 1)
            other = flow
        else:
            x[half, 0], other = (flow, 0), flow
        if step < half:
            flow = passed(flow if step < half - 1 else flow[:1])
        other = swap(other)
        if step < half:
            x[-step, 1], x[-step, 0] = (other, 0), (other, 1)
        else:
            x[half, 1] = (other, 0)
        count = COUNTS[step - 1]
        fresh = LOADS[step - 1] if step <= 2 else 0
        late = LOADS[1] if step == 1 else 0
        acc, bands = add_products(
            offs, weights, acc, bands, [x[key] for key in listing[: seen + count]], count,
            fresh, late,
        )
        seen += count
        if step == half - 2:
            derivs = derivatives(perts, cheb, flat, pert_table)
            acc, *derivs = gate((acc, *derivs))
        if step < half:
            flow, acc = gate((flow, acc))

    decay = decay.reshape(1, rows)
    resid, delta, delta_t, grad_table, grad_eps, grad_decay, others = middle(
        offs, seen, [sides[half, 1]], x[half, 1][0], bands, acc, derivs, flat,
        eps_gain.reshape(1, rows), decay,
    )

    grad_w, base = None, 0

    def sent(step):
        return [sides[step, 1]] if step in (0, half) else [sides[step, 1], sides[step, 0]]

    def kept(step):
        return [sides[step, 0]] if step in (0, half) else [sides[-step, 0], sides[-step, 1]]

    def work(offs, count, sent, kept, grad_w, base):
        others, owns, grad_w = sums(
            offs, base, [x[key] for key in listing[base : base + count]], sent, kept,
            delta, delta_t, bands, slab, grad_w, weights.shape,
        )
        return others, owns, grad_w, base + count

    def joined(others, owns):
        return owns + swap(others).astype(jnp.float32)

    counts = list(PIECES)
    others, offs = gate((others, offs))
    far = swap(others)
    others, owns, _, _ = work(offs, 0, sent(half - 1), kept(half), None, 0)
    far = (owns + far.astype(jnp.float32)).astype(jnp.bfloat16)
    far, offs, others = gate((far, offs, others))
    ready, flow = swap(others), passed(far)
    for step in range(half - 1, 0, -1):
        late = kept(step) if step == half - 1 else []
        others, owns, grad_w, base = work(
            offs, counts.pop(0), sent(step - 1), late + kept(step - 1), grad_w, base
        )
        if step == 1:
            local = local_terms(cheb, resid, decay)
            owns, local = gate((owns, local))
        flow, owns = gate((flow, owns))
        flow = flow.astype(jnp.float32)
        if late:
            share, owns = owns[:2] + ready.astype(jnp.float32), owns[2:]
            total = jnp.concatenate([share[:1] + flow, share[1:]], axis=0)
        else:
            total = share + flow
        total = total.astype(jnp.bfloat16)
        share = joined(others, owns)
        total, offs = gate((total, offs))
        if step > 1:
            flow = passed(total)
        else:
            near, over = passed(total[:1]), passed(total[1:], 1, 1)
    _, _, grad_w, base = work(offs, len(listing) - base, [], [], grad_w, base)
    near, over, local = gate((near, over, local + share[0]))
    grad_x = local + near[0].astype(jnp.float32) + over[0].astype(jnp.float32)
    grad_x = grad_x.reshape(states.shape)
    return (grad_w, grad_x, grad_table, grad_eps.reshape(rows), grad_decay.reshape(rows))


def plain_body(states, weights, pert_table, eps_gain, decay, perts):
    traj, nodes, slab = states.shape
    total = traj * nodes
    cheb = cheb_matrix(nodes)
    xb = states.astype(jnp.bfloat16).reshape(total, slab)
    full = lax.all_gather(xb, "row", axis=1, tiled=True)
    pre = lax.dot_general(
        full, weights, (((1,), (1,)), ((), ())), preferred_element_type=jnp.float32
    )
    onehot = (perts[:, None] == jnp.arange(pert_table.shape[0], dtype=jnp.int32)[None, :]).astype(
        jnp.float32
    )
    drive = jnp.dot(onehot, pert_table, precision=lax.Precision.HIGHEST)
    act = jnp.tanh(pre.reshape(traj, nodes, slab) + drive[:, None, :])
    deriv = SCALE * jnp.einsum("kl,clg->ckg", cheb, states, precision=lax.Precision.HIGHEST)
    resid = deriv - (eps_gain * act - decay * states)
    delta = (-eps_gain * (1.0 - act * act) * resid).astype(jnp.bfloat16)
    dflat = delta.reshape(total, slab)
    grad_w = lax.dot_general(
        dflat, full, (((0,), (0,)), ((), ())), preferred_element_type=jnp.float32
    ).astype(jnp.bfloat16)
    back = jnp.dot(dflat, weights, preferred_element_type=jnp.float32)
    back = lax.psum_scatter(back, "row", scatter_dimension=1, tiled=True)
    grad_x = (
        SCALE * jnp.einsum("lk,clg->ckg", cheb, resid, precision=lax.Precision.HIGHEST)
        + decay * resid
        + back.reshape(traj, nodes, slab)
    )
    node_sums = jnp.sum(delta.astype(jnp.float32), axis=1)
    grad_table = jnp.dot(onehot.T, node_sums, precision=lax.Precision.HIGHEST)
    grad_eps = -jnp.sum(act * resid, axis=(0, 1))
    grad_decay = jnp.sum(states * resid, axis=(0, 1))
    return (grad_w, grad_x, grad_table, grad_eps, grad_decay)


def solution(mesh):
    chips = mesh.shape["row"] // 2
    in_specs = (
        P("rep", None, "row"),
        P(("rep", "row"), None),
        P("rep", "row"),
        P(("rep", "row")),
        P(("rep", "row")),
        P("rep"),
    )
    out_specs = (
        P(("rep", "row"), None),
        P("rep", None, "row"),
        P("rep", "row"),
        P(("rep", "row")),
        P(("rep", "row")),
    )

    def run(states, *others):
        if states.shape[0] == 1 and chips // 2 == len(PIECES) + 1:
            return ring_body(chips, states, *others)
        return plain_body(states, *others)

    return jax.shard_map(run, mesh=mesh, in_specs=in_specs, out_specs=out_specs, check_vma=False)
```

```python
import functools

import jax
import jax.numpy as jnp
import numpy as np
from jax import lax
from jax.experimental import pallas as pl
from jax.experimental.pallas import tpu as pltpu
from jax.sharding import PartitionSpec as P

SCALE = 2.0 / 1024.0
VMEM_LIMIT = 8 * 2**20
BANDS = 16
GROUP = 4
LOADS = (8, 8)
COUNTS = (2, 6, 6, 1)
PIECES = (1, 5, 5)


def cheb_matrix(count):
    index = np.arange(count)
    points = np.cos(np.pi * index / (count - 1))
    signs = np.where(index % 2 == 0, 1.0, -1.0)
    weight_c = signs * np.where((index == 0) | (index == count - 1), 2.0, 1.0)
    same = index[:, None] == index[None, :]
    spread = np.where(same, 1.0, points[:, None] - points[None, :])
    off = np.where(same, 0.0, weight_c[:, None] / weight_c[None, :] / spread)
    return jnp.asarray((off - np.diag(np.sum(off, axis=1))).astype(np.float32))


def chip_ring(chips):
    rows = 4
    cols = chips // rows
    cells = [(0, col) for col in range(cols)]
    for row in range(1, rows):
        span = range(1, cols)
        cells += [(row, col) for col in (reversed(span) if row % 2 else span)]
    cells += [(row, 0) for row in range(rows - 1, 0, -1)]
    return [row * cols + col for row, col in cells]


VMEM_REF = pl.BlockSpec(memory_space=pltpu.VMEM)
SMEM_REF = pl.BlockSpec(memory_space=pltpu.SMEM)
ANY_REF = pl.BlockSpec(memory_space=pl.ANY)
HBM_REF = pl.BlockSpec(memory_space=pltpu.HBM)


def cost(products, nodes, slab, rows):
    return pl.CostEstimate(
        flops=2 * products * nodes * slab * rows // 16,
        bytes_accessed=2 * products * slab * rows // 16,
        transcendentals=0,
    )


def call(kernel, out_shape, out_specs, scratch, costs, aliases=None):
    def run(operands, in_specs):
        return pl.pallas_call(
            kernel,
            out_shape=out_shape,
            in_specs=in_specs,
            out_specs=out_specs,
            scratch_shapes=scratch,
            input_output_aliases=aliases or {},
            compiler_params=pltpu.CompilerParams(vmem_limit_bytes=VMEM_LIMIT),
            cost_estimate=costs,
        )(*operands)

    return run


def columns_of(offs_ref, at, slab):
    return pl.ds(pl.multiple_of(offs_ref[at] * slab, slab), slab)


def band_copies(w_ref, bands, sems, first):
    copies = []
    for at, band_ref in enumerate(bands):
        tile = band_ref.shape[0]
        rows = pl.ds((first + at) * tile, tile)
        copies.append(pltpu.make_async_copy(w_ref.at[rows, :], band_ref, sems.at[at]))
    return copies


def product(bands, here, x_ref):
    return lax.dot_general(
        jnp.concatenate([band_ref[:, here] for band_ref in bands], axis=0), x_ref[...],
        (((1,), (1,)), ((), ())), preferred_element_type=jnp.float32,
    )


def split_pieces(pieces):
    arrays, found = [], []
    for array, index in pieces:
        at = [place for place, other in enumerate(arrays) if other is array]
        if not at:
            arrays.append(array)
        found.append((at[0] if at else len(arrays) - 1, index))
    return arrays, found


def load_kernel(offs_ref, w_ref, mark_ref, *refs):
    mark_ref[...] = jnp.zeros_like(mark_ref)
    copies = band_copies(w_ref, refs[:-1], refs[-1], 0)
    for copy in copies:
        copy.start()
    for copy in copies:
        copy.wait()


def band_shapes(count, weights):
    return [pltpu.VMEM((weights.shape[0] // BANDS, weights.shape[1]), weights.dtype)] * count


def load_first(offs, weights, count):
    mark, *bands = call(
        load_kernel,
        [jax.ShapeDtypeStruct((8, 128), jnp.float32)] + band_shapes(count, weights),
        [VMEM_REF] * (1 + count),
        [pltpu.SemaphoreType.DMA((count,))],
        cost(1, 128, 128, 1024),
    )([offs, weights], [SMEM_REF, HBM_REF])
    return mark, bands


def pre_kernel(found, count, many, fresh, late, offs_ref, acc_ref, *refs):
    if late:
        w_ref, refs = refs[0], refs[1:]
    bands, refs = refs[:many], refs[many:]
    arrays = 1 + max(at for at, _ in found)
    xs, out_ref, others, sems = refs[:arrays], refs[arrays], refs[arrays + 1 : -1], refs[-1]
    slab = xs[0].shape[-1]
    tile = out_ref.shape[0] // BANDS
    copies = band_copies(w_ref, others, sems, many) if late else []
    waiting = list(copies)
    for low in [*range(0, many - fresh, GROUP), *range(many - fresh, many, GROUP)]:
        old = low < many - fresh
        group = bands[low : min(low + GROUP, many - fresh if old else many)]
        rows = pl.ds(low * tile, len(group) * tile)
        total = acc_ref[rows, :] if old else None
        for place in range(len(found) - count if old else 0, len(found)):
            if waiting:
                waiting.pop(0).start()
            at, index = found[place]
            part = product(group, columns_of(offs_ref, place, slab), xs[at].at[index])
            total = part if total is None else total + part
        out_ref[rows, :] = total
    for copy in waiting:
        copy.start()
    for copy in copies:
        copy.wait()


def add_products(offs, weights, acc, bands, pieces, count, fresh, late):
    arrays, found = split_pieces(pieces if fresh else pieces[-count:])
    if not fresh:
        found = [(0, 0)] * (len(pieces) - count) + found
    (_, nodes, slab), rows, many = arrays[0].shape, weights.shape[0], len(bands)
    operands = [offs, acc] + ([weights] if late else []) + [*bands, *arrays]
    acc, *others = call(
        functools.partial(pre_kernel, found, count, many, fresh, late),
        [jax.ShapeDtypeStruct((rows, nodes), jnp.float32)] + band_shapes(late, weights),
        [VMEM_REF] * (1 + late),
        [pltpu.SemaphoreType.DMA((max(late, 1),))],
        cost(count, nodes, slab, rows),
    )(
        operands,
        [SMEM_REF, VMEM_REF] + ([HBM_REF] if late else [])
        + [VMEM_REF] * (many + len(arrays)),
    )
    return acc, [*bands, *others]


def cheb_dot(turned, cheb_ref, array_ref):
    return SCALE * lax.dot_general(
        cheb_ref[...], array_ref[...], (((0 if turned else 1,), (0,)), ((), ())),
        precision=lax.Precision.HIGHEST, preferred_element_type=jnp.float32,
    )


def deriv_kernel(perts_ref, cheb_ref, states_ref, pert_ref, deriv_ref, drive_ref, chosen_ref):
    deriv_ref[...] = cheb_dot(False, cheb_ref, states_ref)
    rows = lax.broadcasted_iota(jnp.int32, chosen_ref.shape, 0)
    chosen = rows == jnp.broadcast_to(perts_ref[...], chosen_ref.shape)
    drive_ref[...] = jnp.sum(jnp.where(chosen, pert_ref[...], 0.0), axis=0, keepdims=True)
    chosen_ref[...] = jnp.where(chosen, 1.0, 0.0)


def derivatives(perts, cheb, states, pert_table):
    return call(
        deriv_kernel,
        [
            jax.ShapeDtypeStruct(states.shape, jnp.float32),
            jax.ShapeDtypeStruct((1, states.shape[1]), jnp.float32),
            jax.ShapeDtypeStruct(pert_table.shape, jnp.float32),
        ],
        [VMEM_REF] * 3,
        [],
        cost(1, *states.shape, states.shape[0]),
    )([perts.reshape(1, 1), cheb, states, pert_table], [VMEM_REF] * 4)


def local_kernel(cheb_ref, resid_ref, decay_ref, out_ref):
    out_ref[...] = cheb_dot(True, cheb_ref, resid_ref) + decay_ref[...] * resid_ref[...]


def local_terms(cheb, resid, decay):
    return call(
        local_kernel,
        jax.ShapeDtypeStruct(resid.shape, jnp.float32),
        VMEM_REF,
        [],
        cost(1, *resid.shape, resid.shape[0]),
    )([cheb, resid, decay], [VMEM_REF] * 3)


def middle_kernel(base, sent, many, offs_ref, x_ref, *refs):
    bands = refs[:many]
    acc_ref, deriv_ref, drive_ref, chosen_ref, states_ref, eps_ref, decay_ref = refs[many:-7]
    resid_ref, delta_ref, delta_t_ref, table_ref, sum_eps_ref, sum_decay_ref = refs[-7:-1]
    tile = GROUP * bands[0].shape[0]
    here = columns_of(offs_ref, base, x_ref.shape[-1])
    for at in range(many // GROUP):
        band = pl.ds(at * tile, tile)
        part = acc_ref[band, :] + product(bands[at * GROUP : (at + 1) * GROUP], here, x_ref.at[0])
        states = states_ref[:, band]
        act = jnp.tanh(part.T + drive_ref[:, band])
        eps = eps_ref[:, band]
        resid = deriv_ref[:, band] - (eps * act - decay_ref[:, band] * states)
        delta = (-eps * (1.0 - act * act) * resid).astype(jnp.bfloat16)
        wide = delta.astype(jnp.float32)
        resid_ref[:, band] = resid
        delta_ref[:, band] = delta
        delta_t_ref[band, :] = wide.T.astype(jnp.bfloat16)
        table_ref[:, band] = chosen_ref[:, band] * jnp.sum(wide, axis=0, keepdims=True)
        sum_eps_ref[:, band] = -jnp.sum(act * resid, axis=0, keepdims=True)
        sum_decay_ref[:, band] = jnp.sum(states * resid, axis=0, keepdims=True)
    share_part(sent, offs_ref, delta_ref, bands, refs[-1])


def middle(offs, base, sent, x, bands, acc, derivs, states, eps, decay):
    _, nodes, slab = x.shape
    rows = acc.shape[0]
    wide = functools.partial(jax.ShapeDtypeStruct, dtype=jnp.float32)
    return call(
        functools.partial(middle_kernel, base, sent, len(bands)),
        [
            wide((nodes, rows)),
            jax.ShapeDtypeStruct((nodes, rows), jnp.bfloat16),
            jax.ShapeDtypeStruct((rows, nodes), jnp.bfloat16),
            wide(derivs[2].shape),
            wide((1, rows)),
            wide((1, rows)),
            jax.ShapeDtypeStruct((len(sent), nodes, slab), jnp.bfloat16),
        ],
        [VMEM_REF] * 7,
        [],
        cost(2, nodes, slab, rows),
    )(
        [offs, x, *bands, acc, *derivs, states, eps, decay],
        [SMEM_REF] + [VMEM_REF] * (8 + len(bands)),
    )


def grad_w_part(base, offs_ref, delta_t_ref, xs, out_ref, held, sems):
    rows, slab = delta_t_ref.shape[0], held.shape[2]
    slots, tile = held.shape[:2]
    step = min(256, slab)
    copies = []
    for at, x_ref in enumerate(xs):
        for start in range(0, rows, tile):
            slot, band = len(copies) % slots, pl.ds(start, tile)
            if len(copies) >= slots:
                copies[-slots].wait()
            for col in range(0, slab, step):
                held[slot, :, col : col + step] = jnp.dot(
                    delta_t_ref[band, :], x_ref[:, col : col + step],
                    preferred_element_type=jnp.float32,
                ).astype(held.dtype)
            there = columns_of(offs_ref, base + at, slab)
            copy = pltpu.make_async_copy(held.at[slot], out_ref.at[band, there], sems.at[slot])
            copy.start()
            copies.append(copy)
    return copies[-slots:]


def share_part(places, offs_ref, delta_ref, bands, out_ref):
    depth, slab = GROUP * bands[0].shape[0], out_ref.shape[2]
    tile = max(slab // 2, 128)
    for index, place in enumerate(places):
        for col in range(0, slab, tile):
            there = pl.ds(pl.multiple_of(offs_ref[place] * slab + col, tile), tile)
            part = None
            for at in range(len(bands) // GROUP):
                group = bands[at * GROUP : (at + 1) * GROUP]
                more = jnp.dot(
                    delta_ref[:, at * depth : (at + 1) * depth],
                    jnp.concatenate([ref[:, there] for ref in group], axis=0),
                    preferred_element_type=jnp.float32,
                )
                part = more if part is None else part + more
            out_ref[index, :, pl.ds(col, tile)] = part.astype(out_ref.dtype)


def sums_kernel(base, found, arrays, sent, kept, many, first, *refs):
    offs_ref, delta_ref, delta_t_ref = refs[:3]
    xs, bands = refs[3 : 3 + arrays], refs[3 + arrays : 3 + arrays + many]
    refs = refs[3 + arrays + many + (0 if first else 1) :]
    copies = []
    if found:
        out_ref, held, sems = refs[-3:]
        views = [xs[at].at[index] for at, index in found]
        copies = grad_w_part(base, offs_ref, delta_t_ref, views, out_ref, held, sems)
    if sent:
        share_part(sent, offs_ref, delta_ref, bands, refs[0])
    if kept:
        share_part(kept, offs_ref, delta_ref, bands, refs[1])
    for copy in copies:
        copy.wait()


def sums(offs, base, pieces, sent, kept, delta, delta_t, bands, slab, so_far, shape):
    nodes, rows = delta.shape
    arrays, found = split_pieces(pieces)
    first = so_far is None
    tile = rows // 2
    shapes, scratch = [], []
    if sent:
        shapes.append(jax.ShapeDtypeStruct((len(sent), nodes, slab), jnp.bfloat16))
    if kept:
        shapes.append(jax.ShapeDtypeStruct((len(kept), nodes, slab), jnp.float32))
    specs = [VMEM_REF] * len(shapes)
    if found:
        shapes, specs = shapes + [jax.ShapeDtypeStruct(shape, jnp.bfloat16)], specs + [ANY_REF]
        scratch = [pltpu.VMEM((4, tile, slab), jnp.bfloat16), pltpu.SemaphoreType.DMA((4,))]
    operands = [offs, delta, delta_t, *arrays, *bands] + ([] if first else [so_far])
    outs = call(
        functools.partial(
            sums_kernel, base, found, len(arrays), sent, kept, len(bands), first
        ),
        shapes,
        specs,
        scratch,
        cost(len(found) + len(sent) + len(kept), nodes, slab, rows),
        {} if first else {len(operands) - 1: len(shapes) - 1},
    )(
        operands,
        [SMEM_REF] + [VMEM_REF] * (2 + len(arrays) + len(bands))
        + ([] if first else [ANY_REF]),
    )
    others, owns = outs[0] if sent else None, outs[1] if kept else None
    return others, owns, outs[-1] if found else so_far


def ring_body(chips, states, weights, pert_table, eps_gain, decay, perts):
    _, nodes, slab = states.shape
    rows = weights.shape[0]
    order = chip_ring(chips)
    place = np.argsort(order)
    half = chips // 2

    listing = [(0, 0), (0, 1)]
    for step in range(1, half):
        listing += [(step, 0), (step, 1), (-step, 1), (-step, 0)]
    listing += [(half, 0), (half, 1)]
    sides = {key: at for at, key in enumerate(listing)}
    table = np.array(
        [
            [
                2 * order[(place[device // 2] + (step if device % 2 else -step)) % chips]
                + (device % 2 ^ side)
                for step, side in listing
            ]
            for device in range(2 * chips)
        ],
        dtype=np.int32,
    )
    me = lax.axis_index("row")
    offs = lax.dynamic_slice(jnp.asarray(table), (me, 0), (1, 2 * chips)).reshape(-1)

    def passed(array, way=1, cross=0):
        pairs = []
        for at, chip in enumerate(order):
            pairs.append((2 * chip, 2 * order[(at + way) % chips] + cross))
            pairs.append((2 * chip + 1, 2 * order[(at - way) % chips] + 1 - cross))
        return lax.ppermute(array, "row", pairs)

    def swap(array):
        return lax.ppermute(array, "row", [(i, i ^ 1) for i in range(2 * chips)])

    gate = lax.optimization_barrier
    weights = pltpu.with_memory_space_constraint(weights, pltpu.HBM)
    cheb = cheb_matrix(nodes)
    flat = states.reshape(nodes, slab)
    xb = states.astype(jnp.bfloat16)

    near, over = passed(xb), passed(xb, -1, 1)
    other = swap(xb)
    mark, bands = load_first(offs, weights, LOADS[0])
    near, over, other, mark = gate((near, over, other, mark))
    x = {(0, 0): (xb, 0), (0, 1): (other, 0)}
    flow = jnp.concatenate([near, over], axis=0)
    acc, seen = mark, 0
    for step in range(1, half + 1):
        if step < half:
            x[step, 0], x[step, 1] = (flow, 0), (flow, 1)
            other = flow
        else:
            x[half, 0], other = (flow, 0), flow
        if step < half:
            flow = passed(flow if step < half - 1 else flow[:1])
        other = swap(other)
        if step < half:
            x[-step, 1], x[-step, 0] = (other, 0), (other, 1)
        else:
            x[half, 1] = (other, 0)
        count = COUNTS[step - 1]
        fresh = LOADS[step - 1] if step <= 2 else 0
        late = LOADS[1] if step == 1 else 0
        acc, bands = add_products(
            offs, weights, acc, bands, [x[key] for key in listing[: seen + count]], count,
            fresh, late,
        )
        seen += count
        if step == half - 2:
            derivs = derivatives(perts, cheb, flat, pert_table)
            acc, *derivs = gate((acc, *derivs))
        if step < half:
            flow, acc = gate((flow, acc))

    decay = decay.reshape(1, rows)
    resid, delta, delta_t, grad_table, grad_eps, grad_decay, others = middle(
        offs, seen, [sides[half, 1]], x[half, 1][0], bands, acc, derivs, flat,
        eps_gain.reshape(1, rows), decay,
    )

    grad_w, base = None, 0

    def sent(step):
        return [sides[step, 1]] if step in (0, half) else [sides[step, 1], sides[step, 0]]

    def kept(step):
        return [sides[step, 0]] if step in (0, half) else [sides[-step, 0], sides[-step, 1]]

    def work(offs, count, sent, kept, grad_w, base):
        others, owns, grad_w = sums(
            offs, base, [x[key] for key in listing[base : base + count]], sent, kept,
            delta, delta_t, bands, slab, grad_w, weights.shape,
        )
        return others, owns, grad_w, base + count

    def joined(others, owns):
        return owns + swap(others).astype(jnp.float32)

    counts = list(PIECES)
    others, offs = gate((others, offs))
    far = swap(others)
    others, owns, _, _ = work(offs, 0, sent(half - 1), kept(half), None, 0)
    far = (owns + far.astype(jnp.float32)).astype(jnp.bfloat16)
    far, offs, others = gate((far, offs, others))
    ready, flow = swap(others), passed(far)
    for step in range(half - 1, 0, -1):
        late = kept(step) if step == half - 1 else []
        others, owns, grad_w, base = work(
            offs, counts.pop(0), sent(step - 1), late + kept(step - 1), grad_w, base
        )
        if step == 1:
            local = local_terms(cheb, resid, decay)
            owns, local = gate((owns, local))
        flow, owns = gate((flow, owns))
        flow = flow.astype(jnp.float32)
        if late:
            share, owns = owns[:2] + ready.astype(jnp.float32), owns[2:]
            total = jnp.concatenate([share[:1] + flow, share[1:]], axis=0)
        else:
            total = share + flow
        total = total.astype(jnp.bfloat16)
        share = joined(others, owns)
        total, offs = gate((total, offs))
        if step > 1:
            flow = passed(total)
        else:
            near, over = passed(total[:1]), passed(total[1:], 1, 1)
    _, _, grad_w, base = work(offs, len(listing) - base, [], [], grad_w, base)
    near, over, local = gate((near, over, local + share[0]))
    grad_x = local + near[0].astype(jnp.float32) + over[0].astype(jnp.float32)
    grad_x = grad_x.reshape(states.shape)
    return (grad_w, grad_x, grad_table, grad_eps.reshape(rows), grad_decay.reshape(rows))


def plain_body(states, weights, pert_table, eps_gain, decay, perts):
    traj, nodes, slab = states.shape
    total = traj * nodes
    cheb = cheb_matrix(nodes)
    xb = states.astype(jnp.bfloat16).reshape(total, slab)
    full = lax.all_gather(xb, "row", axis=1, tiled=True)
    pre = lax.dot_general(
        full, weights, (((1,), (1,)), ((), ())), preferred_element_type=jnp.float32
    )
    onehot = (perts[:, None] == jnp.arange(pert_table.shape[0], dtype=jnp.int32)[None, :]).astype(
        jnp.float32
    )
    drive = jnp.dot(onehot, pert_table, precision=lax.Precision.HIGHEST)
    act = jnp.tanh(pre.reshape(traj, nodes, slab) + drive[:, None, :])
    deriv = SCALE * jnp.einsum("kl,clg->ckg", cheb, states, precision=lax.Precision.HIGHEST)
    resid = deriv - (eps_gain * act - decay * states)
    delta = (-eps_gain * (1.0 - act * act) * resid).astype(jnp.bfloat16)
    dflat = delta.reshape(total, slab)
    grad_w = lax.dot_general(
        dflat, full, (((0,), (0,)), ((), ())), preferred_element_type=jnp.float32
    ).astype(jnp.bfloat16)
    back = jnp.dot(dflat, weights, preferred_element_type=jnp.float32)
    back = lax.psum_scatter(back, "row", scatter_dimension=1, tiled=True)
    grad_x = (
        SCALE * jnp.einsum("lk,clg->ckg", cheb, resid, precision=lax.Precision.HIGHEST)
        + decay * resid
        + back.reshape(traj, nodes, slab)
    )
    node_sums = jnp.sum(delta.astype(jnp.float32), axis=1)
    grad_table = jnp.dot(onehot.T, node_sums, precision=lax.Precision.HIGHEST)
    grad_eps = -jnp.sum(act * resid, axis=(0, 1))
    grad_decay = jnp.sum(states * resid, axis=(0, 1))
    return (grad_w, grad_x, grad_table, grad_eps, grad_decay)


def solution(mesh):
    chips = mesh.shape["row"] // 2
    in_specs = (
        P("rep", None, "row"),
        P(("rep", "row"), None),
        P("rep", "row"),
        P(("rep", "row")),
        P(("rep", "row")),
        P("rep"),
    )
    out_specs = (
        P(("rep", "row"), None),
        P("rep", None, "row"),
        P("rep", "row"),
        P(("rep", "row")),
        P(("rep", "row")),
    )

    def run(states, *others):
        if states.shape[0] == 1 and chips // 2 == len(PIECES) + 1:
            return ring_body(chips, states, *others)
        return plain_body(states, *others)

    return jax.shard_map(run, mesh=mesh, in_specs=in_specs, out_specs=out_specs, check_vma=False)
```
